32 devices in a mesh: dp: 16 (over z, y, x), tensor: 2 (over core).
Axes of the slice: x: 2, y: 2, z: 4, core: 2. Of those that a mesh axis runs over, the one named last changes fastest.
Arguments:
- tokens: bfloat16 [32768, 768], P(('dp', 'tensor')), may hold values from -6 to 6
- cotangent: bfloat16 [32768, 768], P(('dp', 'tensor')), may hold values from -6 to 6
- lengths: int32 [64], P('dp'), may hold values from 1 to 512, as said below
- w_query: float32 [768, 768], P(None, 'tensor'), as said below
- w_key: float32 [768, 768], P(None, 'tensor')
- w_value: float32 [768, 768], P(None, 'tensor')
- w_output: float32 [768, 768], P('tensor')
- w_inner: float32 [768, 3072], P(None, 'tensor'), as said below
- w_outer: float32 [3072, 768], P('tensor')
- b_query: float32 [768], P('tensor'), may hold values from -1.8 to 1.8
- b_value: float32 [768], P('tensor'), may hold values from -1.8 to 1.8
- b_output: float32 [768], replicated, may hold values from -1.8 to 1.8
- b_inner: float32 [3072], P('tensor'), may hold values from -3 to 3
- b_outer: float32 [768], replicated, may hold values from -1.8 to 1.8
- ln_gains: float32 [2, 768], replicated, may hold values from 0.5 to 1.5
- ln_shifts: float32 [2, 768], replicated, may hold values from -1.8 to 1.8
- clip_input: float32 [768], replicated, may hold values from 1 to 3
- clip_context: float32 [768], P('tensor'), may hold values from 0.3 to 1
- clip_middle: float32 [768], replicated, may hold values from 1 to 3
- clip_hidden: float32 [3072], P('tensor'), may hold values from 0.5 to 2
- t_query: bfloat16 [768, 768], P(None, 'tensor'), may hold values from -0.4375 to 0.4375
- t_key: bfloat16 [768, 768], P(None, 'tensor'), may hold values from -0.4375 to 0.4375
- t_value: bfloat16 [768, 768], P(None, 'tensor'), may hold values from -0.21875 to 0.21875
- t_output: bfloat16 [768, 768], P('tensor'), may hold values from -1.75 to 1.75
- t_inner: bfloat16 [768, 3072], P(None, 'tensor'), may hold values from -0.21875 to 0.21875
- t_outer: bfloat16 [3072, 768], P('tensor'), may hold values from -0.109375 to 0.109375
- tb_query: float32 [768], P('tensor'), may hold values from -1.8 to 1.8
- tb_value: float32 [768], P('tensor'), may hold values from -1.8 to 1.8
- tb_output: float32 [768], replicated, may hold values from -1.8 to 1.8
- tb_inner: float32 [3072], P('tensor'), may hold values from -3 to 3
- tb_outer: float32 [768], replicated, may hold values from -1.8 to 1.8
- t_gains: float32 [2, 768], replicated, may hold values from 0.5 to 1.5
- t_shifts: float32 [2, 768], replicated, may hold values from -1.8 to 1.8
Outputs:
- layer_out: bfloat16 [32768, 768], P(('dp', 'tensor'))
- grad_tokens: float32 [32768, 768], P(('dp', 'tensor'))
- g_query: float32 [768, 768], P(None, 'tensor')
- g_key: float32 [768, 768], P(None, 'tensor')
- g_value: float32 [768, 768], P(None, 'tensor')
- g_output: float32 [768, 768], P('tensor')
- g_inner: float32 [768, 3072], P(None, 'tensor')
- g_outer: float32 [3072, 768], P('tensor')
- gb_query: float32 [768], P('tensor')
- gb_value: float32 [768], P('tensor')
- gb_output: float32 [768], replicated
- gb_inner: float32 [3072], P('tensor')
- gb_outer: float32 [768], replicated
- g_gains: float32 [2, 768], replicated
- g_shifts: float32 [2, 768], replicated
- gc_input: float32 [768], replicated
- gc_context: float32 [768], P('tensor')
- gc_middle: float32 [768], replicated
- gc_hidden: float32 [3072], P('tensor')
- summary: float32 [4], replicated
The draws below stay inside these ranges and needn't reach their ends.
Inputs may be any that keep to these rules, and one draw needn't show every extreme that they name: `lengths`: each row holds its valid tokens first and padding after them; in every draw some row has all 512 slots valid. `w_query`: latent weights have magnitudes between 0.25 and 1.25. `w_inner`: latent weights have magnitudes between 0.25 and 1.25.
All inputs are finite; a program needn't handle non-finite values.
Results may differ from the reference program's by a relative error of at most 0.012.
The reference program's roundings to bfloat16 on the way count: a program that leaves them out, or rounds other values in their place, can miss the bound.
Values may be sent and summed in bfloat16 or wider, within the bound.
No kernel may reach another device: no remote copies, remote signals or barrier semaphores. Data moves between devices by JAX's collectives and lax.ppermute only.
A program may use at most 192 MiB of HBM per device.

```python
import math
from functools import partial
import jax
import jax.numpy as jnp
from jax import lax

D = 768
HEADS = 12
FF = 3072
SEQ = 512
SEQS = 4
HD = 64
NSEQ = 64
TOKENS = 32768
N_DP = 16


def latent_draw(key, n_rows, n_cols):
    sign_key, size_key = jax.random.split(key)
    signs = jax.random.randint(sign_key, (n_rows, n_cols), 0, 2).astype(jnp.float32) * 2.0 - 1.0
    magnitude = jax.random.uniform(size_key, (n_rows, n_cols), jnp.float32, 0.25, 1.25)
    return signs * magnitude


def draw_w_query(key, part):
    return latent_draw(jax.random.fold_in(key, 11), D, D)


def draw_w_key(key, part):
    return latent_draw(jax.random.fold_in(key, 12), D, D)


def draw_w_value(key, part):
    return latent_draw(jax.random.fold_in(key, 13), D, D)


def draw_w_output(key, part):
    return latent_draw(jax.random.fold_in(key, 14), D, D)


def draw_w_inner(key, part):
    return latent_draw(jax.random.fold_in(key, 15), D, FF)


def draw_w_outer(key, part):
    return latent_draw(jax.random.fold_in(key, 16), FF, D)


def draw_lengths(key, part):
    key_one, key_two, key_three = jax.random.split(jax.random.fold_in(key, 21), 3)
    factor = jax.random.randint(key_one, (NSEQ,), 1, 33)
    expo = jax.random.randint(key_two, (NSEQ,), 0, 4)
    span = jnp.clip(factor * jnp.power(2, expo).astype(jnp.int32), 1, 64)
    ramp = NSEQ + 2 * jnp.arange(NSEQ, dtype=jnp.int32)
    lens = jnp.clip(span * SEQ * ramp // (64 * 3 * NSEQ), 1, SEQ)
    chosen = jax.random.randint(key_three, (), 0, NSEQ)
    lens = jnp.where(jnp.arange(NSEQ) == chosen, SEQ, lens)
    return lens.astype(jnp.int32)


def level_of(own_key, shape, shards, low, largest):
    factor_of = 1.0
    for position, shards_of in shards:
        draws = jax.random.uniform(jax.random.fold_in(jax.random.fold_in(own_key, 6), position), (shards_of,), jnp.float32, low / len(shards), largest / len(shards))
        factor_of = factor_of * jnp.repeat(jnp.exp(draws), shape[position] // shards_of).reshape((-1,) + (1,) * (len(shape) - 1 - position))
    return factor_of


def scatter_about(key, shape, scale, most, cuts=(), kind=jnp.bfloat16):
    result = scale * jax.random.normal(key, shape, jnp.float32)
    if cuts:
        result = result * level_of(key, shape, cuts, -0.22, 0.18)
    return jnp.clip(result, -most, most).astype(kind)


def setup_inputs(seed: int = 0) -> dict:
    seeds = jax.random.split(jax.random.key(seed), 34)
    tokens = scatter_about(seeds[0], (TOKENS, D), 1.0, 6.0, ((0, 32),))
    cotangent = scatter_about(seeds[1], (TOKENS, D), 1.0, 6.0, ((0, 32),))
    lengths = draw_lengths(jax.random.fold_in(seeds[33], 71), 0)
    w_query = draw_w_query(jax.random.fold_in(seeds[33], 71), 0)
    w_key = draw_w_key(jax.random.fold_in(seeds[33], 71), 0)
    w_value = draw_w_value(jax.random.fold_in(seeds[33], 71), 0)
    w_output = draw_w_output(jax.random.fold_in(seeds[33], 71), 0)
    w_inner = draw_w_inner(jax.random.fold_in(seeds[33], 71), 0)
    w_outer = draw_w_outer(jax.random.fold_in(seeds[33], 71), 0)
    b_query = scatter_about(seeds[9], (D,), 0.3, 1.8, ((0, 2),), jnp.float32)
    b_value = scatter_about(seeds[10], (D,), 0.3, 1.8, ((0, 2),), jnp.float32)
    b_output = scatter_about(seeds[11], (D,), 0.3, 1.8, (), jnp.float32)
    b_inner = scatter_about(seeds[12], (FF,), 0.5, 3.0, ((0, 2),), jnp.float32)
    b_outer = scatter_about(seeds[13], (D,), 0.3, 1.8, (), jnp.float32)
    ln_gains = jnp.clip(1.0 + 0.1 * jax.random.normal(seeds[14], (2, D), jnp.float32), 0.5, 1.5)
    ln_shifts = scatter_about(seeds[15], (2, D), 0.3, 1.8, (), jnp.float32)
    clip_input = jnp.clip(jnp.exp(jax.random.uniform(seeds[16], (D,), jnp.float32, math.log(1.0), math.log(3.0))), 1.0, 3.0)
    clip_context = jnp.clip(jnp.exp(math.log(1.0) - 1.2039728 * jax.random.uniform(seeds[17], (D,), jnp.float32) ** level_of(seeds[17], (D,), ((0, 2),), -0.2, 0.2)), 0.3, 1.0)
    clip_middle = jnp.clip(jnp.exp(jax.random.uniform(seeds[18], (D,), jnp.float32, math.log(1.0), math.log(3.0))), 1.0, 3.0)
    clip_hidden = jnp.clip(jnp.exp(math.log(2.0) - 1.3862944 * jax.random.uniform(seeds[19], (FF,), jnp.float32) ** level_of(seeds[19], (FF,), ((0, 2),), -0.2, 0.2)), 0.5, 2.0)
    t_query = scatter_about(seeds[20], (D, D), (D // 4) ** -0.5, 0.4375, ((1, 2),))
    t_key = scatter_about(seeds[21], (D, D), (D // 4) ** -0.5, 0.4375, ((1, 2),))
    t_value = scatter_about(seeds[22], (D, D), D ** -0.5, 0.21875, ((1, 2),))
    t_output = scatter_about(seeds[23], (D, D), (D // 64) ** -0.5, 1.75, ((0, 2),))
    t_inner = scatter_about(seeds[24], (D, FF), D ** -0.5, 0.21875, ((1, 2),))
    t_outer = scatter_about(seeds[25], (FF, D), FF ** -0.5, 0.109375, ((0, 2),))
    tb_query = scatter_about(seeds[26], (D,), 0.3, 1.8, ((0, 2),), jnp.float32)
    tb_value = scatter_about(seeds[27], (D,), 0.3, 1.8, ((0, 2),), jnp.float32)
    tb_output = scatter_about(seeds[28], (D,), 0.3, 1.8, (), jnp.float32)
    tb_inner = scatter_about(seeds[29], (FF,), 0.5, 3.0, ((0, 2),), jnp.float32)
    tb_outer = scatter_about(seeds[30], (D,), 0.3, 1.8, (), jnp.float32)
    t_gains = jnp.clip(1.0 + 0.1 * jax.random.normal(seeds[31], (2, D), jnp.float32), 0.5, 1.5)
    t_shifts = scatter_about(seeds[32], (2, D), 0.3, 1.8, (), jnp.float32)
    return dict(tokens=tokens, cotangent=cotangent, lengths=lengths, w_query=w_query, w_key=w_key, w_value=w_value, w_output=w_output, w_inner=w_inner, w_outer=w_outer, b_query=b_query, b_value=b_value, b_output=b_output, b_inner=b_inner, b_outer=b_outer, ln_gains=ln_gains, ln_shifts=ln_shifts, clip_input=clip_input, clip_context=clip_context, clip_middle=clip_middle, clip_hidden=clip_hidden, t_query=t_query, t_key=t_key, t_value=t_value, t_output=t_output, t_inner=t_inner, t_outer=t_outer, tb_query=tb_query, tb_value=tb_value, tb_output=tb_output, tb_inner=tb_inner, tb_outer=tb_outer, t_gains=t_gains, t_shifts=t_shifts)


@jax.custom_vjp
def low(v):
    return lax.optimization_barrier(v.astype(jnp.bfloat16)).astype(jnp.float32)

@jax.custom_vjp
def low_back(v):
    return v

def low_keep(v):
    return (low(v), None)

def low_pass(kept, grad):
    return (grad,)

def back_keep(v):
    return (v, None)

def back_low(kept, grad):
    return (low(grad),)
low.defvjp(low_keep, low_pass)
low_back.defvjp(back_keep, back_low)
exact_mode = lax.Precision.HIGHEST
norm_eps = 1e-12

def soft_clip(value, bound):
    return bound * jnp.tanh(value / bound)

def binarize(latent, axis, factor):
    scale_mean = lax.optimization_barrier(jnp.mean(jnp.abs(latent), axis=axis, keepdims=True))
    return scale_mean * jnp.tanh(2.0 * latent) * factor

def layer_norm(resid, gain, shift):
    centered = resid - lax.optimization_barrier(jnp.mean(resid, -1, keepdims=True))
    spread = lax.optimization_barrier(jnp.mean(centered * centered, -1, keepdims=True))
    return centered * lax.rsqrt(spread + norm_eps) * gain + shift

def mat_mul(left, right):
    return jnp.dot(left, right, precision=exact_mode, preferred_element_type=jnp.float32)

def attend_one(item, student):
    q_seq, k_seq, v_seq, length = item
    scores = jnp.einsum('qhd,khd->hqk', q_seq, k_seq, precision=exact_mode) * HD ** (-0.5)
    if student:
        scores = low_back(scores)
    keep_key = jnp.arange(SEQ) < length
    scores = jnp.where(keep_key[None, None, :], scores, -1000000000.0)
    top_score = lax.optimization_barrier(jnp.max(scores, -1, keepdims=True))
    expo = jnp.exp(scores - top_score)
    probs = low(expo / lax.optimization_barrier(jnp.sum(expo, -1, keepdims=True)))
    return jnp.einsum('hqk,khd->qhd', probs, v_seq, precision=exact_mode)

def layer(params, x_rows, lens, student):
    if student:
        w_q = low(binarize(params['w_query'], 0, 2.0 / math.sqrt(D)))
        w_k = low(binarize(params['w_key'], 0, 2.0 / math.sqrt(D)))
        w_v = low(binarize(params['w_value'], 0, 1.0 / math.sqrt(D)))
        w_o = low(binarize(params['w_output'], 1, 8.0 / math.sqrt(D)))
        w_i = low(binarize(params['w_inner'], 0, 1.0 / math.sqrt(D)))
        w_u = low(binarize(params['w_outer'], 1, 1.0 / math.sqrt(FF)))
        x_in = low(soft_clip(x_rows, params['clip_input']))
    else:
        w_q, w_k, w_v = (params['w_query'], params['w_key'], params['w_value'])
        w_o, w_i, w_u = (params['w_output'], params['w_inner'], params['w_outer'])
        x_in = x_rows
    q_val = low(low_back(mat_mul(x_in, w_q)) + params['b_query'])
    k_val = low(low_back(mat_mul(x_in, w_k)))
    v_val = low(low_back(mat_mul(x_in, w_v)) + params['b_value'])
    n_rows = x_rows.shape[0]
    shape_four = (n_rows // SEQ, SEQ, HEADS, HD)
    attend = jax.checkpoint(partial(attend_one, student=student))
    ctx = lax.map(attend, (q_val.reshape(shape_four), k_val.reshape(shape_four), v_val.reshape(shape_four), lens))
    ctx = ctx.reshape(n_rows, D)
    if student:
        ctx_in = low(soft_clip(low_back(ctx), params['clip_context']))
    else:
        ctx_in = low(ctx)
    branch_a = low_back(mat_mul(ctx_in, w_o)) + params['b_output']
    h_one = layer_norm(x_rows + branch_a, params['ln_gains'][0], params['ln_shifts'][0])
    if student:
        h_in = low(soft_clip(h_one, params['clip_middle']))
    else:
        h_in = low(h_one)
    inner = low_back(mat_mul(h_in, w_i)) + params['b_inner']
    act = jax.nn.gelu(inner, approximate=False)
    if student:
        act_in = low(soft_clip(act, params['clip_hidden']))
    else:
        act_in = low(act)
    branch_f = low_back(mat_mul(act_in, w_u)) + params['b_outer']
    resid_two = h_one + branch_f
    out = layer_norm(resid_two, params['ln_gains'][1], params['ln_shifts'][1])
    return (out, resid_two, branch_a, branch_f)

def reference(tokens, cotangent, lengths, w_query, w_key, w_value, w_output, w_inner, w_outer, b_query, b_value, b_output, b_inner, b_outer, ln_gains, ln_shifts, clip_input, clip_context, clip_middle, clip_hidden, t_query, t_key, t_value, t_output, t_inner, t_outer, tb_query, tb_value, tb_output, tb_inner, tb_outer, t_gains, t_shifts):
    f_type = jnp.float32
    student = {'w_query': w_query, 'w_key': w_key, 'w_value': w_value, 'w_output': w_output, 'w_inner': w_inner, 'w_outer': w_outer, 'b_query': b_query, 'b_value': b_value, 'b_output': b_output, 'b_inner': b_inner, 'b_outer': b_outer, 'ln_gains': ln_gains, 'ln_shifts': ln_shifts, 'clip_input': clip_input, 'clip_context': clip_context, 'clip_middle': clip_middle, 'clip_hidden': clip_hidden}
    teacher = {'w_query': t_query.astype(f_type), 'w_key': t_key.astype(f_type), 'w_value': t_value.astype(f_type), 'w_output': t_output.astype(f_type), 'w_inner': t_inner.astype(f_type), 'w_outer': t_outer.astype(f_type), 'b_query': tb_query, 'b_value': tb_value, 'b_output': tb_output, 'b_inner': tb_inner, 'b_outer': tb_outer, 'ln_gains': t_gains, 'ln_shifts': t_shifts}
    group_rows = SEQS * SEQ
    x_groups = tokens.astype(f_type).reshape(N_DP, group_rows, D)
    c_groups = cotangent.astype(f_type).reshape(N_DP, group_rows, D)
    l_groups = lengths.reshape(N_DP, SEQS)

    def group(carry, item):
        x_grp, c_grp, l_grp = item
        t_out = layer(teacher, x_grp, l_grp, False)[0]
        keep = (jnp.arange(SEQ)[None, :] < l_grp[:, None]).reshape(group_rows, 1).astype(f_type)

        def objective(params, x_in):
            out, resid_two, branch_a, branch_f = layer(params, x_in, l_grp, True)
            diff = out - t_out
            loss_sum = jnp.sum(keep * diff * diff)
            total = jnp.sum(c_grp * out) + 0.5 * loss_sum
            sums = jnp.stack([loss_sum, jnp.sum(keep * resid_two * resid_two), jnp.sum(keep * branch_a * branch_a), jnp.sum(keep * branch_f * branch_f)])
            return (total, (out, sums))
        total, pull, (out, sums) = jax.vjp(objective, student, x_grp, has_aux=True)
        g_params, g_x = pull(jnp.ones_like(total))
        acc_grads, acc_sums = carry
        acc_grads = jax.tree.map(lambda a_val, b_val: a_val + b_val, acc_grads, g_params)
        return ((acc_grads, acc_sums + sums), (out.astype(jnp.bfloat16), g_x))
    init = (jax.tree.map(jnp.zeros_like, student), jnp.zeros((4,), f_type))
    (grads, sums), (outs, g_xs) = lax.scan(group, init, (x_groups, c_groups, l_groups))
    count = jnp.asarray(TOKENS * D, f_type)
    summary = jnp.stack([sums[0] / count, jnp.sqrt(sums[1] / count), jnp.sqrt(sums[2] / count), jnp.sqrt(sums[3] / count)])
    return (outs.reshape(TOKENS, D), g_xs.reshape(TOKENS, D), grads['w_query'], grads['w_key'], grads['w_value'], grads['w_output'], grads['w_inner'], grads['w_outer'], grads['b_query'], grads['b_value'], grads['b_output'], grads['b_inner'], grads['b_outer'], grads['ln_gains'], grads['ln_shifts'], grads['clip_input'], grads['clip_context'], grads['clip_middle'], grads['clip_hidden'], summary)
```

```python
from functools import partial
import math

import jax
import jax.numpy as jnp
from jax import lax
import jax.experimental.pallas as pl
import jax.experimental.pallas.tpu as pltpu
from jax.sharding import PartitionSpec as P

D = 768
FF = 3072
SEQ = 512
HD = 64
DH = D // 2
FH = FF // 2
QW = 3 * DH
PAIRS = 6
CH_W = 512
NCH = FH // CH_W
EPS = 1e-12

BI, CHD, TI, BQ, BV, CC, TQ, TV, VEND = 0, 1536, 3072, 4608, 4992, 5376, 5760, 6144, 6528
R_BO, R_BU, R_G0, R_G1, R_S0, R_S1, R_CI, R_CM, R_TBO, R_TBU, R_TG0, R_TG1, R_TS0, R_TS1 = range(14)

f32 = jnp.float32
bf16 = jnp.bfloat16
NT = (((1,), (1,)), ((), ()))
NN = (((1,), (0,)), ((), ()))
TN = (((0,), (0,)), ((), ()))
SDS = jax.ShapeDtypeStruct
VM = 60 * 2**20


def dot(left, right, dims=NN):
    return lax.dot_general(left, right, dims, preferred_element_type=f32)


def params():
    return pltpu.CompilerParams(vmem_limit_bytes=VM)


def whole(shape):
    rank = len(shape)
    return pl.BlockSpec(shape, lambda *_: (0,) * rank, pipeline_mode=pl.Buffered(1))


def norm(resid):
    centered = resid - jnp.mean(resid, -1, keepdims=True)
    inv = lax.rsqrt(jnp.mean(centered * centered, -1, keepdims=True) + EPS)
    return centered * inv, inv


def colsum(value):
    return jnp.sum(value, 0, keepdims=True)


def norm_back(e, normed, inv):
    return inv * (
        e - jnp.mean(e, -1, keepdims=True) - normed * jnp.mean(e * normed, -1, keepdims=True)
    )


def keep_rows(length):
    return (lax.broadcasted_iota(jnp.int32, (SEQ, 1), 0) < length).astype(f32)


def bin_cols(w, factor):
    return (jnp.mean(jnp.abs(w), 0, keepdims=True) * jnp.tanh(2.0 * w) * factor).astype(bf16)


def bin_rows(w, factor):
    return (jnp.mean(jnp.abs(w), 1, keepdims=True) * jnp.tanh(2.0 * w) * factor).astype(bf16)


def prep_kernel(wq, wk, wv, wo, wi, wu, qkv_o, wo_o, wi_o, wu_o):
    i = pl.program_id(0)
    root = 1.0 / math.sqrt(D)
    wi_o[...] = bin_cols(wi[...], root)
    wu_o[...] = bin_rows(wu[...], 1.0 / math.sqrt(FF))

    @pl.when(i < 3)
    def _():
        qkv_o[...] = bin_cols(wq[...], 2.0 * root)

    @pl.when((i >= 3) & (i < 6))
    def _():
        qkv_o[...] = bin_cols(wk[...], 2.0 * root)

    @pl.when((i >= 6) & (i < 9))
    def _():
        qkv_o[...] = bin_cols(wv[...], root)

    @pl.when(i >= 9)
    def _():
        wo_o[...] = bin_rows(wo[...], 8.0 * root)


def prep(wq, wk, wv, wo, wi, wu):
    col = lambda lo, n: pl.BlockSpec((D, 128), lambda i: (0, jnp.clip(i - lo, 0, n - 1)))
    row = lambda lo, n: pl.BlockSpec((128, D), lambda i: (jnp.clip(i - lo, 0, n - 1), 0))
    return pl.pallas_call(
        prep_kernel,
        grid=(12,),
        in_specs=[col(0, 3), col(3, 3), col(6, 3), row(9, 3), col(0, 12), row(0, 12)],
        out_specs=[col(0, 9), row(9, 3), col(0, 12), row(0, 12)],
        out_shape=[
            SDS((D, QW), bf16),
            SDS((DH, D), bf16),
            SDS((D, FH), bf16),
            SDS((FH, D), bf16),
        ],
        compiler_params=params(),
        name="prep",
    )(wq, wk, wv, wo, wi, wu)


def qkv_kernel(x, w_a, w_b, v_a, v_b, rep, out, *, student):
    xx = x[...]
    if student:
        clip = rep[R_CI : R_CI + 1, :]
        xx = (clip * jnp.tanh(xx.astype(f32) * (1.0 / clip))).astype(bf16)
    off_q, off_v = (BQ, BV) if student else (TQ, TV)
    for half, (w, v) in enumerate(((w_a, v_a), (w_b, v_b))):
        res = dot(xx, w[...])
        base = half * QW
        q = (res[:, :DH] + v[:, off_q : off_q + DH]).astype(bf16)
        out[:, base : base + DH] = q * jnp.asarray(HD**-0.5, bf16)
        out[:, base + DH : base + 2 * DH] = res[:, DH : 2 * DH].astype(bf16)
        out[:, base + 2 * DH : base + QW] = (
            res[:, 2 * DH :] + v[:, off_v : off_v + DH]
        ).astype(bf16)


def project(x, w_a, w_b, v_a, v_b, rep, student):
    rows = x.shape[0]
    return pl.pallas_call(
        partial(qkv_kernel, student=student),
        grid=(rows // SEQ,),
        in_specs=[
            pl.BlockSpec((SEQ, D), lambda i: (i, 0)),
            whole((D, QW)),
            whole((D, QW)),
            whole((1, VEND)),
            whole((1, VEND)),
            whole((14, D)),
        ],
        out_specs=pl.BlockSpec((SEQ, 2 * QW), lambda i: (i, 0)),
        out_shape=SDS((rows, 2 * QW), bf16),
        compiler_params=params(),
        name="project",
    )(x, w_a, w_b, v_a, v_b, rep)


def head_lanes(h):
    return lax.broadcasted_iota(jnp.int32, (1, 128), 1) // HD == h


def pair_of(value, h):
    return jnp.where(head_lanes(h), value, jnp.zeros((), value.dtype))


def masked(scores, length):
    return jnp.where(lax.broadcasted_iota(jnp.int32, (SEQ, 1), 0) < length, scores, -1e9)


def attn_kernel(lens, q, k, v, ctx, *lse, student):
    length = lens[pl.program_id(0)]
    qq, kk, vv = q[...], k[...], v[...]
    acc = None
    for h in range(2):
        s = masked(dot(pair_of(kk, h), qq, NT), length)
        top = jnp.max(s, 0, keepdims=True)
        e = jnp.exp(s - top)
        total = jnp.sum(e, 0, keepdims=True)
        p = (e * (1.0 / total)).astype(bf16)
        part = dot(pair_of(vv, h).T, p)
        acc = part if acc is None else acc + part
        if student:
            lse[0][0, h : h + 1, :] = top + jnp.log(total)
    ctx[...] = acc.T.astype(ctx.dtype)


def qkv_spec(part, order):
    def index(*ids):
        s, j = order(*ids[:2])
        return (s, (j // 3) * 9 + j % 3 + 3 * part)

    return pl.BlockSpec((SEQ, 128), index)


def attention(lens, qkv, student):
    rows = qkv.shape[0]
    nseq = rows // SEQ
    order = lambda s, j: (s, j)
    out_specs = [pl.BlockSpec((SEQ, 128), lambda s, j, *_: (s, j))]
    out_shape = [SDS((rows, D), f32 if student else bf16)]
    if student:
        out_specs.append(pl.BlockSpec((1, 2, SEQ), lambda s, j, *_: (s * PAIRS + j, 0, 0)))
        out_shape.append(SDS((nseq * PAIRS, 2, SEQ), f32))
    return pl.pallas_call(
        partial(attn_kernel, student=student),
        grid_spec=pltpu.PrefetchScalarGridSpec(
            num_scalar_prefetch=1,
            grid=(nseq, PAIRS),
            in_specs=[qkv_spec(0, order), qkv_spec(1, order), qkv_spec(2, order)],
            out_specs=out_specs,
        ),
        out_shape=out_shape,
        compiler_params=params(),
        name="attention",
    )(lens, qkv, qkv, qkv)


def post_kernel(lens, x, ctx, wo_a, wo_b, v_a, v_b, rep, *rest, student):
    wo = rest[-1]
    i = pl.program_id(0)

    @pl.when(i == 0)
    def _():
        wo[:DH, :] = wo_a[...]
        wo[DH:, :] = wo_b[...]

    row = lambda n: rep[n : n + 1, :]
    mine = x[...].astype(f32)
    if student:
        r1_o, h1_o, mid_o, sum_o = rest[:4]
        clip = jnp.concatenate([v_a[:, CC : CC + DH], v_b[:, CC : CC + DH]], 1)
        cin = (clip * jnp.tanh(ctx[...] * (1.0 / clip))).astype(bf16)
        branch = dot(cin, wo[...]) + row(R_BO)
        r1 = mine + branch
        normed, _ = norm(r1)
        h1 = normed * row(R_G0) + row(R_S0)
        cm = row(R_CM)
        r1_o[...] = r1
        h1_o[...] = h1
        mid_o[...] = (cm * jnp.tanh(h1 * (1.0 / cm))).astype(bf16)

        @pl.when(i == 0)
        def _():
            sum_o[...] = jnp.zeros_like(sum_o)

        sum_o[0:1, :] += colsum(keep_rows(lens[i]) * branch * branch)
    else:
        h1_o = rest[0]
        branch = dot(ctx[...], wo[...]) + row(R_TBO)
        normed, _ = norm(mine + branch)
        h1_o[...] = normed * row(R_TG0) + row(R_TS0)


def post(lens, x, ctx, wo_a, wo_b, v_a, v_b, rep, student):
    rows = x.shape[0]
    block = pl.BlockSpec((SEQ, D), lambda i, *_: (i, 0))
    out_specs = [block]
    out_shape = [SDS((rows, D), f32)]
    if student:
        out_specs = [block, block, block, pl.BlockSpec((8, D), lambda i, *_: (0, 0))]
        out_shape = [
            SDS((rows, D), f32),
            SDS((rows, D), f32),
            SDS((rows, D), bf16),
            SDS((8, D), f32),
        ]
    return pl.pallas_call(
        partial(post_kernel, student=student),
        grid_spec=pltpu.PrefetchScalarGridSpec(
            num_scalar_prefetch=1,
            grid=(rows // SEQ,),
            in_specs=[
                block,
                block,
                whole((DH, D)),
                whole((DH, D)),
                whole((1, VEND)),
                whole((1, VEND)),
                whole((14, D)),
            ],
            out_specs=out_specs,
            scratch_shapes=[pltpu.VMEM((D, D), bf16)],
        ),
        out_shape=out_shape,
        compiler_params=params(),
        name="post",
    )(lens, x, ctx, wo_a, wo_b, v_a, v_b, rep)


ROWS = 256


def ff_kernel(
    lens, h1, mid, th1, cot, wi_a, wi_b, wu_a, wu_b, ti_a, ti_b, tu_a, tu_b,
    bi_a, bi_b, ch_a, ch_b, tb_a, tb_b, rep,
    ain_o, mul_o, cv_o, lo_o, dr2_o, dfr_o, sum_o, acc_s, acc_t, tmid,
):
    c = pl.program_id(0)
    rows = h1.shape[0]

    @pl.when(c == 0)
    def _():
        acc_s[...] = jnp.zeros_like(acc_s)
        acc_t[...] = jnp.zeros_like(acc_t)
        tmid[...] = th1[...].astype(bf16)

    def chunk(wi, wu, ti, tu, bi, ch, tb):
        inv_clip = 1.0 / ch[...]

        def block(i, carry):
            r = pl.ds(pl.multiple_of(i * ROWS, ROWS), ROWS)
            inner = dot(mid[r, :], wi[...]) + bi[...]
            t_inner = dot(tmid[r, :], ti[...]) + tb[...]
            cdf = 0.5 * (1.0 + lax.erf(inner * (2.0**-0.5)))
            act = inner * cdf
            deriv = cdf + inner * (jnp.exp(-0.5 * inner * inner) * (1.0 / math.sqrt(2.0 * math.pi)))
            ratio = act * inv_clip
            th = jnp.tanh(ratio)
            slope = 1.0 - th * th
            ain = (ch[...] * th).astype(bf16)
            ain_o[r, :] = ain
            mul_o[r, :] = (slope * deriv).astype(bf16)
            cv_o[r, :] = (th - ratio * slope).astype(bf16)
            acc_s[r, :] += dot(ain, wu[...])
            t_act = (t_inner * (0.5 * (1.0 + lax.erf(t_inner * (2.0**-0.5))))).astype(bf16)
            acc_t[r, :] += dot(t_act, tu[...])
            return carry

        lax.fori_loop(0, rows // ROWS, block, 0)

    @pl.when(c < NCH)
    def _():
        chunk(wi_a, wu_a, ti_a, tu_a, bi_a, ch_a, tb_a)

    @pl.when(c >= NCH)
    def _():
        chunk(wi_b, wu_b, ti_b, tu_b, bi_b, ch_b, tb_b)

    @pl.when(c == 2 * NCH - 1)
    def _():
        row = lambda n: rep[n : n + 1, :]
        total = [jnp.zeros((1, D), f32)] * 6
        for s in range(rows // SEQ):
            r = slice(s * SEQ, (s + 1) * SEQ)
            keep = keep_rows(lens[s])
            branch = acc_s[r, :] + row(R_BU)
            r2 = h1[r, :] + branch
            normed, inv = norm(r2)
            out = normed * row(R_G1) + row(R_S1)
            t_normed, _ = norm(th1[r, :] + acc_t[r, :] + row(R_TBU))
            diff = keep * (out - (t_normed * row(R_TG1) + row(R_TS1)))
            d_out = cot[r, :].astype(f32) + diff
            dr2 = norm_back(d_out * row(R_G1), normed, inv)
            lo_o[r, :] = out.astype(bf16)
            dr2_o[r, :] = dr2
            dfr_o[r, :] = dr2.astype(bf16)
            parts = (
                d_out * normed, d_out, dr2, diff * diff, keep * r2 * r2, keep * branch * branch,
            )
            total = [t + colsum(p) for t, p in zip(total, parts)]
        for n in range(6):
            sum_o[n : n + 1, :] = total[n]
        sum_o[6:8, :] = jnp.zeros((2, D), f32)


def half_col(half, width, base=0):
    lo = half * NCH
    return pl.BlockSpec((width, CH_W), lambda c, *_: (0, base + jnp.clip(c - lo, 0, NCH - 1)))


def half_row(half):
    lo = half * NCH
    return pl.BlockSpec((CH_W, D), lambda c, *_: (jnp.clip(c - lo, 0, NCH - 1), 0))


def feed_forward(lens, h1, mid, th1, cot, wi, wu, ti, tu, v_a, v_b, rep):
    rows = h1.shape[0]
    full = whole((rows, D))
    chunk_out = pl.BlockSpec((rows, CH_W), lambda c, *_: (0, c))
    return pl.pallas_call(
        ff_kernel,
        grid_spec=pltpu.PrefetchScalarGridSpec(
            num_scalar_prefetch=1,
            grid=(2 * NCH,),
            in_specs=[
                full, full, full, full,
                half_col(0, D), half_col(1, D), half_row(0), half_row(1),
                half_col(0, D), half_col(1, D), half_row(0), half_row(1),
                half_col(0, 1, BI // CH_W), half_col(1, 1, BI // CH_W),
                half_col(0, 1, CHD // CH_W), half_col(1, 1, CHD // CH_W),
                half_col(0, 1, TI // CH_W), half_col(1, 1, TI // CH_W),
                whole((14, D)),
            ],
            out_specs=[chunk_out, chunk_out, chunk_out, full, full, full, whole((8, D))],
            scratch_shapes=[
                pltpu.VMEM((rows, D), f32),
                pltpu.VMEM((rows, D), f32),
                pltpu.VMEM((rows, D), bf16),
            ],
        ),
        out_shape=[
            SDS((rows, FF), bf16),
            SDS((rows, FF), bf16),
            SDS((rows, FF), bf16),
            SDS((rows, D), bf16),
            SDS((rows, D), f32),
            SDS((rows, D), bf16),
            SDS((8, D), f32),
        ],
        compiler_params=params(),
        name="feed_forward",
    )(
        lens, h1, mid, th1, cot, wi[0], wi[1], wu[0], wu[1], ti[0], ti[1], tu[0], tu[1],
        v_a, v_b, v_a, v_b, v_a, v_b, rep,
    )


def ff_back_kernel(*refs, first):
    if first:
        dfr, mid, ain, mul, cv, wi, wu, gu_o, gi_o, sum_o, dh_o, mid_t = refs
    else:
        dfr, mid, ain, mul, cv, wi, wu, before, gu_o, gi_o, sum_o, dh_o, mid_t = refs
    c = pl.program_id(0)

    @pl.when(c == 0)
    def _():
        mid_t[...] = mid[...].T
        dh_o[...] = jnp.zeros_like(dh_o) if first else before[...]

    gu_o[...] = dot(ain[...], dfr[...], TN).astype(bf16)
    d_ain = dot(dfr[...], wu[...], NT)
    sum_o[1:2, :] = colsum(d_ain * cv[...].astype(f32))
    d_inner = d_ain * mul[...].astype(f32)
    sum_o[0:1, :] = colsum(d_inner)
    sum_o[2:8, :] = jnp.zeros((6, CH_W), f32)
    dir_low = d_inner.astype(bf16)
    gi_o[...] = dot(mid_t[...], dir_low).astype(bf16)
    dh_o[...] += dot(dir_low, wi[...], NT)


def ff_back(half, dfr, mid, ain, mul, cv, wi, wu, before):
    rows = dfr.shape[0]
    full = whole((rows, D))
    chunk = pl.BlockSpec((rows, CH_W), lambda c: (0, half * NCH + c))
    col = pl.BlockSpec((D, CH_W), lambda c: (0, c))
    row = pl.BlockSpec((CH_W, D), lambda c: (c, 0))
    extra = [] if before is None else [before]
    return pl.pallas_call(
        partial(ff_back_kernel, first=before is None),
        grid=(NCH,),
        in_specs=[full, full, chunk, chunk, chunk, col, row] + [full] * len(extra),
        out_specs=[row, col, pl.BlockSpec((8, CH_W), lambda c: (0, c)), full],
        out_shape=[
            SDS((FH, D), bf16),
            SDS((D, FH), bf16),
            SDS((8, FH), f32),
            SDS((rows, D), f32),
        ],
        scratch_shapes=[pltpu.VMEM((D, rows), bf16)],
        compiler_params=params(),
        name="ff_back",
    )(dfr, mid, ain, mul, cv, wi, wu, *extra)


def mid_back_kernel(
    r1, dr2, dhin, ctx, wo_a, wo_b, v_a, v_b, rep, dr1_o, dcr_o, go_a, go_b, sum_o, wo, acc
):
    i = pl.program_id(0)

    @pl.when(i == 0)
    def _():
        wo[:DH, :] = wo_a[...]
        wo[DH:, :] = wo_b[...]
        acc[...] = jnp.zeros_like(acc)
        sum_o[...] = jnp.zeros_like(sum_o)

    row = lambda n: rep[n : n + 1, :]
    normed, inv = norm(r1[...])
    cm = row(R_CM)
    ratio = (normed * row(R_G0) + row(R_S0)) * (1.0 / cm)
    th = jnp.tanh(ratio)
    slope = 1.0 - th * th
    d_hin = dhin[...]
    sum_o[3:4, :] += colsum(d_hin * (th - ratio * slope))
    dh1 = dr2[...] + d_hin * slope
    sum_o[0:1, :] += colsum(dh1 * normed)
    sum_o[1:2, :] += colsum(dh1)
    dr1 = norm_back(dh1 * row(R_G0), normed, inv)
    sum_o[2:3, :] += colsum(dr1)
    dr1_o[...] = dr1
    dar = dr1.astype(bf16)
    clip = jnp.concatenate([v_a[:, CC : CC + DH], v_b[:, CC : CC + DH]], 1)
    ratio = ctx[...] * (1.0 / clip)
    th = jnp.tanh(ratio)
    slope = 1.0 - th * th
    acc[...] += dot(dar, (clip * th).astype(bf16), TN)
    d_cin = dot(dar, wo[...], NT)
    sum_o[4:5, :] += colsum(d_cin * (th - ratio * slope))
    dcr_o[...] = (d_cin * slope).astype(bf16)

    @pl.when(i == pl.num_programs(0) - 1)
    def _():
        go_a[...] = acc[:, :DH].astype(bf16)
        go_b[...] = acc[:, DH:].astype(bf16)


def mid_back(r1, dr2, dhin, ctx, wo_a, wo_b, v_a, v_b, rep):
    rows = r1.shape[0]
    block = pl.BlockSpec((SEQ, D), lambda i: (i, 0))
    return pl.pallas_call(
        mid_back_kernel,
        grid=(rows // SEQ,),
        in_specs=[block] * 4
        + [whole((DH, D)), whole((DH, D)), whole((1, VEND)), whole((1, VEND)), whole((14, D))],
        out_specs=[block, block, whole((D, DH)), whole((D, DH)), whole((8, D))],
        out_shape=[
            SDS((rows, D), f32),
            SDS((rows, D), bf16),
            SDS((D, DH), bf16),
            SDS((D, DH), bf16),
            SDS((8, D), f32),
        ],
        scratch_shapes=[pltpu.VMEM((D, D), bf16), pltpu.VMEM((D, D), f32)],
        compiler_params=params(),
        name="mid_back",
    )(r1, dr2, dhin, ctx, wo_a, wo_b, v_a, v_b, rep)


def attn_back_kernel(lens, q, k, v, dc, lse, dq, dk, dv, sum_o):
    seq = pl.program_id(1)
    length = lens[seq]
    qq, kk, vv, cc = q[...], k[...], v[...], dc[...]
    acc = None
    for h in range(2):
        k_h = pair_of(kk, h)
        s = masked(dot(k_h, qq, NT), length)
        p = jnp.exp(s - lse[0, h : h + 1, :])
        dp = dot(pair_of(vv, h), cc, NT)
        pd = p * dp
        ds = (pd - p * jnp.sum(pd, 0, keepdims=True)).astype(bf16)
        part = (
            dot(k_h.T, ds),
            dot(ds, pair_of(qq, h)),
            dot(p.astype(bf16), pair_of(cc, h)),
        )
        acc = part if acc is None else tuple(a + b for a, b in zip(acc, part))
    d_q = acc[0].T * HD**-0.5
    dq[...] = d_q.astype(bf16)
    dk[...] = acc[1].astype(bf16)
    dv[...] = acc[2].astype(bf16)

    @pl.when(seq == 0)
    def _():
        sum_o[...] = jnp.zeros_like(sum_o)

    sum_o[0:1, :] += colsum(d_q)
    sum_o[1:2, :] += colsum(acc[2])


def attention_back(lens, qkv, dcr, lse):
    rows = qkv.shape[0]
    nseq = rows // SEQ
    order = lambda j, s: (s, j)
    block = pl.BlockSpec((SEQ, 128), lambda j, s, *_: (s, j))
    return pl.pallas_call(
        attn_back_kernel,
        grid_spec=pltpu.PrefetchScalarGridSpec(
            num_scalar_prefetch=1,
            grid=(PAIRS, nseq),
            in_specs=[
                qkv_spec(0, order),
                qkv_spec(1, order),
                qkv_spec(2, order),
                block,
                pl.BlockSpec((1, 2, SEQ), lambda j, s, *_: (s * PAIRS + j, 0, 0)),
            ],
            out_specs=[block, block, block, pl.BlockSpec((8, 128), lambda j, s, *_: (0, j))],
        ),
        out_shape=[SDS((rows, D), bf16)] * 3 + [SDS((8, D), f32)],
        compiler_params=params(),
        name="attention_back",
    )(lens, qkv, qkv, qkv, dcr, lse)


def clip_in(x, rep):
    clip = rep[R_CI : R_CI + 1, :]
    ratio = x[...].astype(f32) * (1.0 / clip)
    th = jnp.tanh(ratio)
    return clip, ratio, th


def attn_grad_kernel(x, dq, dk, dv, got, rep, out, d_all):
    clip, _, th = clip_in(x, rep)
    xin = (clip * th).astype(bf16)
    d_all[:, :DH] = dq[...]
    d_all[:, DH : 2 * DH] = dk[...]
    d_all[:, 2 * DH :] = dv[...]
    res = dot(xin, d_all[...], TN).astype(bf16)
    for c in range(3):
        out[:, c * CH_W : c * CH_W + DH] = res[:, c * DH : (c + 1) * DH]
        out[:, c * CH_W + DH : (c + 1) * CH_W] = got[:, c * 128 : (c + 1) * 128]


def attn_grad(half, x, dq, dk, dv, got, rep):
    rows = x.shape[0]
    col = pl.BlockSpec((rows, DH), lambda i: (0, half))
    return pl.pallas_call(
        attn_grad_kernel,
        grid=(1,),
        in_specs=[whole((rows, D)), col, col, col, whole((D, DH)), whole((14, D))],
        out_specs=whole((D, FH)),
        out_shape=SDS((D, FH), bf16),
        scratch_shapes=[pltpu.VMEM((rows, QW), bf16)],
        compiler_params=params(),
        name="attn_grad",
    )(x, dq, dk, dv, got, rep)


def x_back_kernel(x, dq, dk, dv, dr1, w_a, w_b, rep, grad_o, sum_o, d_all):
    total = None
    for half, w in enumerate((w_a, w_b)):
        cols = slice(half * DH, (half + 1) * DH)
        d_all[:, :DH] = dq[:, cols]
        d_all[:, DH : 2 * DH] = dk[:, cols]
        d_all[:, 2 * DH :] = dv[:, cols]
        part = dot(d_all[...], w[...], NT)
        total = part if total is None else total + part
    _, ratio, th = clip_in(x, rep)
    slope = 1.0 - th * th
    grad_o[...] = dr1[...] + total * slope

    @pl.when(pl.program_id(0) == 0)
    def _():
        sum_o[...] = jnp.zeros_like(sum_o)

    sum_o[0:1, :] += colsum(total * (th - ratio * slope))


def x_back(x, dq, dk, dv, dr1, w_a, w_b, rep):
    rows = x.shape[0]
    block = pl.BlockSpec((SEQ, D), lambda i: (i, 0))
    return pl.pallas_call(
        x_back_kernel,
        grid=(rows // SEQ,),
        in_specs=[block] * 5 + [whole((D, QW)), whole((D, QW)), whole((14, D))],
        out_specs=[block, whole((8, D))],
        out_shape=[SDS((rows, D), f32), SDS((8, D), f32)],
        scratch_shapes=[pltpu.VMEM((SEQ, QW), bf16)],
        compiler_params=params(),
        name="x_back",
    )(x, dq, dk, dv, dr1, w_a, w_b, rep)


BLOCKS = 16


def spread(order, r):
    return sum(mask for p, mask in enumerate(order) if r & (BLOCKS >> (p + 1)))


def fold_kernel(me, own, got, *outs, orders):
    width = own.shape[2] // 3
    for c, order in enumerate(orders):
        high, low = outs[2 * c], outs[2 * c + 1]
        cols = slice(c * width, (c + 1) * width)
        for r in range(BLOCKS):
            src = me[0] ^ spread(order, r)
            value = own[src, :, cols].astype(f32) + got[src, :, cols].astype(f32)
            if r >= BLOCKS // 2:
                high[r - BLOCKS // 2] = value.astype(bf16)
            else:
                low[r] = value.astype(bf16)


def fold(me, own, got, orders):
    rows, cols = own.shape
    shape = (BLOCKS, rows // BLOCKS, cols)
    piece = (BLOCKS // 2, rows // BLOCKS, cols // 3)
    return pl.pallas_call(
        partial(fold_kernel, orders=orders),
        grid_spec=pltpu.PrefetchScalarGridSpec(
            num_scalar_prefetch=1,
            grid=(1,),
            in_specs=[whole(shape), whole(shape)],
            out_specs=[whole(piece)] * 6,
        ),
        out_shape=[SDS(piece, bf16)] * 6,
        compiler_params=params(),
        name="fold",
    )(me, own.reshape(shape), got.reshape(shape))


def swap(value, mask, n_dp):
    return lax.ppermute(value, "dp", [(i, i ^ mask) for i in range(n_dp)])


def reduce_chunks(me, own, got, orders, n_dp):
    pieces = fold(me, own, got, orders)
    send, hold = list(pieces[0::2]), list(pieces[1::2])
    for step in range(4):
        recv = [swap(s, o[step], n_dp) for s, o in zip(send, orders)]
        half = hold[0].shape[0] // 2
        if half:
            send = [h[half:] + r[half:] for h, r in zip(hold, recv)]
            hold = [h[:half] + r[:half] for h, r in zip(hold, recv)]
        else:
            hold = [h + r for h, r in zip(hold, recv)]
    mask = BLOCKS
    while mask < n_dp:
        hold = [h + swap(h, mask, n_dp) for h in hold]
        mask *= 2
    for step in (3, 2, 1):
        recv = [swap(h, o[step], n_dp) for h, o in zip(hold, orders)]
        hold = [jnp.concatenate([h, r], 0) for h, r in zip(hold, recv)]
    recv = [swap(h, o[0], n_dp) for h, o in zip(hold, orders)]
    return [piece for pair in zip(hold, recv) for piece in pair]


def sum_all(value, n_dp):
    mask = 1
    while mask < n_dp:
        value = value + swap(value, mask, n_dp)
        mask *= 2
    return value


def latent(w, g, axis, factor):
    th = jnp.tanh(2.0 * w)
    n = w.shape[axis]
    mean = jnp.sum(jnp.abs(w), axis, keepdims=True) * (1.0 / n)
    inner = jnp.sum(g * th, axis, keepdims=True) * (1.0 / n)
    sign = jnp.where(w > 0, 1.0, jnp.where(w < 0, -1.0, 0.0))
    return factor * (2.0 * mean * (1.0 - th * th) * g + sign * inner)


def collect(me, mine, recv, order, store):
    for r in range(BLOCKS):
        block = (mine[r] if r < BLOCKS // 2 else recv[r - BLOCKS // 2]).astype(f32)
        store(me ^ spread(order, r), block)


def inner_latent_kernel(me, *refs, orders):
    w, out, g = refs[6:]
    for c, order in enumerate(orders):

        @pl.when(pl.program_id(0) == c)
        def _():
            def store(dst, block):
                g[dst] = block

            collect(me[0], refs[2 * c], refs[2 * c + 1], order, store)

    out[...] = latent(w[...], g[...].reshape(w.shape), 0, 1.0 / math.sqrt(D))


def inner_latent(me, pieces, w, orders):
    piece = pieces[0].shape
    col = pl.BlockSpec((D, CH_W), lambda c, *_: (0, c))
    return pl.pallas_call(
        partial(inner_latent_kernel, orders=orders),
        grid_spec=pltpu.PrefetchScalarGridSpec(
            num_scalar_prefetch=1,
            grid=(3,),
            in_specs=[whole(piece)] * 6 + [col],
            out_specs=col,
            scratch_shapes=[pltpu.VMEM((BLOCKS,) + piece[1:], f32)],
        ),
        out_shape=SDS((D, FH), f32),
        compiler_params=params(),
        name="inner_latent",
    )(me, *pieces, w)


def outer_latent_kernel(me, *refs, orders):
    w, out, g = refs[6:]
    width = g.shape[2] // 3

    @pl.when(pl.program_id(0) == 0)
    def _():
        for c, order in enumerate(orders):

            def store(dst, block):
                g[dst, :, c * width : (c + 1) * width] = block

            collect(me[0], refs[2 * c], refs[2 * c + 1], order, store)

    n = BLOCKS // 4
    part = g[pl.ds(pl.program_id(0) * n, n)].reshape(w.shape)
    out[...] = latent(w[...], part, 1, 1.0 / math.sqrt(FF))


def outer_latent(me, pieces, w, orders):
    piece = pieces[0].shape
    row = pl.BlockSpec((FH // 4, D), lambda c, *_: (c, 0))
    return pl.pallas_call(
        partial(outer_latent_kernel, orders=orders),
        grid_spec=pltpu.PrefetchScalarGridSpec(
            num_scalar_prefetch=1,
            grid=(4,),
            in_specs=[whole(piece)] * 6 + [row],
            out_specs=row,
            scratch_shapes=[pltpu.VMEM((BLOCKS, piece[1], 3 * piece[2]), f32)],
        ),
        out_shape=SDS((FH, D), f32),
        compiler_params=params(),
        name="outer_latent",
    )(me, *pieces, w)


def attn_latent_kernel(me, *refs, orders):
    w_in = refs[6:9]
    wo = refs[9]
    outs = refs[10:13]
    go, g = refs[13:]
    root = 1.0 / math.sqrt(D)
    for c, order in enumerate(orders):

        def store(dst, block):
            g[dst] = block

        collect(me[0], refs[2 * c], refs[2 * c + 1], order, store)
        grad = g[...].reshape(D, CH_W)
        outs[c][...] = latent(w_in[c][...], grad[:, :DH], 0, root if c == 2 else 2.0 * root)
        r = slice(c * 128, (c + 1) * 128)
        go[r, :] = latent(wo[r, :], grad[:, DH:].T, 1, 8.0 * root)


def attn_latent(me, pieces, wq, wk, wv, wo, orders):
    piece = pieces[0].shape
    col, row = whole((D, DH)), whole((DH, D))
    return pl.pallas_call(
        partial(attn_latent_kernel, orders=orders),
        grid_spec=pltpu.PrefetchScalarGridSpec(
            num_scalar_prefetch=1,
            grid=(1,),
            in_specs=[whole(piece)] * 6 + [col, col, col, row],
            out_specs=[col, col, col, row],
            scratch_shapes=[pltpu.VMEM((BLOCKS,) + piece[1:], f32)],
        ),
        out_shape=[SDS((D, DH), f32)] * 3 + [SDS((DH, D), f32)],
        compiler_params=params(),
        name="attn_latent",
    )(me, *pieces, wq, wk, wv, wo)


def on_device(
    n_dp,
    tokens, cotangent, lengths, w_query, w_key, w_value, w_output, w_inner, w_outer,
    b_query, b_value, b_output, b_inner, b_outer, ln_gains, ln_shifts,
    clip_input, clip_context, clip_middle, clip_hidden,
    t_query, t_key, t_value, t_output, t_inner, t_outer,
    tb_query, tb_value, tb_output, tb_inner, tb_outer, t_gains, t_shifts,
):
    other = lambda value: lax.ppermute(value, "tensor", [(0, 1), (1, 0)])
    rows = tokens.shape[0]
    nseq = rows // SEQ
    tensor_pos = lax.axis_index("tensor")
    me = lax.axis_index("dp").astype(jnp.int32).reshape(1)
    lens = lax.dynamic_slice(lengths, (tensor_pos * nseq,), (nseq,))
    orders = ((1, 2, 4, 8), (2, 4, 1, 8), (4, 1, 2, 8))

    v_a = jnp.concatenate(
        [b_inner, clip_hidden, tb_inner, b_query, b_value, clip_context, tb_query, tb_value]
    ).reshape(1, VEND)
    rep = jnp.stack(
        [
            b_output, b_outer, ln_gains[0], ln_gains[1], ln_shifts[0], ln_shifts[1],
            clip_input, clip_middle, tb_output, tb_outer,
            t_gains[0], t_gains[1], t_shifts[0], t_shifts[1],
        ]
    )
    t_qkv = jnp.concatenate([t_query, t_key, t_value], 1)
    v_b = other(v_a)
    t_qkv_b = other(t_qkv)
    t_out_b = other(t_output)
    wqkv, wo, wi, wu = prep(w_query, w_key, w_value, w_output, w_inner, w_outer)
    wqkv_b, wo_b = other(wqkv), other(wo)
    ti_b, tu_b = other(t_inner), other(t_outer)
    wi_b, wu_b = other(wi), other(wu)

    t_proj = project(tokens, t_qkv, t_qkv_b, v_a, v_b, rep, False)
    (t_ctx,) = attention(lens, t_proj, False)
    (th1,) = post(lens, tokens, t_ctx, t_output, t_out_b, v_a, v_b, rep, False)
    qkv = project(tokens, wqkv, wqkv_b, v_a, v_b, rep, True)
    ctx, lse = attention(lens, qkv, True)
    r1, h1, mid, sum_a = post(lens, tokens, ctx, wo, wo_b, v_a, v_b, rep, True)
    ain, mul, cv, layer_out, dr2, dfr, sum_f = feed_forward(
        lens, h1, mid, th1, cotangent, (wi, wi_b), (wu, wu_b), (t_inner, ti_b), (t_outer, tu_b),
        v_a, v_b, rep,
    )
    gu_b, gi_b, sum_hb, dh_b = ff_back(1, dfr, mid, ain, mul, cv, wi_b, wu_b, None)
    gu_a, gi_a, sum_ha, dhin = ff_back(0, dfr, mid, ain, mul, cv, wi, wu, dh_b)
    gu = reduce_chunks(me, gu_a, other(gu_b), orders, n_dp)
    gi = reduce_chunks(me, gi_a, other(gi_b), orders, n_dp)

    dr1, dcr, go_a, go_b, sum_m = mid_back(r1, dr2, dhin, ctx, wo, wo_b, v_a, v_b, rep)
    dq, dk, dv, sum_q = attention_back(lens, qkv, dcr, lse)
    gs_b = attn_grad(1, tokens, dq, dk, dv, go_b, rep)
    gs_a = attn_grad(0, tokens, dq, dk, dv, go_a, rep)
    gs = reduce_chunks(me, gs_a, other(gs_b), orders, n_dp)
    grad_tokens, sum_x = x_back(tokens, dq, dk, dv, dr1, wqkv, wqkv_b, rep)

    sides = [
        jnp.concatenate(
            [h[0], h[1], sum_q[0, cols], sum_q[1, cols], sum_m[4, cols]]
        )
        for h, cols in ((sum_ha, slice(0, DH)), (sum_hb, slice(DH, D)))
    ]
    stats = jnp.stack([jnp.sum(sum_f[3]), jnp.sum(sum_f[4]), jnp.sum(sum_a[0]), jnp.sum(sum_f[5])])
    shared = jnp.concatenate(
        [
            sum_m[2], sum_f[2], sum_m[0], sum_f[0], sum_m[1], sum_f[1], sum_x[0], sum_m[3],
            jnp.pad(stats, (0, 124)),
        ]
    )
    n_split = sides[0].shape[0]
    from_other = other(jnp.concatenate([sides[1], shared]))
    small = sum_all(jnp.concatenate([sides[0], shared]) + from_other, n_dp)
    split, shared = small[:n_split], small[n_split:]

    g_outer = outer_latent(me, gu, w_outer, orders)
    g_inner = inner_latent(me, gi, w_inner, orders)
    g_query, g_key, g_value, g_output = attn_latent(
        me, gs, w_query, w_key, w_value, w_output, orders
    )
    count = jnp.asarray(rows * 2 * n_dp * D, f32)
    stats = shared[8 * D : 8 * D + 4] / count
    summary = jnp.concatenate([stats[:1], jnp.sqrt(stats[1:])])
    return (
        layer_out,
        grad_tokens,
        g_query,
        g_key,
        g_value,
        g_output,
        g_inner,
        g_outer,
        split[2 * FH : 2 * FH + DH],
        split[2 * FH + DH : 2 * FH + 2 * DH],
        shared[:D],
        split[:FH],
        shared[D : 2 * D],
        shared[2 * D : 4 * D].reshape(2, D),
        shared[4 * D : 6 * D].reshape(2, D),
        shared[6 * D : 7 * D],
        split[2 * FH + 2 * DH :],
        shared[7 * D : 8 * D],
        split[FH : 2 * FH],
        summary,
    )


def solution(mesh):
    rows, cols, split, full = P(("dp", "tensor"), None), P(None, "tensor"), P("tensor"), P()
    down = P("tensor", None)
    return jax.shard_map(
        partial(on_device, mesh.shape["dp"]),
        mesh=mesh,
        in_specs=(
            rows, rows, P("dp"), cols, cols, cols, down, cols, down,
            split, split, full, split, full, full, full,
            full, split, full, split,
            cols, cols, cols, down, cols, down,
            split, split, full, split, full, full, full,
        ),
        out_specs=(
            rows, rows, cols, cols, cols, down, cols, down,
            split, split, full, split, full, full, full, full, split, full, split, full,
        ),
        check_vma=False,
    )
```

```python
from functools import partial
import math

import jax
import jax.numpy as jnp
from jax import lax
import jax.experimental.pallas as pl
import jax.experimental.pallas.tpu as pltpu
from jax.sharding import PartitionSpec as P

D = 768
FF = 3072
SEQ = 512
HD = 64
DH = D // 2
FH = FF // 2
QW = 3 * DH

CH_W = 512
NCH = FH // CH_W
EPS = 1e-12

BI, CHD, TI, BQ, BV, CC, TQ, TV, VEND = 0, 1536, 3072, 4608, 4992, 5376, 5760, 6144, 6528
R_BO, R_BU, R_G0, R_G1, R_S0, R_S1, R_CI, R_CM, R_TBO, R_TBU, R_TG0, R_TG1, R_TS0, R_TS1 = range(14)

f32 = jnp.float32
bf16 = jnp.bfloat16
NT = (((1,), (1,)), ((), ()))
NN = (((1,), (0,)), ((), ()))
TN = (((0,), (0,)), ((), ()))
SDS = jax.ShapeDtypeStruct
VM = 60 * 2**20


def dot(left, right, dims=NN):
    return lax.dot_general(left, right, dims, preferred_element_type=f32)


def params():
    return pltpu.CompilerParams(vmem_limit_bytes=VM)


def cost(micros):
    return pl.CostEstimate(
        flops=micros * 10**9, transcendentals=0, bytes_accessed=micros * 3 * 10**6
    )


def whole(shape):
    rank = len(shape)
    return pl.BlockSpec(shape, lambda *_: (0,) * rank, pipeline_mode=pl.Buffered(1))


def norm(resid):
    centered = resid - jnp.mean(resid, -1, keepdims=True)
    inv = lax.rsqrt(jnp.mean(centered * centered, -1, keepdims=True) + EPS)
    return centered * inv, inv


def colsum(value):
    return jnp.sum(value, 0, keepdims=True)


def norm_back(e, normed, inv):
    return inv * (
        e - jnp.mean(e, -1, keepdims=True) - normed * jnp.mean(e * normed, -1, keepdims=True)
    )


def keep_rows(length):
    return (lax.broadcasted_iota(jnp.int32, (SEQ, 1), 0) < length).astype(f32)


def bin_cols(w, factor):
    return (jnp.mean(jnp.abs(w), 0, keepdims=True) * jnp.tanh(2.0 * w) * factor).astype(bf16)


def bin_rows(w, factor):
    return (jnp.mean(jnp.abs(w), 1, keepdims=True) * jnp.tanh(2.0 * w) * factor).astype(bf16)


SPLIT = (FH, FH, FH, DH, DH, DH, DH, DH)


def prep_kernel(*refs):
    wq, wk, wv, wo, wi, wu = refs[:6]
    split = refs[6:14]
    full = refs[14:24]
    qkv_o, wo_o, wi_o, wu_o, vec_o, rep_o = refs[24:]
    i = pl.program_id(0)
    root = 1.0 / math.sqrt(D)
    wi_o[...] = bin_cols(wi[...], root)
    wu_o[...] = bin_rows(wu[...], 1.0 / math.sqrt(FF))

    @pl.when(i == 0)
    def _():
        qkv_o[:, :DH] = bin_cols(wq[...], 2.0 * root)
        at = 0
        for ref, n in zip(split, SPLIT):
            vec_o[0, at : at + n] = ref[...]
            at += n
        at = 0
        for ref in full:
            if len(ref.shape) == 1:
                rep_o[at, :] = ref[...]
                at += 1
            else:
                rep_o[at : at + 2, :] = ref[...]
                at += 2

    @pl.when(i == 1)
    def _():
        qkv_o[:, DH : 2 * DH] = bin_cols(wk[...], 2.0 * root)

    @pl.when(i == 2)
    def _():
        qkv_o[:, 2 * DH :] = bin_cols(wv[...], root)

    @pl.when(i == 3)
    def _():
        wo_o[...] = bin_rows(wo[...], 8.0 * root)


def prep(weights, split, full):
    n = 4
    col = pl.BlockSpec((D, FH // n), lambda i: (0, i))
    row = pl.BlockSpec((FH // n, D), lambda i: (i, 0))
    return pl.pallas_call(
        prep_kernel,
        grid=(n,),
        in_specs=[whole((D, DH))] * 3
        + [whole((DH, D)), col, row]
        + [whole(v.shape) for v in (*split, *full)],
        out_specs=[
            whole((D, QW)), whole((DH, D)), col, row, whole((1, VEND)), whole((14, D)),
        ],
        out_shape=[
            SDS((D, QW), bf16),
            SDS((DH, D), bf16),
            SDS((D, FH), bf16),
            SDS((FH, D), bf16),
            SDS((1, VEND), f32),
            SDS((14, D), f32),
        ],
        compiler_params=params(),
        name="prep",
        cost_estimate=cost(8),
    )(*weights, *split, *full)


def head_lanes(h):
    return lax.broadcasted_iota(jnp.int32, (1, 128), 1) // HD == h


def pair_of(value, h):
    return jnp.where(head_lanes(h), value, jnp.zeros((), value.dtype))


def with_mask(qq, kk, length, h):
    lane = lax.broadcasted_iota(jnp.int32, (1, 128), 1)
    spare = lane == HD * (1 - h)
    valid = lax.broadcasted_iota(jnp.int32, (SEQ, 1), 0) < length
    bias = jnp.where(valid, 0.0, -1e9).astype(bf16)
    k_h = jnp.where(spare, bias, pair_of(kk, h))
    return jnp.where(spare, jnp.ones((), bf16), qq), k_h


def attend(length, qkv_half, store):
    heads = [(half, p, h) for half in range(2) for p in range(3) for h in range(2)]

    def score(half, p, h):
        ref, base = qkv_half(half)
        at = base + p * 128
        q_h, k_h = with_mask(ref[:, at : at + 128], ref[:, at + DH : at + DH + 128], length, h)
        return dot(k_h, q_h, NT)

    ones = jnp.ones((16, SEQ), bf16)
    scores = [score(*heads[0]), score(*heads[1])]
    pair = []
    for i, (half, p, h) in enumerate(heads):
        if i + 2 < len(heads):
            scores.append(score(*heads[i + 2]))
        s = scores[i]
        top = jnp.max(s, 0, keepdims=True)
        e = jnp.exp(s - top).astype(bf16)
        ref, base = qkv_half(half)
        if h == 0:
            at = base + 2 * DH + p * 128
            v_t = ref[:, at : at + 128].T
        part = dot(jnp.concatenate([v_t[h * HD : (h + 1) * HD], ones], 0), e)
        total = part[HD : HD + 1]
        pair.append(part[:HD] * (1.0 / total))
        store(half, p, h, pair, top, total)
        if h:
            pair = []


def encode_kernel(lens, first, x, *refs, student):
    n = 1 if student else 3
    weights, refs = refs[: 2 * n], refs[2 * n :]
    wo_a, wo_b, v_a, v_b, rep = refs[:5]
    if student:
        qkv, ctx, lse, r1_o, h1_o, mid_o, xt_o, sum_o, wo = refs[5:]
    else:
        h1_o, mid_o, wo, qkv, ctx, w_all = refs[5:]
    i = pl.program_id(0)

    @pl.when(i == 0)
    def _():
        wo[:DH, :] = wo_a[...]
        wo[DH:, :] = wo_b[...]
        if student:
            sum_o[...] = jnp.zeros_like(sum_o)
        else:
            for k in range(6):
                w_all[:, k * DH : (k + 1) * DH] = weights[k][...]

    row = lambda k: rep[k : k + 1, :]
    length = lens[first[0] + i]
    xx = x[...]
    mine = xx.astype(f32)
    if student:
        clip = row(R_CI)
        xx = (clip * jnp.tanh(mine * (1.0 / clip))).astype(bf16)
        xt_o[...] = xx.T
    off_q, off_v = (BQ, BV) if student else (TQ, TV)
    for half, v in enumerate((v_a, v_b)):
        base = half * QW
        res = dot(xx, weights[half][...] if student else w_all[:, base : base + QW])
        q = (res[:, :DH] + v[:, off_q : off_q + DH]).astype(bf16)
        qkv[:, base : base + DH] = q * jnp.asarray(HD**-0.5, bf16)
        qkv[:, base + DH : base + 2 * DH] = res[:, DH : 2 * DH].astype(bf16)
        qkv[:, base + 2 * DH : base + QW] = (
            res[:, 2 * DH :] + v[:, off_v : off_v + DH]
        ).astype(bf16)

    def store(half, p, h, pair, top, total):
        if h:
            at = half * DH + p * 128
            ctx[:, at : at + 128] = jnp.concatenate(pair, 0).T.astype(ctx.dtype)
        if student:
            lse[half, 2 * p + h : 2 * p + h + 1, :] = top + jnp.log(total)

    attend(length, lambda half: (qkv, half * QW), store)
    if student:
        clip = jnp.concatenate([v_a[:, CC : CC + DH], v_b[:, CC : CC + DH]], 1)
        cin = (clip * jnp.tanh(ctx[...] * (1.0 / clip))).astype(bf16)
        branch = dot(cin, wo[...]) + row(R_BO)
        r1 = mine + branch
        normed, _ = norm(r1)
        h1 = normed * row(R_G0) + row(R_S0)
        cm = row(R_CM)
        r1_o[...] = r1
        h1_o[...] = h1
        mid_o[...] = (cm * jnp.tanh(h1 * (1.0 / cm))).astype(bf16)
        sum_o[0:1, :] += colsum(keep_rows(length) * branch * branch)
    else:
        branch = dot(ctx[...], wo[...]) + row(R_TBO)
        normed, _ = norm(mine + branch)
        h1 = normed * row(R_TG0) + row(R_TS0)
        h1_o[...] = h1
        mid_o[...] = h1.astype(bf16)


def encode(lens, x, weights, wo_a, wo_b, v_a, v_b, rep, student):
    rows = x.shape[0]
    block = pl.BlockSpec((SEQ, D), lambda i, *_: (i, 0))
    wide = SDS((rows, D), f32)
    if student:
        out_specs = [
            pl.BlockSpec((SEQ, 2 * QW), lambda i, *_: (i, 0)),
            block,
            pl.BlockSpec((2, 8, SEQ), lambda i, *_: (i, 0, 0)),
            block,
            block,
            block,
            pl.BlockSpec((D, SEQ), lambda i, *_: (0, i)),
            pl.BlockSpec((8, D), lambda i, *_: (0, 0)),
        ]
        out_shape = [
            SDS((rows, 2 * QW), bf16), wide, SDS((rows // SEQ * 2, 8, SEQ), f32),
            wide, wide, SDS((rows, D), bf16), SDS((D, rows), bf16), SDS((8, D), f32),
        ]
        scratch = [pltpu.VMEM((D, D), bf16)]
    else:
        out_specs = [block, block]
        out_shape = [wide, SDS((rows, D), bf16)]
        scratch = [
            pltpu.VMEM((D, D), bf16),
            pltpu.VMEM((SEQ, 2 * QW), bf16),
            pltpu.VMEM((SEQ, D), bf16),
            pltpu.VMEM((D, 2 * QW), bf16),
        ]
    return pl.pallas_call(
        partial(encode_kernel, student=student),
        grid_spec=pltpu.PrefetchScalarGridSpec(
            num_scalar_prefetch=2,
            grid=(rows // SEQ,),
            in_specs=[block]
            + [whole(w.shape) for w in weights]
            + [whole((DH, D)), whole((DH, D))]
            + [whole((1, VEND)), whole((1, VEND)), whole((14, D))],
            out_specs=out_specs,
            scratch_shapes=scratch,
        ),
        out_shape=out_shape,
        compiler_params=params(),
        name="encode",
        cost_estimate=cost(25),
    )(*lens, x, *weights, wo_a, wo_b, v_a, v_b, rep)


ROWS = 256


def ff_kernel(
    lens, first, h1, mid, th1, tmid, cot, wi_a, wi_b, wu_a, wu_b, ti_a, ti_b, tu_a, tu_b,
    bi_a, bi_b, ch_a, ch_b, tb_a, tb_b, rep,
    ain_o, mul_o, cv_o, lo_o, dr2_o, dfr_o, sum_o, acc_s, acc_t,
):
    c = pl.program_id(0)
    rows = h1.shape[0]

    @pl.when(c == 0)
    def _():
        acc_s[...] = jnp.zeros_like(acc_s)
        acc_t[...] = jnp.zeros_like(acc_t)

    def chunk(wi, wu, ti, tu, bi, ch, tb):
        inv_clip = 1.0 / ch[...]

        def block(i, carry):
            r = pl.ds(pl.multiple_of(i * ROWS, ROWS), ROWS)
            inner = dot(mid[r, :], wi[...]) + bi[...]
            t_inner = dot(tmid[r, :], ti[...]) + tb[...]
            cdf = 0.5 * (1.0 + lax.erf(inner * (2.0**-0.5)))
            act = inner * cdf
            deriv = cdf + inner * (jnp.exp(-0.5 * inner * inner) * (1.0 / math.sqrt(2.0 * math.pi)))
            ratio = act * inv_clip
            th = jnp.tanh(ratio)
            slope = 1.0 - th * th
            ain = (ch[...] * th).astype(bf16)
            ain_o[r, :] = ain
            mul_o[r, :] = (slope * deriv).astype(bf16)
            cv_o[r, :] = (th - ratio * slope).astype(bf16)
            acc_s[r, :] += dot(ain, wu[...])
            t_act = (t_inner * (0.5 * (1.0 + lax.erf(t_inner * (2.0**-0.5))))).astype(bf16)
            acc_t[r, :] += dot(t_act, tu[...])
            return carry

        lax.fori_loop(0, rows // ROWS, block, 0)

    @pl.when(c < NCH)
    def _():
        chunk(wi_a, wu_a, ti_a, tu_a, bi_a, ch_a, tb_a)

    @pl.when(c >= NCH)
    def _():
        chunk(wi_b, wu_b, ti_b, tu_b, bi_b, ch_b, tb_b)

    @pl.when(c == 2 * NCH - 1)
    def _():
        row = lambda n: rep[n : n + 1, :]
        total = [jnp.zeros((1, D), f32)] * 6
        for s in range(rows // SEQ):
            r = slice(s * SEQ, (s + 1) * SEQ)
            keep = keep_rows(lens[first[0] + s])
            branch = acc_s[r, :] + row(R_BU)
            r2 = h1[r, :] + branch
            normed, inv = norm(r2)
            out = normed * row(R_G1) + row(R_S1)
            t_normed, _ = norm(th1[r, :] + acc_t[r, :] + row(R_TBU))
            diff = keep * (out - (t_normed * row(R_TG1) + row(R_TS1)))
            d_out = cot[r, :].astype(f32) + diff
            dr2 = norm_back(d_out * row(R_G1), normed, inv)
            lo_o[r, :] = out.astype(bf16)
            dr2_o[r, :] = dr2
            dfr_o[r, :] = dr2.astype(bf16)
            parts = (
                d_out * normed, d_out, dr2, diff * diff, keep * r2 * r2, keep * branch * branch,
            )
            total = [t + colsum(p) for t, p in zip(total, parts)]
        for n in range(6):
            sum_o[n : n + 1, :] = total[n]
        sum_o[6:8, :] = jnp.zeros((2, D), f32)


def half_col(half, width, base=0):
    lo = half * NCH
    return pl.BlockSpec((width, CH_W), lambda c, *_: (0, base + jnp.clip(c - lo, 0, NCH - 1)))


def half_row(half):
    lo = half * NCH
    return pl.BlockSpec((CH_W, D), lambda c, *_: (jnp.clip(c - lo, 0, NCH - 1), 0))


def feed_forward(lens, h1, mid, th1, tmid, cot, wi, wu, ti, tu, v_a, v_b, rep):
    rows = h1.shape[0]
    full = whole((rows, D))
    chunk_out = pl.BlockSpec((rows, CH_W), lambda c, *_: (0, c))
    return pl.pallas_call(
        ff_kernel,
        grid_spec=pltpu.PrefetchScalarGridSpec(
            num_scalar_prefetch=2,
            grid=(2 * NCH,),
            in_specs=[
                full, full, full, full, full,
                half_col(0, D), half_col(1, D), half_row(0), half_row(1),
                half_col(0, D), half_col(1, D), half_row(0), half_row(1),
                half_col(0, 1, BI // CH_W), half_col(1, 1, BI // CH_W),
                half_col(0, 1, CHD // CH_W), half_col(1, 1, CHD // CH_W),
                half_col(0, 1, TI // CH_W), half_col(1, 1, TI // CH_W),
                whole((14, D)),
            ],
            out_specs=[chunk_out, chunk_out, chunk_out, full, full, full, whole((8, D))],
            scratch_shapes=[
                pltpu.VMEM((rows, D), f32),
                pltpu.VMEM((rows, D), f32),
            ],
        ),
        out_shape=[
            SDS((rows, FF), bf16),
            SDS((rows, FF), bf16),
            SDS((rows, FF), bf16),
            SDS((rows, D), bf16),
            SDS((rows, D), f32),
            SDS((rows, D), bf16),
            SDS((8, D), f32),
        ],
        compiler_params=params(),
        name="feed_forward",
        cost_estimate=cost(45),
    )(
        *lens, h1, mid, th1, tmid, cot, wi[0], wi[1], wu[0], wu[1], ti[0], ti[1], tu[0], tu[1],
        v_a, v_b, v_a, v_b, v_a, v_b, rep,
    )


def outer_grad_kernel(dfr, ain, gu_o):
    gu_o[...] = dot(ain[...], dfr[...], TN).astype(bf16)


def outer_grad(half, dfr, ain):
    rows = dfr.shape[0]
    return pl.pallas_call(
        outer_grad_kernel,
        grid=(NCH,),
        in_specs=[whole((rows, D)), pl.BlockSpec((rows, CH_W), lambda c: (0, half * NCH + c))],
        out_specs=pl.BlockSpec((CH_W, D), lambda c: (c, 0)),
        out_shape=SDS((FH, D), bf16),
        compiler_params=params(),
        name="outer_grad",
        cost_estimate=cost(6),
    )(dfr, ain)


def ff_back_kernel(*refs, first):
    if first:
        dfr, mid, mul, cv, wi, wu, gi_o, sum_o, dh_o, mid_t = refs
    else:
        dfr, mid, mul, cv, wi, wu, before, gi_o, sum_o, dh_o, mid_t = refs
    c = pl.program_id(0)

    @pl.when(c == 0)
    def _():
        mid_t[...] = mid[...].T
        dh_o[...] = jnp.zeros_like(dh_o) if first else before[...]

    d_ain = dot(dfr[...], wu[...], NT)
    sum_o[1:2, :] = colsum(d_ain * cv[...].astype(f32))
    d_inner = d_ain * mul[...].astype(f32)
    sum_o[0:1, :] = colsum(d_inner)
    sum_o[2:8, :] = jnp.zeros((6, CH_W), f32)
    dir_low = d_inner.astype(bf16)
    gi_o[...] = dot(mid_t[...], dir_low).astype(bf16)
    dh_o[...] += dot(dir_low, wi[...], NT)


def ff_back(half, dfr, mid, mul, cv, wi, wu, before):
    rows = dfr.shape[0]
    full = whole((rows, D))
    chunk = pl.BlockSpec((rows, CH_W), lambda c: (0, half * NCH + c))
    col = pl.BlockSpec((D, CH_W), lambda c: (0, c))
    row = pl.BlockSpec((CH_W, D), lambda c: (c, 0))
    extra = [] if before is None else [before]
    return pl.pallas_call(
        partial(ff_back_kernel, first=before is None),
        grid=(NCH,),
        in_specs=[full, full, chunk, chunk, col, row] + [full] * len(extra),
        out_specs=[col, pl.BlockSpec((8, CH_W), lambda c: (0, c)), full],
        out_shape=[SDS((D, FH), bf16), SDS((8, FH), f32), SDS((rows, D), f32)],
        scratch_shapes=[pltpu.VMEM((D, rows), bf16)],
        compiler_params=params(),
        name="ff_back",
        cost_estimate=cost(14),
    )(dfr, mid, mul, cv, wi, wu, *extra)


def mid_back_kernel(
    r1, dr2, dhin, ctx, wo_a, wo_b, v_a, v_b, rep, dr1_o, dcr_o, go_a, go_b, sum_o, wo, acc
):
    i = pl.program_id(0)

    @pl.when(i == 0)
    def _():
        wo[:DH, :] = wo_a[...]
        wo[DH:, :] = wo_b[...]
        acc[...] = jnp.zeros_like(acc)
        sum_o[...] = jnp.zeros_like(sum_o)

    row = lambda n: rep[n : n + 1, :]
    normed, inv = norm(r1[...])
    cm = row(R_CM)
    ratio = (normed * row(R_G0) + row(R_S0)) * (1.0 / cm)
    th = jnp.tanh(ratio)
    slope = 1.0 - th * th
    d_hin = dhin[...]
    sum_o[3:4, :] += colsum(d_hin * (th - ratio * slope))
    dh1 = dr2[...] + d_hin * slope
    sum_o[0:1, :] += colsum(dh1 * normed)
    sum_o[1:2, :] += colsum(dh1)
    dr1 = norm_back(dh1 * row(R_G0), normed, inv)
    sum_o[2:3, :] += colsum(dr1)
    dr1_o[...] = dr1
    dar = dr1.astype(bf16)
    clip = jnp.concatenate([v_a[:, CC : CC + DH], v_b[:, CC : CC + DH]], 1)
    ratio = ctx[...] * (1.0 / clip)
    th = jnp.tanh(ratio)
    slope = 1.0 - th * th
    acc[...] += dot(dar, (clip * th).astype(bf16), TN)
    d_cin = dot(dar, wo[...], NT)
    sum_o[4:5, :] += colsum(d_cin * (th - ratio * slope))
    dcr_o[...] = (d_cin * slope).astype(bf16)

    @pl.when(i == pl.num_programs(0) - 1)
    def _():
        go_a[...] = acc[:, :DH].astype(bf16)
        go_b[...] = acc[:, DH:].astype(bf16)


def mid_back(r1, dr2, dhin, ctx, wo_a, wo_b, v_a, v_b, rep):
    rows = r1.shape[0]
    block = pl.BlockSpec((RB, D), lambda i: (i, 0))
    return pl.pallas_call(
        mid_back_kernel,
        grid=(rows // RB,),
        in_specs=[block] * 4
        + [whole((DH, D)), whole((DH, D)), whole((1, VEND)), whole((1, VEND)), whole((14, D))],
        out_specs=[block, block, whole((D, DH)), whole((D, DH)), whole((8, D))],
        out_shape=[
            SDS((rows, D), f32),
            SDS((rows, D), bf16),
            SDS((D, DH), bf16),
            SDS((D, DH), bf16),
            SDS((8, D), f32),
        ],
        scratch_shapes=[pltpu.VMEM((D, D), bf16), pltpu.VMEM((D, D), f32)],
        compiler_params=params(),
        name="mid_back",
        cost_estimate=cost(12),
    )(r1, dr2, dhin, ctx, wo_a, wo_b, v_a, v_b, rep)


def attn_back_kernel(lens, first, qkv, dc, ctx, lse, xt, got, d_o, grad, sum_o, acc):
    seq = pl.program_id(0)
    length = lens[first[0] + seq]
    pick = lax.broadcasted_iota(jnp.int32, (8, DH), 1) // HD
    pick = (pick == lax.broadcasted_iota(jnp.int32, (8, DH), 0)).astype(f32)
    deltas = lax.dot_general(
        pick, dc[...].astype(f32) * ctx[...], NT, precision=lax.Precision.HIGHEST,
        preferred_element_type=f32,
    )
    heads = [(p, h) for p in range(3) for h in range(2)]
    part_of = lambda n, p: qkv[:, n * DH + p * 128 : n * DH + (p + 1) * 128]
    dc_of = lambda p: dc[:, p * 128 : (p + 1) * 128]

    def score(p, h):
        q_h, k_h = with_mask(part_of(0, p), part_of(1, p), length, h)
        return dot(k_h, q_h, NT), dot(pair_of(part_of(2, p), h), dc_of(p), NT)

    @pl.when(seq == 0)
    def _():
        sum_o[...] = jnp.zeros_like(sum_o)

    scores = [score(*heads[0])]
    for i, (p, h) in enumerate(heads):
        if i + 1 < len(heads):
            scores.append(score(*heads[i + 1]))
        s, dp = scores[i]
        n = 2 * p + h
        prob = jnp.exp(s - lse[0, n : n + 1, :])
        ds = (prob * (dp - deltas[n : n + 1, :])).astype(bf16)
        if h == 0:
            k_t = part_of(1, p).T
        part_q = dot(k_t[h * HD : (h + 1) * HD], ds)
        part_k, part_v = dot(ds, pair_of(part_of(0, p), h)), dot(prob.astype(bf16), pair_of(dc_of(p), h))
        if h == 0:
            d_q, d_k, d_v = part_q, part_k, part_v
        else:
            d_q = jnp.concatenate([d_q, part_q], 0).T * HD**-0.5
            d_v = d_v + part_v
            at = slice(p * 128, (p + 1) * 128)
            for k, d in enumerate((d_q, d_k + part_k, d_v)):
                d_o[:, k * DH + p * 128 : k * DH + (p + 1) * 128] = d.astype(bf16)
            sum_o[0:1, at] += colsum(d_q)
            sum_o[1:2, at] += colsum(d_v)
    part = dot(xt[...], d_o[...])

    @pl.when(seq == 0)
    def _():
        acc[...] = part

    @pl.when(seq > 0)
    def _():
        acc[...] += part

    @pl.when(seq == pl.num_programs(0) - 1)
    def _():
        grad[:, :QW] = acc[...].astype(bf16)
        grad[:, QW:] = got[...]


def attention_back(half, lens, qkv, dcr, ctx, lse, x_t, got):
    rows = qkv.shape[0]
    nseq = rows // SEQ
    given = pl.BlockSpec((SEQ, DH), lambda s, *_: (s, half))
    return pl.pallas_call(
        attn_back_kernel,
        grid_spec=pltpu.PrefetchScalarGridSpec(
            num_scalar_prefetch=2,
            grid=(nseq,),
            in_specs=[
                pl.BlockSpec((SEQ, QW), lambda s, *_: (s, half)),
                given,
                given,
                pl.BlockSpec((1, 8, SEQ), lambda s, *_: (2 * s + half, 0, 0)),
                pl.BlockSpec((D, SEQ), lambda s, *_: (0, s)),
                whole((D, DH)),
            ],
            out_specs=[
                pl.BlockSpec((SEQ, QW), lambda s, *_: (s, 0)),
                whole((D, FH)),
                whole((8, DH)),
            ],
            scratch_shapes=[pltpu.VMEM((D, QW), f32)],
        ),
        out_shape=[SDS((rows, QW), bf16), SDS((D, FH), bf16), SDS((8, DH), f32)],
        compiler_params=params(),
        name="attention_back",
        cost_estimate=cost(14),
    )(*lens, qkv, dcr, ctx, lse, x_t, got)


def clip_in(x, rep):
    clip = rep[R_CI : R_CI + 1, :]
    ratio = x[...].astype(f32) * (1.0 / clip)
    return ratio, jnp.tanh(ratio)


def x_back_kernel(x, d_a, d_b, dr1, w_a, w_b, rep, grad_o, sum_o):
    total = dot(d_a[...], w_a[...], NT) + dot(d_b[...], w_b[...], NT)
    ratio, th = clip_in(x, rep)
    slope = 1.0 - th * th
    grad_o[...] = dr1[...] + total * slope

    @pl.when(pl.program_id(0) == 0)
    def _():
        sum_o[...] = jnp.zeros_like(sum_o)

    sum_o[0:1, :] += colsum(total * (th - ratio * slope))


RB = 256


def x_back(x, d_a, d_b, dr1, w_a, w_b, rep):
    rows = x.shape[0]
    block = pl.BlockSpec((RB, D), lambda i: (i, 0))
    wide = pl.BlockSpec((RB, QW), lambda i: (i, 0))
    return pl.pallas_call(
        x_back_kernel,
        grid=(rows // RB,),
        in_specs=[block, wide, wide, block, whole((D, QW)), whole((D, QW)), whole((14, D))],
        out_specs=[block, whole((8, D))],
        out_shape=[SDS((rows, D), f32), SDS((8, D), f32)],
        compiler_params=params(),
        name="x_back",
        cost_estimate=cost(8),
    )(x, d_a, d_b, dr1, w_a, w_b, rep)


def pack_kernel(ha, hb, qa, qb, m, f, a, x, out):
    for side, (h, q) in enumerate(((ha, qa), (hb, qb))):
        base = 6 * side
        for n in range(2):
            out[base + 2 * n : base + 2 * n + 1, :] = h[n : n + 1, :D]
            out[base + 2 * n + 1 : base + 2 * n + 2, :] = h[n : n + 1, D:]
        out[base + 4 : base + 5, :DH] = q[0:1, :]
        out[base + 4 : base + 5, DH:] = q[1:2, :]
        out[base + 5 : base + 6, :DH] = m[4:5, side * DH : (side + 1) * DH]
        out[base + 5 : base + 6, DH:] = jnp.zeros((1, DH), f32)
    rows = (
        (m, 2), (f, 2), (m, 0), (f, 0), (m, 1), (f, 1), (x, 0), (m, 3),
        (f, 3), (f, 4), (a, 0), (f, 5),
    )
    for n, (ref, k) in enumerate(rows):
        out[12 + n : 13 + n, :] = ref[k : k + 1, :]


def pack(*sums):
    return pl.pallas_call(
        pack_kernel,
        grid=(1,),
        in_specs=[whole(v.shape) for v in sums],
        out_specs=whole((24, D)),
        out_shape=SDS((24, D), f32),
        compiler_params=params(),
        name="pack",
        cost_estimate=cost(1),
    )(*sums)


BLOCKS = 16
OUTER, INNER, ATTN = range(3)
ORDERS = (
    ((1, 2, 4, 8), (2, 4, 1, 8)),
    ((4, 1, 2, 8), (1, 4, 2, 8)),
    ((1, 2, 4, 8), (2, 4, 1, 8)),
)


def spread(order, r):
    return sum(mask for p, mask in enumerate(order) if r & (BLOCKS >> (p + 1)))


def place_table(me, core):
    rows = []
    for pair in ORDERS:
        a, b = [jnp.asarray([spread(o, r) for r in range(BLOCKS)], jnp.int32) for o in pair]
        rows.append(jnp.where(core == 0, a, b) ^ me)
    return jnp.concatenate(rows)


def fold_kernel(place, own, got, high, low, *, kind):
    for r in range(BLOCKS):
        src = place[kind * BLOCKS + r]
        value = (own[src].astype(f32) + got[src].astype(f32)).astype(bf16)
        if r >= BLOCKS // 2:
            high[r - BLOCKS // 2] = value
        else:
            low[r] = value


def fold(place, own, got, kind):
    shape = (BLOCKS, own.shape[0] // BLOCKS, own.shape[1])
    piece = (BLOCKS // 2,) + shape[1:]
    return pl.pallas_call(
        partial(fold_kernel, kind=kind),
        grid_spec=pltpu.PrefetchScalarGridSpec(
            num_scalar_prefetch=1,
            grid=(1,),
            in_specs=[whole(shape)] * 2,
            out_specs=[whole(piece)] * 2,
        ),
        out_shape=[SDS(piece, bf16)] * 2,
        compiler_params=params(),
        name="fold",
        cost_estimate=cost(5),
    )(place, own.reshape(shape), got.reshape(shape))


def swap(value, masks, n_dp):
    pairs = [(2 * i + t, 2 * (i ^ masks[t]) + t) for i in range(n_dp) for t in range(2)]
    return lax.ppermute(value, ("dp", "tensor"), pairs)


class Sum:
    def __init__(self, pieces, kind, n_dp):
        self.kind, self.n_dp = kind, n_dp
        self.send, self.hold = pieces
        self.step = 0
        self.recv = self.swap(0)

    def swap(self, step):
        return swap(self.send, tuple(order[step] for order in ORDERS[self.kind]), self.n_dp)

    def advance(self, *done):
        self.recv, *done = lax.optimization_barrier((self.recv, *done))
        self.step += 1
        half = self.hold.shape[0] // 2
        if self.step <= 3:
            self.send = self.hold[half:] + self.recv[half:]
            self.hold = self.hold[:half] + self.recv[:half]
            self.recv = self.swap(self.step)
        elif self.step == 4:
            self.send = self.hold + self.recv
            mask = BLOCKS
            while mask < self.n_dp:
                self.send = self.send + swap(self.send, (mask, mask), self.n_dp)
                mask *= 2
            self.recv = self.swap(3)
        elif self.step <= 7:
            self.send = jnp.concatenate([self.send, self.recv], 0)
            self.recv = self.swap(7 - self.step)
        return done

    def result(self, *done):
        self.recv, *done = lax.optimization_barrier((self.recv, *done))
        return (self.send, self.recv)


def sum_all(value, n_dp):
    mask = 1
    while mask < n_dp:
        value = value + swap(value, (mask, mask), n_dp)
        mask *= 2
    return value


def behind(streams, *values):
    sent = [s.send for s in streams]
    return lax.optimization_barrier((*sent, *values))[len(sent) :]


def latent(w, g, axis, factor):
    th = jnp.tanh(2.0 * w)
    n = w.shape[axis]
    mean = jnp.sum(jnp.abs(w), axis, keepdims=True) * (1.0 / n)
    inner = jnp.sum(g * th, axis, keepdims=True) * (1.0 / n)
    sign = jnp.where(w > 0, 1.0, jnp.where(w < 0, -1.0, 0.0))
    return factor * (2.0 * mean * (1.0 - th * th) * g + sign * inner)


def collect(place, mine, recv, kind, target):
    n = mine.shape[1]
    for r in range(BLOCKS):
        at = pl.multiple_of(place[kind * BLOCKS + r] * n, 16)
        target[pl.ds(at, n), :] = (mine if r < BLOCKS // 2 else recv)[r % 8]


def latent_kernel(place, mine, recv, w, out, g, *, kind):
    i = pl.program_id(0)

    @pl.when(i == 0)
    def _():
        collect(place, mine, recv, kind, g)

    n = FH // 4
    at = pl.ds(pl.multiple_of(i * n, 128), n)
    if kind == OUTER:
        out[...] = latent(w[...], g[at, :].astype(f32), 1, 1.0 / math.sqrt(FF))
    else:
        out[...] = latent(w[...], g[:, at].astype(f32), 0, 1.0 / math.sqrt(D))


def ffn_latent(kind, place, pieces, w):
    if kind == OUTER:
        block = pl.BlockSpec((FH // 4, D), lambda i, *_: (i, 0))
    else:
        block = pl.BlockSpec((D, FH // 4), lambda i, *_: (0, i))
    return pl.pallas_call(
        partial(latent_kernel, kind=kind),
        grid_spec=pltpu.PrefetchScalarGridSpec(
            num_scalar_prefetch=1,
            grid=(4,),
            in_specs=[whole(p.shape) for p in pieces] + [block],
            out_specs=block,
            scratch_shapes=[pltpu.VMEM(w.shape, bf16)],
        ),
        out_shape=SDS(w.shape, f32),
        compiler_params=params(),
        name="ffn_latent",
        cost_estimate=cost(8),
    )(place, *pieces, w)


def attn_latent_kernel(place, mine, recv, *refs):
    w_in, wo, outs, go, g = refs[:3], refs[3], refs[4:7], refs[7], refs[8]
    root = 1.0 / math.sqrt(D)
    collect(place, mine, recv, ATTN, g)
    for c in range(3):
        grad = g[:, c * DH : (c + 1) * DH].astype(f32)
        outs[c][...] = latent(w_in[c][...], grad, 0, root if c == 2 else 2.0 * root)
    go[...] = latent(wo[...], g[:, QW:].astype(f32).T, 1, 8.0 * root)


def attn_latent(place, pieces, wq, wk, wv, wo):
    col, row = whole((D, DH)), whole((DH, D))
    return pl.pallas_call(
        attn_latent_kernel,
        grid_spec=pltpu.PrefetchScalarGridSpec(
            num_scalar_prefetch=1,
            grid=(1,),
            in_specs=[whole(p.shape) for p in pieces] + [col, col, col, row],
            out_specs=[col, col, col, row],
            scratch_shapes=[pltpu.VMEM((D, FH), bf16)],
        ),
        out_shape=[SDS((D, DH), f32)] * 3 + [SDS((DH, D), f32)],
        compiler_params=params(),
        name="attn_latent",
        cost_estimate=cost(9),
    )(place, *pieces, wq, wk, wv, wo)


def on_device(
    n_dp,
    tokens, cotangent, lengths, w_query, w_key, w_value, w_output, w_inner, w_outer,
    b_query, b_value, b_output, b_inner, b_outer, ln_gains, ln_shifts,
    clip_input, clip_context, clip_middle, clip_hidden,
    t_query, t_key, t_value, t_output, t_inner, t_outer,
    tb_query, tb_value, tb_output, tb_inner, tb_outer, t_gains, t_shifts,
):
    other = lambda value: lax.ppermute(value, "tensor", [(0, 1), (1, 0)])
    rows = tokens.shape[0]
    nseq = rows // SEQ
    core = lax.axis_index("tensor")
    place = place_table(lax.axis_index("dp").astype(jnp.int32), core)
    lens = (lengths, (core * nseq).astype(jnp.int32).reshape(1))

    t_own = (t_query, t_key, t_value)
    t_other = tuple(other(w) for w in t_own)
    t_out_b = other(t_output)
    wqkv, wo, wi, wu, v_a, rep = prep(
        (w_query, w_key, w_value, w_output, w_inner, w_outer),
        (b_inner, clip_hidden, tb_inner, b_query, b_value, clip_context, tb_query, tb_value),
        (
            b_output, b_outer, ln_gains, ln_shifts, clip_input, clip_middle,
            tb_output, tb_outer, t_gains, t_shifts,
        ),
    )
    v_b = other(v_a)
    wqkv_b, wo_b = other(wqkv), other(wo)
    th1, tmid = encode(lens, tokens, t_own + t_other, t_output, t_out_b, v_a, v_b, rep, False)
    late = lax.optimization_barrier((v_b, t_inner, t_outer, wi, wu))[1:]
    ti_b, tu_b, wi_b, wu_b = [other(w) for w in late]
    qkv, ctx, lse, r1, h1, mid, x_t, sum_a = encode(
        lens, tokens, (wqkv, wqkv_b), wo, wo_b, v_a, v_b, rep, True
    )
    ain, mul, cv, layer_out, dr2, dfr, sum_f = feed_forward(
        lens, h1, mid, th1, tmid, cotangent, (wi, wi_b), (wu, wu_b), (t_inner, ti_b),
        (t_outer, tu_b), v_a, v_b, rep,
    )
    gu_b = outer_grad(1, dfr, ain)
    dfr, gu_b = lax.optimization_barrier((dfr, gu_b))
    gu_a = outer_grad(0, dfr, ain)
    outer = Sum(fold(place, gu_a, other(gu_b), OUTER), OUTER, n_dp)

    (dfr,) = behind([outer], dfr)
    gi_b, sum_hb, dh_b = ff_back(1, dfr, mid, mul, cv, wi_b, wu_b, None)
    (dh_b,) = outer.advance(dh_b)
    (dh_b,) = behind([outer], dh_b)
    gi_a, sum_ha, dhin = ff_back(0, dfr, mid, mul, cv, wi, wu, dh_b)
    (gi_a,) = outer.advance(gi_a)
    inner = Sum(fold(place, gi_a, other(gi_b), INNER), INNER, n_dp)

    (dhin,) = behind([outer, inner], dhin)
    dr1, dcr, go_a, go_b, sum_m = mid_back(r1, dr2, dhin, ctx, wo, wo_b, v_a, v_b, rep)
    (dcr,) = outer.advance(dcr)
    (dcr,) = inner.advance(dcr)
    (dcr,) = behind([outer, inner], dcr)
    d_b, gs_b, sum_qb = attention_back(1, lens, qkv, dcr, ctx, lse, x_t, go_b)
    (gs_b,) = outer.advance(gs_b)
    (gs_b,) = inner.advance(gs_b)
    gs_b, dcr = behind([outer, inner], gs_b, dcr)
    d_a, gs_a, sum_qa = attention_back(0, lens, qkv, dcr, ctx, lse, x_t, go_a)
    (gs_a,) = outer.advance(gs_a)
    (gs_a,) = inner.advance(gs_a)
    attn = Sum(fold(place, gs_a, other(gs_b), ATTN), ATTN, n_dp)
    streams = [outer, inner, attn]
    dr1, _ = outer.advance(dr1, gs_a)
    dr1, _ = inner.advance(dr1, gs_a)
    (dr1,) = behind(streams, dr1)
    grad_tokens, sum_x = x_back(tokens, d_a, d_b, dr1, wqkv, wqkv_b, rep)
    sums = pack(sum_ha, sum_hb, sum_qa, sum_qb, sum_m, sum_f, sum_a, sum_x)
    (sums,) = attn.advance(sums)
    (sums,) = outer.advance(sums)
    (sums,) = inner.advance(sums)
    (sums,) = behind(streams, sums)
    small = jnp.concatenate([sums[:6], sums[12:]], 0) + other(sums[6:])
    (small,) = attn.advance(small)
    (small,) = inner.advance(small)
    small = sum_all(small, n_dp)
    (w_o,) = behind([attn, inner], w_outer)
    g_outer = ffn_latent(OUTER, place, outer.result(), w_o)
    (g_outer,) = attn.advance(g_outer)
    (w_i,) = behind([attn], w_inner)
    (g_outer,) = inner.advance(g_outer)
    g_inner = ffn_latent(INNER, place, inner.result(), w_i)
    for _ in range(4):
        attn.advance()
    g_query, g_key, g_value, g_output = attn_latent(
        place, attn.result(), w_query, w_key, w_value, w_output
    )
    split, shared = small[:6], small[6:]
    count = jnp.asarray(rows * 2 * n_dp * D, f32)
    stats = jnp.sum(shared[8:], 1) / count
    summary = jnp.concatenate([stats[:1], jnp.sqrt(stats[1:])])
    return (
        layer_out,
        grad_tokens,
        g_query,
        g_key,
        g_value,
        g_output,
        g_inner,
        g_outer,
        split[4, :DH],
        split[4, DH:],
        shared[0],
        split[0:2].reshape(FH),
        shared[1],
        shared[2:4],
        shared[4:6],
        shared[6],
        split[5, :DH],
        shared[7],
        split[2:4].reshape(FH),
        summary,
    )


def solution(mesh):
    rows, cols, split, full = P(("dp", "tensor"), None), P(None, "tensor"), P("tensor"), P()
    down = P("tensor", None)
    return jax.shard_map(
        partial(on_device, mesh.shape["dp"]),
        mesh=mesh,
        in_specs=(
            rows, rows, P("dp"), cols, cols, cols, down, cols, down,
            split, split, full, split, full, full, full,
            full, split, full, split,
            cols, cols, cols, down, cols, down,
            split, split, full, split, full, full, full,
        ),
        out_specs=(
            rows, rows, cols, cols, cols, down, cols, down,
            split, split, full, split, full, full, full, full, split, full, split, full,
        ),
        check_vma=False,
    )
```

```python
from functools import partial
import math

import jax
import jax.numpy as jnp
from jax import lax
import jax.experimental.pallas as pl
import jax.experimental.pallas.tpu as pltpu
from jax.sharding import PartitionSpec as P

D = 768
FF = 3072
SEQ = 512
HD = 64
DH = D // 2
FH = FF // 2
QW = 3 * DH

CH_W = 512
NCH = FH // CH_W
EPS = 1e-12

BI, CHD, TI, BQ, BV, CC, TQ, TV, VEND = 0, 1536, 3072, 4608, 4992, 5376, 5760, 6144, 6528
R_BO, R_BU, R_G0, R_G1, R_S0, R_S1, R_CI, R_CM, R_TBO, R_TBU, R_TG0, R_TG1, R_TS0, R_TS1 = range(14)

f32 = jnp.float32
bf16 = jnp.bfloat16
NT = (((1,), (1,)), ((), ()))
NN = (((1,), (0,)), ((), ()))
TN = (((0,), (0,)), ((), ()))
SDS = jax.ShapeDtypeStruct


def dot(left, right, dims=NN):
    return lax.dot_general(left, right, dims, preferred_element_type=f32)


def params(mib):
    return pltpu.CompilerParams(vmem_limit_bytes=mib * 2**20)


def cost(micros):
    return pl.CostEstimate(
        flops=micros * 10**9, transcendentals=0, bytes_accessed=micros * 3 * 10**6
    )


def whole(shape):
    rank = len(shape)
    return pl.BlockSpec(shape, lambda *_: (0,) * rank, pipeline_mode=pl.Buffered(1))


def norm(resid):
    centered = resid - jnp.mean(resid, -1, keepdims=True)
    inv = lax.rsqrt(jnp.mean(centered * centered, -1, keepdims=True) + EPS)
    return centered * inv, inv


def colsum(value):
    return jnp.sum(value, 0, keepdims=True)


def norm_back(e, normed, inv):
    return inv * (
        e - jnp.mean(e, -1, keepdims=True) - normed * jnp.mean(e * normed, -1, keepdims=True)
    )


def keep_rows(length):
    return (lax.broadcasted_iota(jnp.int32, (SEQ, 1), 0) < length).astype(f32)


def bin_cols(w, factor):
    return (jnp.mean(jnp.abs(w), 0, keepdims=True) * jnp.tanh(2.0 * w) * factor).astype(bf16)


def bin_rows(w, factor):
    return (jnp.mean(jnp.abs(w), 1, keepdims=True) * jnp.tanh(2.0 * w) * factor).astype(bf16)


SPLIT = (FH, FH, FH, DH, DH, DH, DH, DH)


def prep_kernel(*refs):
    wq, wk, wv, wo, wi, wu = refs[:6]
    split = refs[6:14]
    full = refs[14:24]
    qkv_o, wo_o, wi_o, wu_o, vec_o, rep_o = refs[24:]
    i = pl.program_id(0)
    root = 1.0 / math.sqrt(D)
    wi_o[...] = bin_cols(wi[...], root)
    wu_o[...] = bin_rows(wu[...], 1.0 / math.sqrt(FF))

    @pl.when(i == 0)
    def _():
        qkv_o[:, :DH] = bin_cols(wq[...], 2.0 * root)
        at = 0
        for ref, n in zip(split, SPLIT):
            vec_o[0, at : at + n] = ref[...]
            at += n
        at = 0
        for ref in full:
            if len(ref.shape) == 1:
                rep_o[at, :] = ref[...]
                at += 1
            else:
                rep_o[at : at + 2, :] = ref[...]
                at += 2

    @pl.when(i == 1)
    def _():
        qkv_o[:, DH : 2 * DH] = bin_cols(wk[...], 2.0 * root)

    @pl.when(i == 2)
    def _():
        qkv_o[:, 2 * DH :] = bin_cols(wv[...], root)

    @pl.when(i == 3)
    def _():
        wo_o[...] = bin_rows(wo[...], 8.0 * root)


def prep(weights, split, full):
    n = 4
    col = pl.BlockSpec((D, FH // n), lambda i: (0, i))
    row = pl.BlockSpec((FH // n, D), lambda i: (i, 0))
    return pl.pallas_call(
        prep_kernel,
        grid=(n,),
        in_specs=[whole((D, DH))] * 3
        + [whole((DH, D)), col, row]
        + [whole(v.shape) for v in (*split, *full)],
        out_specs=[
            whole((D, QW)), whole((DH, D)), col, row, whole((1, VEND)), whole((14, D)),
        ],
        out_shape=[
            SDS((D, QW), bf16),
            SDS((DH, D), bf16),
            SDS((D, FH), bf16),
            SDS((FH, D), bf16),
            SDS((1, VEND), f32),
            SDS((14, D), f32),
        ],
        compiler_params=params(60),
        name="prep",
        cost_estimate=cost(8),
    )(*weights, *split, *full)


def head_lanes(h):
    return lax.broadcasted_iota(jnp.int32, (1, 128), 1) // HD == h


def pair_of(value, h):
    return jnp.where(head_lanes(h), value, jnp.zeros((), value.dtype))


def with_mask(qq, kk, length, h):
    lane = lax.broadcasted_iota(jnp.int32, (1, 128), 1)
    spare = lane == HD * (1 - h)
    valid = lax.broadcasted_iota(jnp.int32, (SEQ, 1), 0) < length
    bias = jnp.where(valid, 0.0, -1e9).astype(bf16)
    k_h = jnp.where(spare, bias, pair_of(kk, h))
    return jnp.where(spare, jnp.ones((), bf16), qq), k_h


def attend(length, qkv_half, store):
    heads = [(half, p, h) for half in range(2) for p in range(3) for h in range(2)]

    def score(half, p, h):
        ref, base = qkv_half(half)
        at = base + p * 128
        q_h, k_h = with_mask(ref[:, at : at + 128], ref[:, at + DH : at + DH + 128], length, h)
        return dot(k_h, q_h, NT)

    ones = jnp.ones((16, SEQ), bf16)
    scores = [score(*heads[0]), score(*heads[1])]
    pair = []
    for i, (half, p, h) in enumerate(heads):
        if i + 2 < len(heads):
            scores.append(score(*heads[i + 2]))
        s = scores[i]
        top = jnp.max(s, 0, keepdims=True)
        e = jnp.exp(s - top).astype(bf16)
        ref, base = qkv_half(half)
        if h == 0:
            at = base + 2 * DH + p * 128
            v_t = ref[:, at : at + 128].T
        part = dot(jnp.concatenate([v_t[h * HD : (h + 1) * HD], ones], 0), e)
        total = part[HD : HD + 1]
        pair.append(part[:HD] * (1.0 / total))
        store(half, p, h, pair, top, total)
        if h:
            pair = []


def encode_kernel(lens, first, x, *refs, student):
    n = 1 if student else 3
    weights, refs = refs[: 2 * n], refs[2 * n :]
    wo_a, wo_b, v_a, v_b, rep = refs[:5]
    if student:
        qkv, ctx, lse, r1_o, h1_o, mid_o, xt_o, sum_o, wo = refs[5:]
    else:
        h1_o, mid_o, wo, qkv, ctx, w_all = refs[5:]
    i = pl.program_id(0)

    @pl.when(i == 0)
    def _():
        wo[:DH, :] = wo_a[...]
        wo[DH:, :] = wo_b[...]
        if student:
            sum_o[...] = jnp.zeros_like(sum_o)
        else:
            for k in range(6):
                w_all[:, k * DH : (k + 1) * DH] = weights[k][...]

    row = lambda k: rep[k : k + 1, :]
    length = lens[first[0] + i]
    xx = x[...]
    mine = xx.astype(f32)
    if student:
        clip = row(R_CI)
        xx = (clip * jnp.tanh(mine * (1.0 / clip))).astype(bf16)
        xt_o[...] = xx.T
    off_q, off_v = (BQ, BV) if student else (TQ, TV)
    for half, v in enumerate((v_a, v_b)):
        base = half * QW
        res = dot(xx, weights[half][...] if student else w_all[:, base : base + QW])
        q = (res[:, :DH] + v[:, off_q : off_q + DH]).astype(bf16)
        qkv[:, base : base + DH] = q * jnp.asarray(HD**-0.5, bf16)
        qkv[:, base + DH : base + 2 * DH] = res[:, DH : 2 * DH].astype(bf16)
        qkv[:, base + 2 * DH : base + QW] = (
            res[:, 2 * DH :] + v[:, off_v : off_v + DH]
        ).astype(bf16)

    def store(half, p, h, pair, top, total):
        if h:
            at = half * DH + p * 128
            ctx[:, at : at + 128] = jnp.concatenate(pair, 0).T.astype(ctx.dtype)
        if student:
            lse[half, 2 * p + h : 2 * p + h + 1, :] = top + jnp.log(total)

    attend(length, lambda half: (qkv, half * QW), store)
    if student:
        clip = jnp.concatenate([v_a[:, CC : CC + DH], v_b[:, CC : CC + DH]], 1)
        cin = (clip * jnp.tanh(ctx[...] * (1.0 / clip))).astype(bf16)
        branch = dot(cin, wo[...]) + row(R_BO)
        r1 = mine + branch
        normed, _ = norm(r1)
        h1 = normed * row(R_G0) + row(R_S0)
        cm = row(R_CM)
        r1_o[...] = r1
        h1_o[...] = h1
        mid_o[...] = (cm * jnp.tanh(h1 * (1.0 / cm))).astype(bf16)
        sum_o[0:1, :] += colsum(keep_rows(length) * branch * branch)
    else:
        branch = dot(ctx[...], wo[...]) + row(R_TBO)
        normed, _ = norm(mine + branch)
        h1 = normed * row(R_TG0) + row(R_TS0)
        h1_o[...] = h1
        mid_o[...] = h1.astype(bf16)


def encode(lens, x, weights, wo_a, wo_b, v_a, v_b, rep, student):
    rows = x.shape[0]
    block = pl.BlockSpec((SEQ, D), lambda i, *_: (i, 0))
    wide = SDS((rows, D), f32)
    if student:
        out_specs = [
            pl.BlockSpec((SEQ, 2 * QW), lambda i, *_: (i, 0)),
            block,
            pl.BlockSpec((2, 8, SEQ), lambda i, *_: (i, 0, 0)),
            block,
            block,
            block,
            pl.BlockSpec((D, SEQ), lambda i, *_: (0, i)),
            pl.BlockSpec((8, D), lambda i, *_: (0, 0)),
        ]
        out_shape = [
            SDS((rows, 2 * QW), bf16), wide, SDS((rows // SEQ * 2, 8, SEQ), f32),
            wide, wide, SDS((rows, D), bf16), SDS((D, rows), bf16), SDS((8, D), f32),
        ]
        scratch = [pltpu.VMEM((D, D), bf16)]
    else:
        out_specs = [block, block]
        out_shape = [wide, SDS((rows, D), bf16)]
        scratch = [
            pltpu.VMEM((D, D), bf16),
            pltpu.VMEM((SEQ, 2 * QW), bf16),
            pltpu.VMEM((SEQ, D), bf16),
            pltpu.VMEM((D, 2 * QW), bf16),
        ]
    return pl.pallas_call(
        partial(encode_kernel, student=student),
        grid_spec=pltpu.PrefetchScalarGridSpec(
            num_scalar_prefetch=2,
            grid=(rows // SEQ,),
            in_specs=[block]
            + [whole(w.shape) for w in weights]
            + [whole((DH, D)), whole((DH, D))]
            + [whole((1, VEND)), whole((1, VEND)), whole((14, D))],
            out_specs=out_specs,
            scratch_shapes=scratch,
        ),
        out_shape=out_shape,
        compiler_params=params(60),
        name="encode",
        cost_estimate=cost(25),
    )(*lens, x, *weights, wo_a, wo_b, v_a, v_b, rep)


ROWS = 256


def ff_kernel(
    lens, first, h1, mid, th1, tmid, cot, wi_a, wi_b, wu_a, wu_b, ti_a, ti_b, tu_a, tu_b,
    bi_a, bi_b, ch_a, ch_b, tb_a, tb_b, rep,
    ain_o, mul_o, cv_o, lo_o, dr2_o, dfr_o, sum_o, acc_s, acc_t, h1_v, th1_v, cot_v, sems,
):
    c = pl.program_id(0)
    rows = h1.shape[0]
    late = [
        pltpu.make_async_copy(src, dst, sems.at[n])
        for n, (src, dst) in enumerate(((h1, h1_v), (th1, th1_v), (cot, cot_v)))
    ]

    @pl.when(c == 0)
    def _():
        acc_s[...] = jnp.zeros_like(acc_s)
        acc_t[...] = jnp.zeros_like(acc_t)
        for copy in late:
            copy.start()

    def chunk(wi, wu, ti, tu, bi, ch, tb):
        inv_clip = 1.0 / ch[...]

        def block(i, carry):
            r = pl.ds(pl.multiple_of(i * ROWS, ROWS), ROWS)
            inner = dot(mid[r, :], wi[...]) + bi[...]
            t_inner = dot(tmid[r, :], ti[...]) + tb[...]
            cdf = 0.5 * (1.0 + lax.erf(inner * (2.0**-0.5)))
            act = inner * cdf
            deriv = cdf + inner * (jnp.exp(-0.5 * inner * inner) * (1.0 / math.sqrt(2.0 * math.pi)))
            ratio = act * inv_clip
            th = jnp.tanh(ratio)
            slope = 1.0 - th * th
            ain = (ch[...] * th).astype(bf16)
            ain_o[r, :] = ain
            mul_o[r, :] = (slope * deriv).astype(bf16)
            cv_o[r, :] = (th - ratio * slope).astype(bf16)
            acc_s[r, :] += dot(ain, wu[...])
            t_act = (t_inner * (0.5 * (1.0 + lax.erf(t_inner * (2.0**-0.5))))).astype(bf16)
            acc_t[r, :] += dot(t_act, tu[...])
            return carry

        lax.fori_loop(0, rows // ROWS, block, 0, unroll=True)

    @pl.when(c < NCH)
    def _():
        chunk(wi_a, wu_a, ti_a, tu_a, bi_a, ch_a, tb_a)

    @pl.when(c >= NCH)
    def _():
        chunk(wi_b, wu_b, ti_b, tu_b, bi_b, ch_b, tb_b)

    @pl.when(c == 2 * NCH - 1)
    def _():
        for copy in late:
            copy.wait()
        row = lambda n: rep[n : n + 1, :]
        total = [jnp.zeros((1, D), f32)] * 6
        for s in range(rows // SEQ):
            r = slice(s * SEQ, (s + 1) * SEQ)
            keep = keep_rows(lens[first[0] + s])
            branch = acc_s[r, :] + row(R_BU)
            r2 = h1_v[r, :] + branch
            normed, inv = norm(r2)
            out = normed * row(R_G1) + row(R_S1)
            t_normed, _ = norm(th1_v[r, :] + acc_t[r, :] + row(R_TBU))
            diff = keep * (out - (t_normed * row(R_TG1) + row(R_TS1)))
            d_out = cot_v[r, :].astype(f32) + diff
            dr2 = norm_back(d_out * row(R_G1), normed, inv)
            lo_o[r, :] = out.astype(bf16)
            dr2_o[r, :] = dr2
            dfr_o[r, :] = dr2.astype(bf16)
            parts = (
                d_out * normed, d_out, dr2, diff * diff, keep * r2 * r2, keep * branch * branch,
            )
            total = [t + colsum(p) for t, p in zip(total, parts)]
        for n in range(6):
            sum_o[n : n + 1, :] = total[n]
        sum_o[6:8, :] = jnp.zeros((2, D), f32)


def half_col(half, width, base=0):
    lo = half * NCH
    return pl.BlockSpec((width, CH_W), lambda c, *_: (0, base + jnp.clip(c - lo, 0, NCH - 1)))


def half_row(half):
    lo = half * NCH
    return pl.BlockSpec((CH_W, D), lambda c, *_: (jnp.clip(c - lo, 0, NCH - 1), 0))


def feed_forward(lens, h1, mid, th1, tmid, cot, wi, wu, ti, tu, v_a, v_b, rep):
    rows = h1.shape[0]
    full = whole((rows, D))
    anywhere = pl.BlockSpec(memory_space=pl.ANY)
    chunk_out = pl.BlockSpec((rows, CH_W), lambda c, *_: (0, c))
    return pl.pallas_call(
        ff_kernel,
        grid_spec=pltpu.PrefetchScalarGridSpec(
            num_scalar_prefetch=2,
            grid=(2 * NCH,),
            in_specs=[
                anywhere, full, anywhere, full, anywhere,
                half_col(0, D), half_col(1, D), half_row(0), half_row(1),
                half_col(0, D), half_col(1, D), half_row(0), half_row(1),
                half_col(0, 1, BI // CH_W), half_col(1, 1, BI // CH_W),
                half_col(0, 1, CHD // CH_W), half_col(1, 1, CHD // CH_W),
                half_col(0, 1, TI // CH_W), half_col(1, 1, TI // CH_W),
                whole((14, D)),
            ],
            out_specs=[chunk_out, chunk_out, chunk_out, full, full, full, whole((8, D))],
            scratch_shapes=[
                pltpu.VMEM((rows, D), f32),
                pltpu.VMEM((rows, D), f32),
                pltpu.VMEM((rows, D), f32),
                pltpu.VMEM((rows, D), f32),
                pltpu.VMEM((rows, D), bf16),
                pltpu.SemaphoreType.DMA((3,)),
            ],
        ),
        out_shape=[
            SDS((rows, FF), bf16),
            SDS((rows, FF), bf16),
            SDS((rows, FF), bf16),
            SDS((rows, D), bf16),
            SDS((rows, D), f32),
            SDS((rows, D), bf16),
            SDS((8, D), f32),
        ],
        compiler_params=params(42),
        name="feed_forward",
        cost_estimate=cost(45),
    )(
        *lens, h1, mid, th1, tmid, cot, wi[0], wi[1], wu[0], wu[1], ti[0], ti[1], tu[0], tu[1],
        v_a, v_b, v_a, v_b, v_a, v_b, rep,
    )


def fold(place, kind, own, got, high, low):
    n = high.shape[1]
    for r in range(BLOCKS):
        at = pl.ds(pl.multiple_of(place[kind * BLOCKS + r] * n, 16), n)
        value = (own[at, :] + got[at, :].astype(f32)).astype(bf16)
        if r >= BLOCKS // 2:
            high[r - BLOCKS // 2] = value
        else:
            low[r] = value


def fold_shapes(rows, cols):
    return [SDS((BLOCKS // 2, rows // BLOCKS, cols), bf16)] * 2


def outer_grad_kernel(place, dfr, ain, *refs):
    c = pl.program_id(0)
    part = dot(ain[...], dfr[...], TN)
    if len(refs) == 1:
        refs[0][...] = part.astype(bf16)
    else:
        got, high, low, acc = refs
        acc[pl.ds(pl.multiple_of(c * CH_W, CH_W), CH_W), :] = part

        @pl.when(c == NCH - 1)
        def _():
            fold(place, OUTER, acc, got, high, low)


def outer_grad(half, place, dfr, ain, got=None):
    rows = dfr.shape[0]
    in_specs = [
        whole((rows, D)), pl.BlockSpec((rows, CH_W), lambda c, *_: (0, half * NCH + c))
    ]
    if got is None:
        extra, scratch = [], []
        out_shape = SDS((FH, D), bf16)
        out_specs = pl.BlockSpec((CH_W, D), lambda c, *_: (c, 0))
    else:
        extra, scratch = [got], [pltpu.VMEM((FH, D), f32)]
        in_specs.append(whole((FH, D)))
        out_shape = fold_shapes(FH, D)
        out_specs = [whole(v.shape) for v in out_shape]
    return pl.pallas_call(
        outer_grad_kernel,
        grid_spec=pltpu.PrefetchScalarGridSpec(
            num_scalar_prefetch=1,
            grid=(NCH,),
            in_specs=in_specs,
            out_specs=out_specs,
            scratch_shapes=scratch,
        ),
        out_shape=out_shape,
        compiler_params=params(24),
        name="outer_grad",
        cost_estimate=cost(6),
    )(place, dfr, ain, *extra)


def ff_back_kernel(place, dfr, mid, mul, cv, wi, wu, *refs, first):
    if first:
        gi_o, sum_o, dh_o, mid_t = refs
    else:
        before, got, high, low, sum_o, dh_o, mid_t, acc = refs
    c = pl.program_id(0)

    @pl.when(c == 0)
    def _():
        mid_t[...] = mid[...].T
        dh_o[...] = jnp.zeros_like(dh_o) if first else before[...]

    d_ain = dot(dfr[...], wu[...], NT)
    sum_o[1:2, :] = colsum(d_ain * cv[...].astype(f32))
    d_inner = d_ain * mul[...].astype(f32)
    sum_o[0:1, :] = colsum(d_inner)
    sum_o[2:8, :] = jnp.zeros((6, CH_W), f32)
    dir_low = d_inner.astype(bf16)
    part = dot(mid_t[...], dir_low)
    if first:
        gi_o[...] = part.astype(bf16)
    else:
        acc[...] = part
        fold(place, INNER, acc, got, high, low)
    dh_o[...] += dot(dir_low, wi[...], NT)


def ff_back(half, place, dfr, mid, mul, cv, wi, wu, before=None, got=None):
    rows = dfr.shape[0]
    first = before is None
    full = whole((rows, D))
    chunk = pl.BlockSpec((rows, CH_W), lambda c, *_: (0, half * NCH + c))
    col = pl.BlockSpec((D, CH_W), lambda c, *_: (0, c))
    row = pl.BlockSpec((CH_W, D), lambda c, *_: (c, 0))
    in_specs = [full, full, chunk, chunk, col, row]
    scratch = [pltpu.VMEM((D, rows), bf16)]
    if first:
        extra, grad_shape, grad_specs = [], [SDS((D, FH), bf16)], [col]
    else:
        extra, grad_shape = [before, got], fold_shapes(D, FH)
        in_specs += [full, col]
        piece = grad_shape[0].shape
        grad_specs = [pl.BlockSpec(piece[:2] + (CH_W,), lambda c, *_: (0, 0, c))] * 2
        scratch.append(pltpu.VMEM((D, CH_W), f32))
    return pl.pallas_call(
        partial(ff_back_kernel, first=first),
        grid_spec=pltpu.PrefetchScalarGridSpec(
            num_scalar_prefetch=1,
            grid=(NCH,),
            in_specs=in_specs,
            out_specs=grad_specs + [pl.BlockSpec((8, CH_W), lambda c, *_: (0, c)), full],
            scratch_shapes=scratch,
        ),
        out_shape=grad_shape + [SDS((8, FH), f32), SDS((rows, D), f32)],
        compiler_params=params(32),
        name="ff_back",
        cost_estimate=cost(14),
    )(place, dfr, mid, mul, cv, wi, wu, *extra)


def mid_back_kernel(
    r1, dr2, dhin, ctx, wo_a, wo_b, v_a, v_b, rep, dr1_o, dcr_o, go_a, go_b, sum_o, wo, acc
):
    i = pl.program_id(0)

    @pl.when(i == 0)
    def _():
        wo[:DH, :] = wo_a[...]
        wo[DH:, :] = wo_b[...]
        acc[...] = jnp.zeros_like(acc)
        sum_o[...] = jnp.zeros_like(sum_o)

    row = lambda n: rep[n : n + 1, :]
    normed, inv = norm(r1[...])
    cm = row(R_CM)
    ratio = (normed * row(R_G0) + row(R_S0)) * (1.0 / cm)
    th = jnp.tanh(ratio)
    slope = 1.0 - th * th
    d_hin = dhin[...]
    sum_o[3:4, :] += colsum(d_hin * (th - ratio * slope))
    dh1 = dr2[...] + d_hin * slope
    sum_o[0:1, :] += colsum(dh1 * normed)
    sum_o[1:2, :] += colsum(dh1)
    dr1 = norm_back(dh1 * row(R_G0), normed, inv)
    sum_o[2:3, :] += colsum(dr1)
    dr1_o[...] = dr1
    dar = dr1.astype(bf16)
    clip = jnp.concatenate([v_a[:, CC : CC + DH], v_b[:, CC : CC + DH]], 1)
    ratio = ctx[...] * (1.0 / clip)
    th = jnp.tanh(ratio)
    slope = 1.0 - th * th
    acc[...] += dot(dar, (clip * th).astype(bf16), TN)
    d_cin = dot(dar, wo[...], NT)
    sum_o[4:5, :] += colsum(d_cin * (th - ratio * slope))
    dcr_o[...] = (d_cin * slope).astype(bf16)

    @pl.when(i == pl.num_programs(0) - 1)
    def _():
        go_a[...] = acc[:, :DH].astype(bf16)
        go_b[...] = acc[:, DH:].astype(bf16)


def mid_back(r1, dr2, dhin, ctx, wo_a, wo_b, v_a, v_b, rep):
    rows = r1.shape[0]
    block = pl.BlockSpec((RB, D), lambda i: (i, 0))
    return pl.pallas_call(
        mid_back_kernel,
        grid=(rows // RB,),
        in_specs=[block] * 4
        + [whole((DH, D)), whole((DH, D)), whole((1, VEND)), whole((1, VEND)), whole((14, D))],
        out_specs=[block, block, whole((D, DH)), whole((D, DH)), whole((8, D))],
        out_shape=[
            SDS((rows, D), f32),
            SDS((rows, D), bf16),
            SDS((D, DH), bf16),
            SDS((D, DH), bf16),
            SDS((8, D), f32),
        ],
        scratch_shapes=[pltpu.VMEM((D, D), bf16), pltpu.VMEM((D, D), f32)],
        compiler_params=params(20),
        name="mid_back",
        cost_estimate=cost(12),
    )(r1, dr2, dhin, ctx, wo_a, wo_b, v_a, v_b, rep)


LEAD, REST = 128, 256


def attn_back_kernel(
    lens, first, place, qkv, dc, ctx, lse, xt, *refs, pairs, kind, with_out, folded
):
    refs = list(refs)
    got_out = refs.pop(0) if with_out else None
    got = refs.pop(0) if folded else None
    d_o, *grads = refs[: 3 if folded else 2]
    sum_o, acc = refs[-2:]
    seq = pl.program_id(0)
    length = lens[first[0] + seq]
    width = 128 * len(pairs)
    lo = pairs[0] * 128
    pick = lax.broadcasted_iota(jnp.int32, (8, width), 1) // HD
    pick = (pick == lax.broadcasted_iota(jnp.int32, (8, width), 0)).astype(f32)
    cols = slice(lo, lo + width)
    deltas = lax.dot_general(
        pick, dc[:, cols].astype(f32) * ctx[:, cols], NT, precision=lax.Precision.HIGHEST,
        preferred_element_type=f32,
    )
    heads = [(n, h) for n in range(len(pairs)) for h in range(2)]

    def part_of(n, k):
        at = pairs[n] * 128 + k * DH
        return qkv[:, at : at + 128]

    def dc_of(n):
        return dc[:, pairs[n] * 128 : (pairs[n] + 1) * 128]

    def score(n, h):
        q_h, k_h = with_mask(part_of(n, 0), part_of(n, 1), length, h)
        return dot(k_h, q_h, NT), dot(pair_of(part_of(n, 2), h), dc_of(n), NT)

    @pl.when(seq == 0)
    def _():
        sum_o[...] = jnp.zeros_like(sum_o)

    scores = [score(*heads[0])]
    for i, (n, h) in enumerate(heads):
        if i + 1 < len(heads):
            scores.append(score(*heads[i + 1]))
        s, dp = scores[i]
        row = 2 * pairs[n] + h
        prob = jnp.exp(s - lse[0, row : row + 1, :])
        row = 2 * n + h
        ds = (prob * (dp - deltas[row : row + 1, :])).astype(bf16)
        if h == 0:
            k_t = part_of(n, 1).T
        part_q = dot(k_t[h * HD : (h + 1) * HD], ds)
        part_k = dot(ds, pair_of(part_of(n, 0), h))
        part_v = dot(prob.astype(bf16), pair_of(dc_of(n), h))
        if h == 0:
            d_q, d_k, d_v = part_q, part_k, part_v
        else:
            d_q = jnp.concatenate([d_q, part_q], 0).T * HD**-0.5
            d_v = d_v + part_v
            for k, d in enumerate((d_q, d_k + part_k, d_v)):
                at = k * width + n * 128
                d_o[:, at : at + 128] = d.astype(bf16)
            cols = slice(n * 128, (n + 1) * 128)
            sum_o[0:1, cols] += colsum(d_q)
            sum_o[1:2, cols] += colsum(d_v)
    part = dot(xt[...], d_o[...])
    n = 3 * width

    @pl.when(seq == 0)
    def _():
        acc[:, :n] = part
        if with_out:
            acc[:, n:] = got_out[...].astype(f32)

    @pl.when(seq > 0)
    def _():
        acc[:, :n] += part

    @pl.when(seq == pl.num_programs(0) - 1)
    def _():
        if folded:
            fold(place, kind, acc, got, *grads)
        else:
            grads[0][...] = acc[...].astype(bf16)


def attention_back(half, kind, lens, place, qkv, dcr, ctx, lse, x_t, out_grad=None, got=None):
    rows = qkv.shape[0]
    nseq = rows // SEQ
    pairs = (0,) if kind == FIRST else (1, 2)
    width = 128 * len(pairs)
    block = lambda n: pl.BlockSpec((SEQ, n), lambda s, *_: (s, half))
    in_specs = [
        block(QW),
        block(DH),
        block(DH),
        pl.BlockSpec((1, 8, SEQ), lambda s, *_: (2 * s + half, 0, 0)),
        pl.BlockSpec((D, SEQ), lambda s, *_: (0, s)),
    ]
    extra = [v for v in (out_grad, got) if v is not None]
    grad_shape = [SDS((D, D), bf16)] if got is None else fold_shapes(D, D)
    return pl.pallas_call(
        partial(
            attn_back_kernel,
            pairs=pairs, kind=kind, with_out=out_grad is not None, folded=got is not None,
        ),
        grid_spec=pltpu.PrefetchScalarGridSpec(
            num_scalar_prefetch=3,
            grid=(nseq,),
            in_specs=in_specs + [whole(v.shape) for v in extra],
            out_specs=[pl.BlockSpec((SEQ, 3 * width), lambda s, *_: (s, 0))]
            + [whole(v.shape) for v in grad_shape]
            + [whole((8, width))],
            scratch_shapes=[pltpu.VMEM((D, D), f32)],
        ),
        out_shape=[SDS((rows, 3 * width), bf16)] + grad_shape + [SDS((8, width), f32)],
        compiler_params=params(20),
        name="attention_back",
        cost_estimate=cost(6 * len(pairs)),
    )(*lens, place, qkv, dcr, ctx, lse, x_t, *extra)


def clip_in(x, rep):
    clip = rep[R_CI : R_CI + 1, :]
    ratio = x[...].astype(f32) * (1.0 / clip)
    return ratio, jnp.tanh(ratio)


def x_back_kernel(x, d_la, d_lb, d_a, d_b, dr1, w_a, w_b, rep, grad_o, sum_o, w_lead, w_rest):
    @pl.when(pl.program_id(0) == 0)
    def _():
        sum_o[...] = jnp.zeros_like(sum_o)
        for half, w in enumerate((w_a, w_b)):
            for k in range(3):
                at = half * DH + k * LEAD
                w_lead[:, at : at + LEAD] = w[:, k * DH : k * DH + LEAD]
                at = half * D + k * REST
                w_rest[:, at : at + REST] = w[:, k * DH + LEAD : (k + 1) * DH]

    total = (
        dot(jnp.concatenate([d_la[...], d_lb[...]], 1), w_lead[...], NT)
        + dot(d_a[...], w_rest[:, :D], NT)
        + dot(d_b[...], w_rest[:, D:], NT)
    )
    ratio, th = clip_in(x, rep)
    slope = 1.0 - th * th
    grad_o[...] = dr1[...] + total * slope
    sum_o[0:1, :] += colsum(total * (th - ratio * slope))


RB = 256


def x_back(x, d_la, d_lb, d_a, d_b, dr1, w_a, w_b, rep):
    rows = x.shape[0]
    block = pl.BlockSpec((RB, D), lambda i: (i, 0))
    narrow = pl.BlockSpec((RB, DH), lambda i: (i, 0))
    return pl.pallas_call(
        x_back_kernel,
        grid=(rows // RB,),
        in_specs=[block, narrow, narrow, block, block, block] + [whole((D, QW)), whole((D, QW)), whole((14, D))],
        out_specs=[block, whole((8, D))],
        out_shape=[SDS((rows, D), f32), SDS((8, D), f32)],
        scratch_shapes=[pltpu.VMEM((D, D), bf16), pltpu.VMEM((D, 2 * D), bf16)],
        compiler_params=params(20),
        name="x_back",
        cost_estimate=cost(8),
    )(x, d_la, d_lb, d_a, d_b, dr1, w_a, w_b, rep)


def pack_kernel(ha, hb, la, lb, qa, qb, m, f, a, x, out):
    for side, (h, l, q) in enumerate(((ha, la, qa), (hb, lb, qb))):
        base = 6 * side
        for n in range(2):
            out[base + 2 * n : base + 2 * n + 1, :] = h[n : n + 1, :D]
            out[base + 2 * n + 1 : base + 2 * n + 2, :] = h[n : n + 1, D:]
        for k in range(2):
            at = k * DH
            out[base + 4 : base + 5, at : at + LEAD] = l[k : k + 1, :]
            out[base + 4 : base + 5, at + LEAD : at + DH] = q[k : k + 1, :]
        out[base + 5 : base + 6, :DH] = m[4:5, side * DH : (side + 1) * DH]
        out[base + 5 : base + 6, DH:] = jnp.zeros((1, DH), f32)
    rows = (
        (m, 2), (f, 2), (m, 0), (f, 0), (m, 1), (f, 1), (x, 0), (m, 3),
        (f, 3), (f, 4), (a, 0), (f, 5),
    )
    for n, (ref, k) in enumerate(rows):
        out[12 + n : 13 + n, :] = ref[k : k + 1, :]


def pack(*sums):
    return pl.pallas_call(
        pack_kernel,
        grid=(1,),
        in_specs=[whole(v.shape) for v in sums],
        out_specs=whole((24, D)),
        out_shape=SDS((24, D), f32),
        compiler_params=params(4),
        name="pack",
        cost_estimate=cost(1),
    )(*sums)


BLOCKS = 16
OUTER, INNER, FIRST, LAST = range(4)
ORDERS = (
    ((1, 2, 4, 8), (2, 4, 1, 8)),
    ((4, 1, 2, 8), (1, 4, 2, 8)),
    ((1, 2, 4, 8), (2, 4, 1, 8)),
    ((1, 2, 4, 8), (2, 4, 1, 8)),
)


def spread(order, r):
    return sum(mask for p, mask in enumerate(order) if r & (BLOCKS >> (p + 1)))


def place_table(me, core):
    rows = []
    for pair in ORDERS:
        a, b = [jnp.asarray([spread(o, r) for r in range(BLOCKS)], jnp.int32) for o in pair]
        rows.append(jnp.where(core == 0, a, b) ^ me)
    return jnp.concatenate(rows)


def swap(value, masks, n_dp):
    pairs = [(2 * i + t, 2 * (i ^ masks[t]) + t) for i in range(n_dp) for t in range(2)]
    return lax.ppermute(value, ("dp", "tensor"), pairs)


class Sum:
    def __init__(self, pieces, kind, n_dp):
        self.kind, self.n_dp = kind, n_dp
        self.send, self.hold = pieces
        self.step = 0
        self.recv = self.swap(0)

    def swap(self, step):
        return swap(self.send, tuple(order[step] for order in ORDERS[self.kind]), self.n_dp)

    def advance(self, *done):
        self.recv, *done = lax.optimization_barrier((self.recv, *done))
        self.step += 1
        half = self.hold.shape[0] // 2
        if self.step <= 3:
            self.send = self.hold[half:] + self.recv[half:]
            self.hold = self.hold[:half] + self.recv[:half]
            self.recv = self.swap(self.step)
        elif self.step == 4:
            self.send = self.hold + self.recv
            mask = BLOCKS
            while mask < self.n_dp:
                self.send = self.send + swap(self.send, (mask, mask), self.n_dp)
                mask *= 2
            self.recv = self.swap(3)
        elif self.step <= 7:
            self.send = jnp.concatenate([self.send, self.recv], 0)
            self.recv = self.swap(7 - self.step)
        return done

    def result(self, *done):
        self.recv, *done = lax.optimization_barrier((self.recv, *done))
        return (self.send, self.recv)


class Small(Sum):
    def __init__(self, value, n_dp):
        self.n_dp = n_dp
        self.mask, self.send = 1, value
        self.recv = swap(value, (1, 1), n_dp)

    def advance(self, *done):
        self.recv, *done = lax.optimization_barrier((self.recv, *done))
        self.send = self.send + self.recv
        self.mask *= 2
        if self.mask < self.n_dp:
            self.recv = swap(self.send, (self.mask, self.mask), self.n_dp)
        return done

    def result(self):
        while self.mask < self.n_dp:
            self.advance()
        return self.send


def step(streams, *values):
    for stream in streams:
        values = stream.advance(*values)
    return behind(streams, *values)


def behind(streams, *values):
    sent = [s.send for s in streams]
    return lax.optimization_barrier((*sent, *values))[len(sent) :]


def latent(w, g, axis, factor):
    th = jnp.tanh(2.0 * w)
    n = w.shape[axis]
    mean = jnp.sum(jnp.abs(w), axis, keepdims=True) * (1.0 / n)
    inner = jnp.sum(g * th, axis, keepdims=True) * (1.0 / n)
    sign = jnp.where(w > 0, 1.0, jnp.where(w < 0, -1.0, 0.0))
    return factor * (2.0 * mean * (1.0 - th * th) * g + sign * inner)


def collect(place, mine, recv, kind, target):
    n = mine.shape[1]
    for r in range(BLOCKS):
        at = pl.multiple_of(place[kind * BLOCKS + r] * n, 16)
        target[pl.ds(at, n), :] = (mine if r < BLOCKS // 2 else recv)[r % 8]


def latent_kernel(place, mine, recv, w, out, g, *, kind):
    i = pl.program_id(0)

    @pl.when(i == 0)
    def _():
        collect(place, mine, recv, kind, g)

    n = FH // 4
    at = pl.ds(pl.multiple_of(i * n, 128), n)
    if kind == OUTER:
        out[...] = latent(w[...], g[at, :].astype(f32), 1, 1.0 / math.sqrt(FF))
    else:
        out[...] = latent(w[...], g[:, at].astype(f32), 0, 1.0 / math.sqrt(D))


def ffn_latent(kind, place, pieces, w):
    if kind == OUTER:
        block = pl.BlockSpec((FH // 4, D), lambda i, *_: (i, 0))
    else:
        block = pl.BlockSpec((D, FH // 4), lambda i, *_: (0, i))
    return pl.pallas_call(
        partial(latent_kernel, kind=kind),
        grid_spec=pltpu.PrefetchScalarGridSpec(
            num_scalar_prefetch=1,
            grid=(4,),
            in_specs=[whole(p.shape) for p in pieces] + [block],
            out_specs=block,
            scratch_shapes=[pltpu.VMEM(w.shape, bf16)],
        ),
        out_shape=SDS(w.shape, f32),
        compiler_params=params(16),
        name="ffn_latent",
        cost_estimate=cost(8),
    )(place, *pieces, w)


def attn_latent_kernel(place, *refs):
    pieces, w_in, wo, outs, go, g, h = refs[:4], refs[4:7], refs[7], refs[8:11], *refs[11:]
    root = 1.0 / math.sqrt(D)
    collect(place, *pieces[:2], FIRST, g)
    collect(place, *pieces[2:], LAST, h)
    for c in range(3):
        for src, at, n in ((g, 0, LEAD), (h, LEAD, REST)):
            grad = src[:, c * n : (c + 1) * n].astype(f32)
            cols = slice(at, at + n)
            outs[c][:, cols] = latent(w_in[c][:, cols], grad, 0, root if c == 2 else 2.0 * root)
    go[...] = latent(wo[...], g[:, DH:].astype(f32).T, 1, 8.0 * root)


def attn_latent(place, pieces, wq, wk, wv, wo):
    col, row = whole((D, DH)), whole((DH, D))
    return pl.pallas_call(
        attn_latent_kernel,
        grid_spec=pltpu.PrefetchScalarGridSpec(
            num_scalar_prefetch=1,
            grid=(1,),
            in_specs=[whole(p.shape) for p in pieces] + [col, col, col, row],
            out_specs=[col, col, col, row],
            scratch_shapes=[pltpu.VMEM((D, D), bf16)] * 2,
        ),
        out_shape=[SDS((D, DH), f32)] * 3 + [SDS((DH, D), f32)],
        compiler_params=params(24),
        name="attn_latent",
        cost_estimate=cost(9),
    )(place, *pieces, wq, wk, wv, wo)


def on_device(
    n_dp,
    tokens, cotangent, lengths, w_query, w_key, w_value, w_output, w_inner, w_outer,
    b_query, b_value, b_output, b_inner, b_outer, ln_gains, ln_shifts,
    clip_input, clip_context, clip_middle, clip_hidden,
    t_query, t_key, t_value, t_output, t_inner, t_outer,
    tb_query, tb_value, tb_output, tb_inner, tb_outer, t_gains, t_shifts,
):
    other = lambda value: lax.ppermute(value, "tensor", [(0, 1), (1, 0)])
    rows = tokens.shape[0]
    nseq = rows // SEQ
    core = lax.axis_index("tensor")
    place = place_table(lax.axis_index("dp").astype(jnp.int32), core)
    lens = (lengths, (core * nseq).astype(jnp.int32).reshape(1))

    t_own = (t_query, t_key, t_value)
    t_other = tuple(other(w) for w in t_own)
    t_out_b = other(t_output)
    wqkv, wo, wi, wu, v_a, rep = prep(
        (w_query, w_key, w_value, w_output, w_inner, w_outer),
        (b_inner, clip_hidden, tb_inner, b_query, b_value, clip_context, tb_query, tb_value),
        (
            b_output, b_outer, ln_gains, ln_shifts, clip_input, clip_middle,
            tb_output, tb_outer, t_gains, t_shifts,
        ),
    )
    v_b = other(v_a)
    wqkv_b, wo_b = other(wqkv), other(wo)
    th1, tmid = encode(lens, tokens, t_own + t_other, t_output, t_out_b, v_a, v_b, rep, False)
    late = lax.optimization_barrier((v_b, t_inner, t_outer, wi, wu))[1:]
    ti_b, tu_b, wi_b, wu_b = [other(w) for w in late]
    qkv, ctx, lse, r1, h1, mid, x_t, sum_a = encode(
        lens, tokens, (wqkv, wqkv_b), wo, wo_b, v_a, v_b, rep, True
    )
    ain, mul, cv, layer_out, dr2, dfr, sum_f = feed_forward(
        lens, h1, mid, th1, tmid, cotangent, (wi, wi_b), (wu, wu_b), (t_inner, ti_b),
        (t_outer, tu_b), v_a, v_b, rep,
    )
    gu_b = outer_grad(1, place, dfr, ain)
    gu_c = other(gu_b)
    dfr, _ = lax.optimization_barrier((dfr, gu_b))
    gi_b, sum_hb, dh_b = ff_back(1, place, dfr, mid, mul, cv, wi_b, wu_b)
    gi_c = other(gi_b)
    dfr, gu_c, _ = lax.optimization_barrier((dfr, gu_c, gi_b))
    outer = Sum(outer_grad(0, place, dfr, ain, gu_c), OUTER, n_dp)
    dh_b, gi_c = behind([outer], dh_b, gi_c)
    *gi, sum_ha, dhin = ff_back(0, place, dfr, mid, mul, cv, wi, wu, dh_b, gi_c)
    inner = Sum(gi, INNER, n_dp)
    (dhin,) = outer.advance(dhin)
    (dhin,) = behind([outer, inner], dhin)
    dr1, dcr, go_a, go_b, sum_m = mid_back(r1, dr2, dhin, ctx, wo, wo_b, v_a, v_b, rep)
    (dcr,) = step([outer, inner], dcr)
    saved = (qkv, dcr, ctx, lse, x_t)
    d_lb, gl_b, sum_lb = attention_back(1, FIRST, lens, place, *saved, go_b)
    gl_c = other(gl_b)
    dcr, _ = step([outer, inner], dcr, gl_b)
    saved = (qkv, dcr, ctx, lse, x_t)
    d_b, gs_b, sum_b = attention_back(1, LAST, lens, place, *saved)
    gs_c = other(gs_b)
    gl_c, dcr, _ = step([outer, inner], gl_c, dcr, gs_b)
    saved = (qkv, dcr, ctx, lse, x_t)
    d_la, *gl, sum_la = attention_back(0, FIRST, lens, place, *saved, go_a, gl_c)
    lead = Sum(gl, FIRST, n_dp)
    gs_c, dcr, _ = step([outer, inner], gs_c, dcr, d_la)
    gs_c, dcr = behind([lead], gs_c, dcr)
    saved = (qkv, dcr, ctx, lse, x_t)
    d_a, *gs, sum_q = attention_back(0, LAST, lens, place, *saved, None, gs_c)
    last = Sum(gs, LAST, n_dp)
    dr1, _ = step([outer, inner, lead], dr1, d_a)
    (dr1,) = behind([last], dr1)
    grad_tokens, sum_x = x_back(tokens, d_la, d_lb, d_a, d_b, dr1, wqkv, wqkv_b, rep)
    sums = pack(sum_ha, sum_hb, sum_la, sum_lb, sum_q, sum_b, sum_m, sum_f, sum_a, sum_x)
    from_other = other(sums[6:])
    (sums,) = step([last, outer, inner, lead], sums)
    small = Small(jnp.concatenate([sums[:6], sums[12:]], 0) + from_other, n_dp)
    step([last, inner, lead, small])
    (w_o,) = step([last, inner, lead, small], w_outer)
    g_outer = ffn_latent(OUTER, place, outer.result(), w_o)
    step([last, lead, small], g_outer)
    step([last, lead, small])
    step([last, lead])
    (w_i,) = step([last], w_inner)
    small = small.result()
    g_inner = ffn_latent(INNER, place, inner.result(), w_i)
    last.recv, g_inner = lax.optimization_barrier((last.recv, g_inner))
    g_query, g_key, g_value, g_output = attn_latent(
        place, lead.result() + last.result(), w_query, w_key, w_value, w_output
    )
    split, shared = small[:6], small[6:]
    count = jnp.asarray(rows * 2 * n_dp * D, f32)
    stats = jnp.sum(shared[8:], 1) / count
    summary = jnp.concatenate([stats[:1], jnp.sqrt(stats[1:])])
    return (
        layer_out,
        grad_tokens,
        g_query,
        g_key,
        g_value,
        g_output,
        g_inner,
        g_outer,
        split[4, :DH],
        split[4, DH:],
        shared[0],
        split[0:2].reshape(FH),
        shared[1],
        shared[2:4],
        shared[4:6],
        shared[6],
        split[5, :DH],
        shared[7],
        split[2:4].reshape(FH),
        summary,
    )


def solution(mesh):
    rows, cols, split, full = P(("dp", "tensor"), None), P(None, "tensor"), P("tensor"), P()
    down = P("tensor", None)
    return jax.shard_map(
        partial(on_device, mesh.shape["dp"]),
        mesh=mesh,
        in_specs=(
            rows, rows, P("dp"), cols, cols, cols, down, cols, down,
            split, split, full, split, full, full, full,
            full, split, full, split,
            cols, cols, cols, down, cols, down,
            split, split, full, split, full, full, full,
        ),
        out_specs=(
            rows, rows, cols, cols, cols, down, cols, down,
            split, split, full, split, full, full, full, full, split, full, split, full,
        ),
        check_vma=False,
    )
```

```python
from functools import partial
import math

import jax
import jax.numpy as jnp
from jax import lax
import jax.experimental.pallas as pl
import jax.experimental.pallas.tpu as pltpu
from jax.sharding import PartitionSpec as P

D = 768
FF = 3072
SEQ = 512
HD = 64
DH = D // 2
FH = FF // 2
QW = 3 * DH

CH_W = 512
NCH = FH // CH_W
EPS = 1e-12

BI, CHD, TI, BQ, BV, CC, TQ, TV, VEND = 0, 1536, 3072, 4608, 4992, 5376, 5760, 6144, 6528
R_BO, R_BU, R_G0, R_G1, R_S0, R_S1, R_CI, R_CM, R_TBO, R_TBU, R_TG0, R_TG1, R_TS0, R_TS1 = range(14)

f32 = jnp.float32
bf16 = jnp.bfloat16
NT = (((1,), (1,)), ((), ()))
NN = (((1,), (0,)), ((), ()))
TN = (((0,), (0,)), ((), ()))
SDS = jax.ShapeDtypeStruct


def dot(left, right, dims=NN):
    return lax.dot_general(left, right, dims, preferred_element_type=f32)


def params(mib):
    return pltpu.CompilerParams(vmem_limit_bytes=mib * 2**20)


def cost(micros):
    return pl.CostEstimate(
        flops=micros * 10**9, transcendentals=0, bytes_accessed=micros * 3 * 10**6
    )


def whole(shape):
    rank = len(shape)
    return pl.BlockSpec(shape, lambda *_: (0,) * rank, pipeline_mode=pl.Buffered(1))


def norm(resid):
    centered = resid - jnp.mean(resid, -1, keepdims=True)
    inv = lax.rsqrt(jnp.mean(centered * centered, -1, keepdims=True) + EPS)
    return centered * inv, inv


def colsum(value):
    return jnp.sum(value, 0, keepdims=True)


def norm_back(e, normed, inv):
    return inv * (
        e - jnp.mean(e, -1, keepdims=True) - normed * jnp.mean(e * normed, -1, keepdims=True)
    )


def keep_rows(length):
    return (lax.broadcasted_iota(jnp.int32, (SEQ, 1), 0) < length).astype(f32)


def bin_cols(w, factor):
    return (jnp.mean(jnp.abs(w), 0, keepdims=True) * jnp.tanh(2.0 * w) * factor).astype(bf16)


def bin_rows(w, factor):
    return (jnp.mean(jnp.abs(w), 1, keepdims=True) * jnp.tanh(2.0 * w) * factor).astype(bf16)


SPLIT = (FH, FH, FH, DH, DH, DH, DH, DH)


def prep_kernel(*refs):
    wq, wk, wv, wo, wi, wu = refs[:6]
    split = refs[6:14]
    full = refs[14:24]
    qkv_o, wo_o, wi_o, wu_o, vec_o, rep_o = refs[24:]
    i = pl.program_id(0)
    root = 1.0 / math.sqrt(D)
    wi_o[...] = bin_cols(wi[...], root)
    wu_o[...] = bin_rows(wu[...], 1.0 / math.sqrt(FF))

    @pl.when(i == 0)
    def _():
        qkv_o[:, :DH] = bin_cols(wq[...], 2.0 * root)
        at = 0
        for ref, n in zip(split, SPLIT):
            vec_o[0, at : at + n] = ref[...]
            at += n
        at = 0
        for ref in full:
            if len(ref.shape) == 1:
                rep_o[at, :] = ref[...]
                at += 1
            else:
                rep_o[at : at + 2, :] = ref[...]
                at += 2

    @pl.when(i == 1)
    def _():
        qkv_o[:, DH : 2 * DH] = bin_cols(wk[...], 2.0 * root)

    @pl.when(i == 2)
    def _():
        qkv_o[:, 2 * DH :] = bin_cols(wv[...], root)

    @pl.when(i == 3)
    def _():
        wo_o[...] = bin_rows(wo[...], 8.0 * root)


def prep(weights, split, full):
    n = 4
    col = pl.BlockSpec((D, FH // n), lambda i: (0, i))
    row = pl.BlockSpec((FH // n, D), lambda i: (i, 0))
    return pl.pallas_call(
        prep_kernel,
        grid=(n,),
        in_specs=[whole((D, DH))] * 3
        + [whole((DH, D)), col, row]
        + [whole(v.shape) for v in (*split, *full)],
        out_specs=[
            whole((D, QW)), whole((DH, D)), col, row, whole((1, VEND)), whole((14, D)),
        ],
        out_shape=[
            SDS((D, QW), bf16),
            SDS((DH, D), bf16),
            SDS((D, FH), bf16),
            SDS((FH, D), bf16),
            SDS((1, VEND), f32),
            SDS((14, D), f32),
        ],
        compiler_params=params(60),
        name="prep",
        cost_estimate=cost(8),
    )(*weights, *split, *full)


def head_lanes(h):
    return lax.broadcasted_iota(jnp.int32, (1, 128), 1) // HD == h


def pair_of(value, h):
    return jnp.where(head_lanes(h), value, jnp.zeros((), value.dtype))


def with_mask(qq, kk, length, h):
    lane = lax.broadcasted_iota(jnp.int32, (1, 128), 1)
    spare = lane == HD * (1 - h)
    valid = lax.broadcasted_iota(jnp.int32, (SEQ, 1), 0) < length
    bias = jnp.where(valid, 0.0, -1e9).astype(bf16)
    k_h = jnp.where(spare, bias, pair_of(kk, h))
    return jnp.where(spare, jnp.ones((), bf16), qq), k_h


def attend(length, qkv_half, store):
    heads = [(half, p, h) for half in range(2) for p in range(3) for h in range(2)]

    def score(half, p, h):
        ref, base = qkv_half(half)
        at = base + p * 128
        q_h, k_h = with_mask(ref[:, at : at + 128], ref[:, at + DH : at + DH + 128], length, h)
        return dot(k_h, q_h, NT)

    ones = jnp.ones((16, SEQ), bf16)
    scores = [score(*heads[0]), score(*heads[1])]
    pair = []
    for i, (half, p, h) in enumerate(heads):
        if i + 2 < len(heads):
            scores.append(score(*heads[i + 2]))
        s = scores[i]
        top = jnp.max(s, 0, keepdims=True)
        e = jnp.exp(s - top).astype(bf16)
        ref, base = qkv_half(half)
        if h == 0:
            at = base + 2 * DH + p * 128
            v_t = ref[:, at : at + 128].T
        part = dot(jnp.concatenate([v_t[h * HD : (h + 1) * HD], ones], 0), e)
        total = part[HD : HD + 1]
        pair.append(part[:HD] * (1.0 / total))
        store(half, p, h, pair, top, total)
        if h:
            pair = []


def encode_kernel(lens, first, x, *refs, student):
    n = 1 if student else 3
    weights, refs = refs[: 2 * n], refs[2 * n :]
    wo_a, wo_b, v_a, v_b, rep = refs[:5]
    if student:
        qkv, ctx, lse, r1_o, h1_o, mid_o, xt_o, sum_o, wo = refs[5:]
    else:
        h1_o, mid_o, wo, qkv, ctx, w_all = refs[5:]
    i = pl.program_id(0)

    @pl.when(i == 0)
    def _():
        wo[:DH, :] = wo_a[...]
        wo[DH:, :] = wo_b[...]
        if student:
            sum_o[...] = jnp.zeros_like(sum_o)
        else:
            for k in range(6):
                w_all[:, k * DH : (k + 1) * DH] = weights[k][...]

    row = lambda k: rep[k : k + 1, :]
    length = lens[first[0] + i]
    xx = x[...]
    mine = xx.astype(f32)
    if student:
        clip = row(R_CI)
        xx = (clip * jnp.tanh(mine * (1.0 / clip))).astype(bf16)
        xt_o[...] = xx.T
    off_q, off_v = (BQ, BV) if student else (TQ, TV)
    for half, v in enumerate((v_a, v_b)):
        base = half * QW
        res = dot(xx, weights[half][...] if student else w_all[:, base : base + QW])
        q = (res[:, :DH] + v[:, off_q : off_q + DH]).astype(bf16)
        qkv[:, base : base + DH] = q * jnp.asarray(HD**-0.5, bf16)
        qkv[:, base + DH : base + 2 * DH] = res[:, DH : 2 * DH].astype(bf16)
        qkv[:, base + 2 * DH : base + QW] = (
            res[:, 2 * DH :] + v[:, off_v : off_v + DH]
        ).astype(bf16)

    def store(half, p, h, pair, top, total):
        if h:
            at = half * DH + p * 128
            ctx[:, at : at + 128] = jnp.concatenate(pair, 0).T.astype(ctx.dtype)
        if student:
            lse[half, 2 * p + h : 2 * p + h + 1, :] = top + jnp.log(total)

    attend(length, lambda half: (qkv, half * QW), store)
    if student:
        clip = jnp.concatenate([v_a[:, CC : CC + DH], v_b[:, CC : CC + DH]], 1)
        cin = (clip * jnp.tanh(ctx[...] * (1.0 / clip))).astype(bf16)
        branch = dot(cin, wo[...]) + row(R_BO)
        r1 = mine + branch
        normed, _ = norm(r1)
        h1 = normed * row(R_G0) + row(R_S0)
        cm = row(R_CM)
        r1_o[...] = r1
        h1_o[...] = h1
        mid_o[...] = (cm * jnp.tanh(h1 * (1.0 / cm))).astype(bf16)
        sum_o[0:1, :] += colsum(keep_rows(length) * branch * branch)
    else:
        branch = dot(ctx[...], wo[...]) + row(R_TBO)
        normed, _ = norm(mine + branch)
        h1 = normed * row(R_TG0) + row(R_TS0)
        h1_o[...] = h1
        mid_o[...] = h1.astype(bf16)


def encode(lens, x, weights, wo_a, wo_b, v_a, v_b, rep, student):
    rows = x.shape[0]
    block = pl.BlockSpec((SEQ, D), lambda i, *_: (i, 0))
    wide = SDS((rows, D), f32)
    if student:
        out_specs = [
            pl.BlockSpec((SEQ, 2 * QW), lambda i, *_: (i, 0)),
            block,
            pl.BlockSpec((2, 8, SEQ), lambda i, *_: (i, 0, 0)),
            block,
            block,
            block,
            pl.BlockSpec((D, SEQ), lambda i, *_: (0, i)),
            pl.BlockSpec((8, D), lambda i, *_: (0, 0)),
        ]
        out_shape = [
            SDS((rows, 2 * QW), bf16), wide, SDS((rows // SEQ * 2, 8, SEQ), f32),
            wide, wide, SDS((rows, D), bf16), SDS((D, rows), bf16), SDS((8, D), f32),
        ]
        scratch = [pltpu.VMEM((D, D), bf16)]
    else:
        out_specs = [block, block]
        out_shape = [wide, SDS((rows, D), bf16)]
        scratch = [
            pltpu.VMEM((D, D), bf16),
            pltpu.VMEM((SEQ, 2 * QW), bf16),
            pltpu.VMEM((SEQ, D), bf16),
            pltpu.VMEM((D, 2 * QW), bf16),
        ]
    return pl.pallas_call(
        partial(encode_kernel, student=student),
        grid_spec=pltpu.PrefetchScalarGridSpec(
            num_scalar_prefetch=2,
            grid=(rows // SEQ,),
            in_specs=[block]
            + [whole(w.shape) for w in weights]
            + [whole((DH, D)), whole((DH, D))]
            + [whole((1, VEND)), whole((1, VEND)), whole((14, D))],
            out_specs=out_specs,
            scratch_shapes=scratch,
        ),
        out_shape=out_shape,
        compiler_params=params(44 if student else 60),
        name="encode",
        cost_estimate=cost(25),
    )(*lens, x, *weights, wo_a, wo_b, v_a, v_b, rep)


ROWS = 256


def ff_kernel(
    lens, first, h1, mid, th1, tmid, cot, wi_a, wi_b, wu_a, wu_b, ti_a, ti_b, tu_a, tu_b,
    bi_a, bi_b, ch_a, ch_b, tb_a, tb_b, rep,
    ain_o, mul_o, cv_o, lo_o, dr2_o, dfr_o, sum_o, acc_s, acc_t, h1_v, th1_v, cot_v, sems,
):
    c = pl.program_id(0)
    rows = h1.shape[0]
    late = [
        pltpu.make_async_copy(src, dst, sems.at[n])
        for n, (src, dst) in enumerate(((h1, h1_v), (th1, th1_v), (cot, cot_v)))
    ]

    @pl.when(c == 0)
    def _():
        acc_s[...] = jnp.zeros_like(acc_s)
        acc_t[...] = jnp.zeros_like(acc_t)
        for copy in late:
            copy.start()

    def chunk(wi, wu, ti, tu, bi, ch, tb):
        inv_clip = 1.0 / ch[...]

        def block(i, carry):
            r = pl.ds(pl.multiple_of(i * ROWS, ROWS), ROWS)
            inner = dot(mid[r, :], wi[...]) + bi[...]
            t_inner = dot(tmid[r, :], ti[...]) + tb[...]
            cdf = 0.5 * (1.0 + lax.erf(inner * (2.0**-0.5)))
            act = inner * cdf
            deriv = cdf + inner * (jnp.exp(-0.5 * inner * inner) * (1.0 / math.sqrt(2.0 * math.pi)))
            ratio = act * inv_clip
            th = jnp.tanh(ratio)
            slope = 1.0 - th * th
            ain = (ch[...] * th).astype(bf16)
            ain_o[r, :] = ain
            mul_o[r, :] = (slope * deriv).astype(bf16)
            cv_o[r, :] = (th - ratio * slope).astype(bf16)
            acc_s[r, :] += dot(ain, wu[...])
            t_act = (t_inner * (0.5 * (1.0 + lax.erf(t_inner * (2.0**-0.5))))).astype(bf16)
            acc_t[r, :] += dot(t_act, tu[...])
            return carry

        lax.fori_loop(0, rows // ROWS, block, 0, unroll=True)

    @pl.when(c < NCH)
    def _():
        chunk(wi_a, wu_a, ti_a, tu_a, bi_a, ch_a, tb_a)

    @pl.when(c >= NCH)
    def _():
        chunk(wi_b, wu_b, ti_b, tu_b, bi_b, ch_b, tb_b)

    @pl.when(c == 2 * NCH - 1)
    def _():
        for copy in late:
            copy.wait()
        row = lambda n: rep[n : n + 1, :]
        total = [jnp.zeros((1, D), f32)] * 6
        for s in range(rows // SEQ):
            r = slice(s * SEQ, (s + 1) * SEQ)
            keep = keep_rows(lens[first[0] + s])
            branch = acc_s[r, :] + row(R_BU)
            r2 = h1_v[r, :] + branch
            normed, inv = norm(r2)
            out = normed * row(R_G1) + row(R_S1)
            t_normed, _ = norm(th1_v[r, :] + acc_t[r, :] + row(R_TBU))
            diff = keep * (out - (t_normed * row(R_TG1) + row(R_TS1)))
            d_out = cot_v[r, :].astype(f32) + diff
            dr2 = norm_back(d_out * row(R_G1), normed, inv)
            lo_o[r, :] = out.astype(bf16)
            dr2_o[r, :] = dr2
            dfr_o[r, :] = dr2.astype(bf16)
            parts = (
                d_out * normed, d_out, dr2, diff * diff, keep * r2 * r2, keep * branch * branch,
            )
            total = [t + colsum(p) for t, p in zip(total, parts)]
        for n in range(6):
            sum_o[n : n + 1, :] = total[n]
        sum_o[6:8, :] = jnp.zeros((2, D), f32)


def half_col(half, width, base=0):
    lo = half * NCH
    return pl.BlockSpec((width, CH_W), lambda c, *_: (0, base + jnp.clip(c - lo, 0, NCH - 1)))


def half_row(half):
    lo = half * NCH
    return pl.BlockSpec((CH_W, D), lambda c, *_: (jnp.clip(c - lo, 0, NCH - 1), 0))


def feed_forward(lens, h1, mid, th1, tmid, cot, wi, wu, ti, tu, v_a, v_b, rep):
    rows = h1.shape[0]
    full = whole((rows, D))
    anywhere = pl.BlockSpec(memory_space=pl.ANY)
    chunk_out = pl.BlockSpec((rows, CH_W), lambda c, *_: (0, c))
    return pl.pallas_call(
        ff_kernel,
        grid_spec=pltpu.PrefetchScalarGridSpec(
            num_scalar_prefetch=2,
            grid=(2 * NCH,),
            in_specs=[
                anywhere, full, anywhere, full, anywhere,
                half_col(0, D), half_col(1, D), half_row(0), half_row(1),
                half_col(0, D), half_col(1, D), half_row(0), half_row(1),
                half_col(0, 1, BI // CH_W), half_col(1, 1, BI // CH_W),
                half_col(0, 1, CHD // CH_W), half_col(1, 1, CHD // CH_W),
                half_col(0, 1, TI // CH_W), half_col(1, 1, TI // CH_W),
                whole((14, D)),
            ],
            out_specs=[chunk_out, chunk_out, chunk_out, full, full, full, whole((8, D))],
            scratch_shapes=[
                pltpu.VMEM((rows, D), f32),
                pltpu.VMEM((rows, D), f32),
                pltpu.VMEM((rows, D), f32),
                pltpu.VMEM((rows, D), f32),
                pltpu.VMEM((rows, D), bf16),
                pltpu.SemaphoreType.DMA((3,)),
            ],
        ),
        out_shape=[
            SDS((rows, FF), bf16),
            SDS((rows, FF), bf16),
            SDS((rows, FF), bf16),
            SDS((rows, D), bf16),
            SDS((rows, D), f32),
            SDS((rows, D), bf16),
            SDS((8, D), f32),
        ],
        compiler_params=params(42),
        name="feed_forward",
        cost_estimate=cost(45),
    )(
        *lens, h1, mid, th1, tmid, cot, wi[0], wi[1], wu[0], wu[1], ti[0], ti[1], tu[0], tu[1],
        v_a, v_b, v_a, v_b, v_a, v_b, rep,
    )


def fold(place, kind, own, got, high, low):
    n = high.shape[1]
    for r in range(BLOCKS):
        at = pl.ds(pl.multiple_of(place[kind * BLOCKS + r] * n, 16), n)
        value = (own[at, :] + got[at, :].astype(f32)).astype(bf16)
        if r >= BLOCKS // 2:
            high[r - BLOCKS // 2] = value
        else:
            low[r] = value


def fold_shapes(rows, cols):
    return [SDS((BLOCKS // 2, rows // BLOCKS, cols), bf16)] * 2


def outer_grad_kernel(place, dfr, ain, *refs):
    c = pl.program_id(0)
    part = dot(ain[...], dfr[...], TN)
    if len(refs) == 1:
        refs[0][...] = part.astype(bf16)
    else:
        got, high, low, acc = refs
        acc[pl.ds(pl.multiple_of(c * CH_W, CH_W), CH_W), :] = part

        @pl.when(c == NCH - 1)
        def _():
            fold(place, OUTER, acc, got, high, low)


def outer_grad(half, place, dfr, ain, got=None):
    rows = dfr.shape[0]
    in_specs = [
        whole((rows, D)), pl.BlockSpec((rows, CH_W), lambda c, *_: (0, half * NCH + c))
    ]
    if got is None:
        extra, scratch = [], []
        out_shape = SDS((FH, D), bf16)
        out_specs = pl.BlockSpec((CH_W, D), lambda c, *_: (c, 0))
    else:
        extra, scratch = [got], [pltpu.VMEM((FH, D), f32)]
        in_specs.append(whole((FH, D)))
        out_shape = fold_shapes(FH, D)
        out_specs = [whole(v.shape) for v in out_shape]
    return pl.pallas_call(
        outer_grad_kernel,
        grid_spec=pltpu.PrefetchScalarGridSpec(
            num_scalar_prefetch=1,
            grid=(NCH,),
            in_specs=in_specs,
            out_specs=out_specs,
            scratch_shapes=scratch,
        ),
        out_shape=out_shape,
        compiler_params=params(24),
        name="outer_grad",
        cost_estimate=cost(6),
    )(place, dfr, ain, *extra)


def ff_back_kernel(place, dfr, mid, mul, cv, wi, wu, *refs, first):
    if first:
        gi_o, sum_o, dh_o, mid_t = refs
    else:
        before, got, high, low, sum_o, dh_o, mid_t, acc = refs
    c = pl.program_id(0)

    @pl.when(c == 0)
    def _():
        mid_t[...] = mid[...].T
        dh_o[...] = jnp.zeros_like(dh_o) if first else before[...]

    d_ain = dot(dfr[...], wu[...], NT)
    sum_o[1:2, :] = colsum(d_ain * cv[...].astype(f32))
    d_inner = d_ain * mul[...].astype(f32)
    sum_o[0:1, :] = colsum(d_inner)
    sum_o[2:8, :] = jnp.zeros((6, CH_W), f32)
    dir_low = d_inner.astype(bf16)
    part = dot(mid_t[...], dir_low)
    if first:
        gi_o[...] = part.astype(bf16)
    else:
        acc[...] = part
        fold(place, INNER, acc, got, high, low)
    dh_o[...] += dot(dir_low, wi[...], NT)


def ff_back(half, place, dfr, mid, mul, cv, wi, wu, before=None, got=None):
    rows = dfr.shape[0]
    first = before is None
    full = whole((rows, D))
    chunk = pl.BlockSpec((rows, CH_W), lambda c, *_: (0, half * NCH + c))
    col = pl.BlockSpec((D, CH_W), lambda c, *_: (0, c))
    row = pl.BlockSpec((CH_W, D), lambda c, *_: (c, 0))
    in_specs = [full, full, chunk, chunk, col, row]
    scratch = [pltpu.VMEM((D, rows), bf16)]
    if first:
        extra, grad_shape, grad_specs = [], [SDS((D, FH), bf16)], [col]
    else:
        extra, grad_shape = [before, got], fold_shapes(D, FH)
        in_specs += [full, col]
        piece = grad_shape[0].shape
        grad_specs = [pl.BlockSpec(piece[:2] + (CH_W,), lambda c, *_: (0, 0, c))] * 2
        scratch.append(pltpu.VMEM((D, CH_W), f32))
    return pl.pallas_call(
        partial(ff_back_kernel, first=first),
        grid_spec=pltpu.PrefetchScalarGridSpec(
            num_scalar_prefetch=1,
            grid=(NCH,),
            in_specs=in_specs,
            out_specs=grad_specs + [pl.BlockSpec((8, CH_W), lambda c, *_: (0, c)), full],
            scratch_shapes=scratch,
        ),
        out_shape=grad_shape + [SDS((8, FH), f32), SDS((rows, D), f32)],
        compiler_params=params(32),
        name="ff_back",
        cost_estimate=cost(14),
    )(place, dfr, mid, mul, cv, wi, wu, *extra)


def mid_back_kernel(
    r1, dr2, dhin, ctx, wo_a, wo_b, v_a, v_b, rep, dr1_o, dcr_o, go_a, go_b, sum_o, wo, acc
):
    i = pl.program_id(0)

    @pl.when(i == 0)
    def _():
        wo[:DH, :] = wo_a[...]
        wo[DH:, :] = wo_b[...]
        acc[...] = jnp.zeros_like(acc)
        sum_o[...] = jnp.zeros_like(sum_o)

    row = lambda n: rep[n : n + 1, :]
    normed, inv = norm(r1[...])
    cm = row(R_CM)
    ratio = (normed * row(R_G0) + row(R_S0)) * (1.0 / cm)
    th = jnp.tanh(ratio)
    slope = 1.0 - th * th
    d_hin = dhin[...]
    sum_o[3:4, :] += colsum(d_hin * (th - ratio * slope))
    dh1 = dr2[...] + d_hin * slope
    sum_o[0:1, :] += colsum(dh1 * normed)
    sum_o[1:2, :] += colsum(dh1)
    dr1 = norm_back(dh1 * row(R_G0), normed, inv)
    sum_o[2:3, :] += colsum(dr1)
    dr1_o[...] = dr1
    dar = dr1.astype(bf16)
    clip = jnp.concatenate([v_a[:, CC : CC + DH], v_b[:, CC : CC + DH]], 1)
    ratio = ctx[...] * (1.0 / clip)
    th = jnp.tanh(ratio)
    slope = 1.0 - th * th
    acc[...] += dot(dar, (clip * th).astype(bf16), TN)
    d_cin = dot(dar, wo[...], NT)
    sum_o[4:5, :] += colsum(d_cin * (th - ratio * slope))
    dcr_o[...] = (d_cin * slope).astype(bf16)

    @pl.when(i == pl.num_programs(0) - 1)
    def _():
        go_a[...] = acc[:, :DH].astype(bf16)
        go_b[...] = acc[:, DH:].astype(bf16)


def mid_back(r1, dr2, dhin, ctx, wo_a, wo_b, v_a, v_b, rep):
    rows = r1.shape[0]
    block = pl.BlockSpec((RB, D), lambda i: (i, 0))
    return pl.pallas_call(
        mid_back_kernel,
        grid=(rows // RB,),
        in_specs=[block] * 4
        + [whole((DH, D)), whole((DH, D)), whole((1, VEND)), whole((1, VEND)), whole((14, D))],
        out_specs=[block, block, whole((D, DH)), whole((D, DH)), whole((8, D))],
        out_shape=[
            SDS((rows, D), f32),
            SDS((rows, D), bf16),
            SDS((D, DH), bf16),
            SDS((D, DH), bf16),
            SDS((8, D), f32),
        ],
        scratch_shapes=[pltpu.VMEM((D, D), bf16), pltpu.VMEM((D, D), f32)],
        compiler_params=params(20),
        name="mid_back",
        cost_estimate=cost(12),
    )(r1, dr2, dhin, ctx, wo_a, wo_b, v_a, v_b, rep)


LEAD, REST = 128, 256


def attn_back_kernel(
    lens, first, place, qkv, dc, ctx, lse, xt, *refs, pairs, kind, with_out, folded
):
    refs = list(refs)
    got_out = refs.pop(0) if with_out else None
    got = refs.pop(0) if folded else None
    d_o, *grads = refs[: 3 if folded else 2]
    sum_o, acc = refs[-2:]
    seq = pl.program_id(0)
    length = lens[first[0] + seq]
    width = 128 * len(pairs)
    lo = pairs[0] * 128
    pick = lax.broadcasted_iota(jnp.int32, (8, width), 1) // HD
    pick = (pick == lax.broadcasted_iota(jnp.int32, (8, width), 0)).astype(f32)
    cols = slice(lo, lo + width)
    deltas = lax.dot_general(
        pick, dc[:, cols].astype(f32) * ctx[:, cols], NT, precision=lax.Precision.HIGHEST,
        preferred_element_type=f32,
    )
    heads = [(n, h) for n in range(len(pairs)) for h in range(2)]

    def part_of(n, k):
        at = pairs[n] * 128 + k * DH
        return qkv[:, at : at + 128]

    def dc_of(n):
        return dc[:, pairs[n] * 128 : (pairs[n] + 1) * 128]

    def score(n, h):
        q_h, k_h = with_mask(part_of(n, 0), part_of(n, 1), length, h)
        return dot(k_h, q_h, NT), dot(pair_of(part_of(n, 2), h), dc_of(n), NT)

    @pl.when(seq == 0)
    def _():
        sum_o[...] = jnp.zeros_like(sum_o)

    scores = [score(*heads[0])]
    for i, (n, h) in enumerate(heads):
        if i + 1 < len(heads):
            scores.append(score(*heads[i + 1]))
        s, dp = scores[i]
        row = 2 * pairs[n] + h
        prob = jnp.exp(s - lse[0, row : row + 1, :])
        row = 2 * n + h
        ds = (prob * (dp - deltas[row : row + 1, :])).astype(bf16)
        if h == 0:
            k_t = part_of(n, 1).T
        part_q = dot(k_t[h * HD : (h + 1) * HD], ds)
        part_k = dot(ds, pair_of(part_of(n, 0), h))
        part_v = dot(prob.astype(bf16), pair_of(dc_of(n), h))
        if h == 0:
            d_q, d_k, d_v = part_q, part_k, part_v
        else:
            d_q = jnp.concatenate([d_q, part_q], 0).T * HD**-0.5
            d_v = d_v + part_v
            for k, d in enumerate((d_q, d_k + part_k, d_v)):
                at = k * width + n * 128
                d_o[:, at : at + 128] = d.astype(bf16)
            cols = slice(n * 128, (n + 1) * 128)
            sum_o[0:1, cols] += colsum(d_q)
            sum_o[1:2, cols] += colsum(d_v)
    part = dot(xt[...], d_o[...])
    n = 3 * width

    @pl.when(seq == 0)
    def _():
        acc[:, :n] = part
        if with_out:
            acc[:, n:] = got_out[...].astype(f32)

    @pl.when(seq > 0)
    def _():
        acc[:, :n] += part

    @pl.when(seq == pl.num_programs(0) - 1)
    def _():
        if folded:
            fold(place, kind, acc, got, *grads)
        else:
            grads[0][...] = acc[...].astype(bf16)


def attention_back(half, kind, lens, place, qkv, dcr, ctx, lse, x_t, out_grad=None, got=None):
    rows = qkv.shape[0]
    nseq = rows // SEQ
    pairs = (0,) if kind == FIRST else (1, 2)
    width = 128 * len(pairs)
    block = lambda n: pl.BlockSpec((SEQ, n), lambda s, *_: (s, half))
    in_specs = [
        block(QW),
        block(DH),
        block(DH),
        pl.BlockSpec((1, 8, SEQ), lambda s, *_: (2 * s + half, 0, 0)),
        pl.BlockSpec((D, SEQ), lambda s, *_: (0, s)),
    ]
    extra = [v for v in (out_grad, got) if v is not None]
    grad_shape = [SDS((D, D), bf16)] if got is None else fold_shapes(D, D)
    return pl.pallas_call(
        partial(
            attn_back_kernel,
            pairs=pairs, kind=kind, with_out=out_grad is not None, folded=got is not None,
        ),
        grid_spec=pltpu.PrefetchScalarGridSpec(
            num_scalar_prefetch=3,
            grid=(nseq,),
            in_specs=in_specs + [whole(v.shape) for v in extra],
            out_specs=[pl.BlockSpec((SEQ, 3 * width), lambda s, *_: (s, 0))]
            + [whole(v.shape) for v in grad_shape]
            + [whole((8, width))],
            scratch_shapes=[pltpu.VMEM((D, D), f32)],
        ),
        out_shape=[SDS((rows, 3 * width), bf16)] + grad_shape + [SDS((8, width), f32)],
        compiler_params=params(20),
        name="attention_back",
        cost_estimate=cost(6 * len(pairs)),
    )(*lens, place, qkv, dcr, ctx, lse, x_t, *extra)


def clip_in(x, rep):
    clip = rep[R_CI : R_CI + 1, :]
    ratio = x[...].astype(f32) * (1.0 / clip)
    return ratio, jnp.tanh(ratio)


def x_back_kernel(x, d_la, d_lb, d_a, d_b, dr1, w_a, w_b, rep, grad_o, sum_o, w_lead, w_rest):
    @pl.when(pl.program_id(0) == 0)
    def _():
        sum_o[...] = jnp.zeros_like(sum_o)
        for half, w in enumerate((w_a, w_b)):
            for k in range(3):
                at = half * DH + k * LEAD
                w_lead[:, at : at + LEAD] = w[:, k * DH : k * DH + LEAD]
                at = half * D + k * REST
                w_rest[:, at : at + REST] = w[:, k * DH + LEAD : (k + 1) * DH]

    total = (
        dot(jnp.concatenate([d_la[...], d_lb[...]], 1), w_lead[...], NT)
        + dot(d_a[...], w_rest[:, :D], NT)
        + dot(d_b[...], w_rest[:, D:], NT)
    )
    ratio, th = clip_in(x, rep)
    slope = 1.0 - th * th
    grad_o[...] = dr1[...] + total * slope
    sum_o[0:1, :] += colsum(total * (th - ratio * slope))


RB = 256


def x_back(x, d_la, d_lb, d_a, d_b, dr1, w_a, w_b, rep):
    rows = x.shape[0]
    block = pl.BlockSpec((RB, D), lambda i: (i, 0))
    narrow = pl.BlockSpec((RB, DH), lambda i: (i, 0))
    return pl.pallas_call(
        x_back_kernel,
        grid=(rows // RB,),
        in_specs=[block, narrow, narrow, block, block, block] + [whole((D, QW)), whole((D, QW)), whole((14, D))],
        out_specs=[block, whole((8, D))],
        out_shape=[SDS((rows, D), f32), SDS((8, D), f32)],
        scratch_shapes=[pltpu.VMEM((D, D), bf16), pltpu.VMEM((D, 2 * D), bf16)],
        compiler_params=params(20),
        name="x_back",
        cost_estimate=cost(8),
    )(x, d_la, d_lb, d_a, d_b, dr1, w_a, w_b, rep)


def pack_kernel(ha, hb, la, lb, qa, qb, m, f, a, x, out):
    for side, (h, l, q) in enumerate(((ha, la, qa), (hb, lb, qb))):
        base = 6 * side
        for n in range(2):
            out[base + 2 * n : base + 2 * n + 1, :] = h[n : n + 1, :D]
            out[base + 2 * n + 1 : base + 2 * n + 2, :] = h[n : n + 1, D:]
        for k in range(2):
            at = k * DH
            out[base + 4 : base + 5, at : at + LEAD] = l[k : k + 1, :]
            out[base + 4 : base + 5, at + LEAD : at + DH] = q[k : k + 1, :]
        out[base + 5 : base + 6, :DH] = m[4:5, side * DH : (side + 1) * DH]
        out[base + 5 : base + 6, DH:] = jnp.zeros((1, DH), f32)
    rows = (
        (m, 2), (f, 2), (m, 0), (f, 0), (m, 1), (f, 1), (x, 0), (m, 3),
        (f, 3), (f, 4), (a, 0), (f, 5),
    )
    for n, (ref, k) in enumerate(rows):
        out[12 + n : 13 + n, :] = ref[k : k + 1, :]


def pack(*sums):
    return pl.pallas_call(
        pack_kernel,
        grid=(1,),
        in_specs=[whole(v.shape) for v in sums],
        out_specs=whole((24, D)),
        out_shape=SDS((24, D), f32),
        compiler_params=params(4),
        name="pack",
        cost_estimate=cost(1),
    )(*sums)


BLOCKS = 16
OUTER, INNER, FIRST, LAST = range(4)
ORDERS = (
    ((1, 2, 4, 8), (2, 4, 1, 8)),
    ((4, 1, 2, 8), (1, 4, 2, 8)),
    ((1, 2, 4, 8), (2, 1, 4, 8)),
    ((1, 2, 4, 8), (2, 1, 4, 8)),
)


def spread(order, r):
    return sum(mask for p, mask in enumerate(order) if r & (BLOCKS >> (p + 1)))


def place_table(me, core):
    rows = []
    for pair in ORDERS:
        a, b = [jnp.asarray([spread(o, r) for r in range(BLOCKS)], jnp.int32) for o in pair]
        rows.append(jnp.where(core == 0, a, b) ^ me)
    return jnp.concatenate(rows)


def swap(value, masks, n_dp):
    pairs = [(2 * i + t, 2 * (i ^ masks[t]) + t) for i in range(n_dp) for t in range(2)]
    return lax.ppermute(value, ("dp", "tensor"), pairs)


class Sum:
    def __init__(self, pieces, kind, n_dp):
        self.kind, self.n_dp = kind, n_dp
        self.send, self.hold = pieces
        self.step = 0
        self.recv = self.swap(0)

    def swap(self, step):
        return swap(self.send, tuple(order[step] for order in ORDERS[self.kind]), self.n_dp)

    def advance(self, *done):
        self.recv, *done = lax.optimization_barrier((self.recv, *done))
        self.step += 1
        half = self.hold.shape[0] // 2
        if self.step <= 3:
            self.send = self.hold[half:] + self.recv[half:]
            self.hold = self.hold[:half] + self.recv[:half]
            self.recv = self.swap(self.step)
        elif self.step == 4:
            self.send = self.hold + self.recv
            mask = BLOCKS
            while mask < self.n_dp:
                self.send = self.send + swap(self.send, (mask, mask), self.n_dp)
                mask *= 2
            self.recv = self.swap(3)
        elif self.step <= 7:
            self.send = jnp.concatenate([self.send, self.recv], 0)
            self.recv = self.swap(7 - self.step)
        return done

    def result(self):
        assert self.step == 7
        return (self.send, self.recv)


class Small(Sum):
    def __init__(self, value, n_dp):
        self.n_dp = n_dp
        self.mask, self.send = 1, value
        self.recv = swap(value, (1, 1), n_dp)

    def advance(self, *done):
        self.recv, *done = lax.optimization_barrier((self.recv, *done))
        self.send = self.send + self.recv
        self.mask *= 2
        if self.mask < self.n_dp:
            self.recv = swap(self.send, (self.mask, self.mask), self.n_dp)
        return done

    def result(self):
        while self.mask < self.n_dp:
            self.advance()
        return self.send


def step(streams, *values):
    for stream in streams:
        values = stream.advance(*values)
    return behind(streams, *values)


def behind(streams, *values):
    sent = [s.send for s in streams]
    return lax.optimization_barrier((*sent, *values))[len(sent) :]


def latent(w, g, axis, factor):
    th = jnp.tanh(2.0 * w)
    n = w.shape[axis]
    mean = jnp.sum(jnp.abs(w), axis, keepdims=True) * (1.0 / n)
    inner = jnp.sum(g * th, axis, keepdims=True) * (1.0 / n)
    sign = jnp.where(w > 0, 1.0, jnp.where(w < 0, -1.0, 0.0))
    return factor * (2.0 * mean * (1.0 - th * th) * g + sign * inner)


def collect(place, mine, recv, kind, target):
    n = mine.shape[1]
    for r in range(BLOCKS):
        at = pl.multiple_of(place[kind * BLOCKS + r] * n, 16)
        target[pl.ds(at, n), :] = (mine if r < BLOCKS // 2 else recv)[r % 8]


def latent_kernel(place, mine, recv, w, out, g, *, kind):
    i = pl.program_id(0)

    @pl.when(i == 0)
    def _():
        collect(place, mine, recv, kind, g)

    n = FH // 4
    at = pl.ds(pl.multiple_of(i * n, 128), n)
    if kind == OUTER:
        out[...] = latent(w[...], g[at, :].astype(f32), 1, 1.0 / math.sqrt(FF))
    else:
        out[...] = latent(w[...], g[:, at].astype(f32), 0, 1.0 / math.sqrt(D))


def ffn_latent(kind, place, pieces, w):
    if kind == OUTER:
        block = pl.BlockSpec((FH // 4, D), lambda i, *_: (i, 0))
    else:
        block = pl.BlockSpec((D, FH // 4), lambda i, *_: (0, i))
    return pl.pallas_call(
        partial(latent_kernel, kind=kind),
        grid_spec=pltpu.PrefetchScalarGridSpec(
            num_scalar_prefetch=1,
            grid=(4,),
            in_specs=[whole(p.shape) for p in pieces] + [block],
            out_specs=block,
            scratch_shapes=[pltpu.VMEM(w.shape, bf16)],
        ),
        out_shape=SDS(w.shape, f32),
        compiler_params=params(16),
        name="ffn_latent",
        cost_estimate=cost(8),
    )(place, *pieces, w)


def attn_latent_kernel(place, *refs):
    pieces, w_in, wo, outs, go, g, h = refs[:4], refs[4:7], refs[7], refs[8:11], *refs[11:]
    root = 1.0 / math.sqrt(D)
    collect(place, *pieces[:2], FIRST, g)
    collect(place, *pieces[2:], LAST, h)
    for c in range(3):
        for src, at, n in ((g, 0, LEAD), (h, LEAD, REST)):
            grad = src[:, c * n : (c + 1) * n].astype(f32)
            cols = slice(at, at + n)
            outs[c][:, cols] = latent(w_in[c][:, cols], grad, 0, root if c == 2 else 2.0 * root)
    go[...] = latent(wo[...], g[:, DH:].astype(f32).T, 1, 8.0 * root)


def attn_latent(place, pieces, wq, wk, wv, wo):
    col, row = whole((D, DH)), whole((DH, D))
    return pl.pallas_call(
        attn_latent_kernel,
        grid_spec=pltpu.PrefetchScalarGridSpec(
            num_scalar_prefetch=1,
            grid=(1,),
            in_specs=[whole(p.shape) for p in pieces] + [col, col, col, row],
            out_specs=[col, col, col, row],
            scratch_shapes=[pltpu.VMEM((D, D), bf16)] * 2,
        ),
        out_shape=[SDS((D, DH), f32)] * 3 + [SDS((DH, D), f32)],
        compiler_params=params(24),
        name="attn_latent",
        cost_estimate=cost(9),
    )(place, *pieces, wq, wk, wv, wo)


def on_device(
    n_dp,
    tokens, cotangent, lengths, w_query, w_key, w_value, w_output, w_inner, w_outer,
    b_query, b_value, b_output, b_inner, b_outer, ln_gains, ln_shifts,
    clip_input, clip_context, clip_middle, clip_hidden,
    t_query, t_key, t_value, t_output, t_inner, t_outer,
    tb_query, tb_value, tb_output, tb_inner, tb_outer, t_gains, t_shifts,
):
    other = lambda value: lax.ppermute(value, "tensor", [(0, 1), (1, 0)])
    rows = tokens.shape[0]
    nseq = rows // SEQ
    core = lax.axis_index("tensor")
    place = place_table(lax.axis_index("dp").astype(jnp.int32), core)
    lens = (lengths, (core * nseq).astype(jnp.int32).reshape(1))

    t_own = (t_query, t_key, t_value)
    t_other = tuple(other(w) for w in t_own)
    t_out_b = other(t_output)
    wqkv, wo, wi, wu, v_a, rep = prep(
        (w_query, w_key, w_value, w_output, w_inner, w_outer),
        (b_inner, clip_hidden, tb_inner, b_query, b_value, clip_context, tb_query, tb_value),
        (
            b_output, b_outer, ln_gains, ln_shifts, clip_input, clip_middle,
            tb_output, tb_outer, t_gains, t_shifts,
        ),
    )
    v_a, *t_other, t_out_b = lax.optimization_barrier((v_a, *t_other, t_out_b))
    t_other = tuple(t_other)
    v_b = other(v_a)
    wqkv_b, wo_b = other(wqkv), other(wo)
    th1, tmid = encode(lens, tokens, t_own + t_other, t_output, t_out_b, v_a, v_b, rep, False)
    late = lax.optimization_barrier((v_b, t_inner, t_outer, wi, wu))[1:]
    ti_b, tu_b, wi_b, wu_b = [other(w) for w in late]
    qkv, ctx, lse, r1, h1, mid, x_t, sum_a = encode(
        lens, tokens, (wqkv, wqkv_b), wo, wo_b, v_a, v_b, rep, True
    )
    ain, mul, cv, layer_out, dr2, dfr, sum_f = feed_forward(
        lens, h1, mid, th1, tmid, cotangent, (wi, wi_b), (wu, wu_b), (t_inner, ti_b),
        (t_outer, tu_b), v_a, v_b, rep,
    )
    gu_b = outer_grad(1, place, dfr, ain)
    outer = Sum(outer_grad(0, place, dfr, ain, other(gu_b)), OUTER, n_dp)
    dfr, mid, mul, cv = behind([outer], dfr, mid, mul, cv)
    gi_b, sum_hb, dh_b = ff_back(1, place, dfr, mid, mul, cv, wi_b, wu_b)
    dh_b, gi_b = outer.advance(dh_b, gi_b)
    gi_c = other(gi_b)
    (dh_b,) = behind([outer], dh_b)
    *gi, sum_ha, dhin = ff_back(0, place, dfr, mid, mul, cv, wi, wu, dh_b, gi_c)
    (dhin,) = outer.advance(dhin)
    inner = Sum(gi, INNER, n_dp)
    (dhin,) = behind([outer, inner], dhin)
    dr1, dcr, go_a, go_b, sum_m = mid_back(r1, dr2, dhin, ctx, wo, wo_b, v_a, v_b, rep)
    (dcr,) = step([outer, inner], dcr)
    saved = (qkv, dcr, ctx, lse, x_t)
    d_lb, gl_b, sum_lb = attention_back(1, FIRST, lens, place, *saved, go_b)
    gl_c = other(gl_b)
    dcr, _ = step([inner], dcr, gl_b)
    saved = (qkv, dcr, ctx, lse, x_t)
    d_b, gs_b, sum_b = attention_back(1, LAST, lens, place, *saved)
    gs_c = other(gs_b)
    gl_c, dcr, _ = step([outer, inner], gl_c, dcr, gs_b)
    saved = (qkv, dcr, ctx, lse, x_t)
    d_la, *gl, sum_la = attention_back(0, FIRST, lens, place, *saved, go_a, gl_c)
    lead = Sum(gl, FIRST, n_dp)
    gs_c, dcr, _ = step([outer, inner], gs_c, dcr, d_la)
    gs_c, dcr = behind([lead], gs_c, dcr)
    saved = (qkv, dcr, ctx, lse, x_t)
    d_a, *gs, sum_q = attention_back(0, LAST, lens, place, *saved, None, gs_c)
    last = Sum(gs, LAST, n_dp)
    dr1, _ = step([lead, outer, inner], dr1, d_a)
    (dr1,) = behind([last], dr1)
    grad_tokens, sum_x = x_back(tokens, d_la, d_lb, d_a, d_b, dr1, wqkv, wqkv_b, rep)
    sums = pack(sum_ha, sum_hb, sum_la, sum_lb, sum_q, sum_b, sum_m, sum_f, sum_a, sum_x)
    from_other = other(sums[6:])
    (sums,) = last.advance(sums)
    lead.advance(last.send)
    small = Small(jnp.concatenate([sums[:6], sums[12:]], 0) + from_other, n_dp)
    outer.advance(lead.send)
    inner.advance(lead.send)
    for _ in range(3):
        last.advance()
        lead.advance(last.send)
        small.advance(lead.send)
    last.advance()
    lead.advance(last.send)
    small.advance(lead.send)
    (w_o,) = behind([last, lead], w_outer)
    g_outer = ffn_latent(OUTER, place, outer.result(), w_o)
    inner.advance(g_outer)
    last.advance()
    lead.advance(last.send)
    last.advance()
    (w_i,) = behind([last], w_inner)
    (small.recv,) = behind([last], small.recv)
    small = small.result()
    g_inner = ffn_latent(INNER, place, inner.result(), w_i)
    last.recv, g_inner = lax.optimization_barrier((last.recv, g_inner))
    g_query, g_key, g_value, g_output = attn_latent(
        place, lead.result() + last.result(), w_query, w_key, w_value, w_output
    )
    split, shared = small[:6], small[6:]
    count = jnp.asarray(rows * 2 * n_dp * D, f32)
    stats = jnp.sum(shared[8:], 1) / count
    summary = jnp.concatenate([stats[:1], jnp.sqrt(stats[1:])])
    return (
        layer_out,
        grad_tokens,
        g_query,
        g_key,
        g_value,
        g_output,
        g_inner,
        g_outer,
        split[4, :DH],
        split[4, DH:],
        shared[0],
        split[0:2].reshape(FH),
        shared[1],
        shared[2:4],
        shared[4:6],
        shared[6],
        split[5, :DH],
        shared[7],
        split[2:4].reshape(FH),
        summary,
    )


def solution(mesh):
    rows, cols, split, full = P(("dp", "tensor"), None), P(None, "tensor"), P("tensor"), P()
    down = P("tensor", None)
    return jax.shard_map(
        partial(on_device, mesh.shape["dp"]),
        mesh=mesh,
        in_specs=(
            rows, rows, P("dp"), cols, cols, cols, down, cols, down,
            split, split, full, split, full, full, full,
            full, split, full, split,
            cols, cols, cols, down, cols, down,
            split, split, full, split, full, full, full,
        ),
        out_specs=(
            rows, rows, cols, cols, cols, down, cols, down,
            split, split, full, split, full, full, full, full, split, full, split, full,
        ),
        check_vma=False,
    )
```

```python
from functools import partial
import math

import jax
import jax.numpy as jnp
from jax import lax
import jax.experimental.pallas as pl
import jax.experimental.pallas.tpu as pltpu
from jax.sharding import PartitionSpec as P

D = 768
FF = 3072
SEQ = 512
HD = 64
DH = D // 2
FH = FF // 2
QW = 3 * DH

CH_W = 512
NCH = FH // CH_W
EPS = 1e-12

BI, CHD, TI, BQ, BV, CC, TQ, TV, VEND = 0, 1536, 3072, 4608, 4992, 5376, 5760, 6144, 6528
R_BO, R_BU, R_G0, R_G1, R_S0, R_S1, R_CI, R_CM, R_TBO, R_TBU, R_TG0, R_TG1, R_TS0, R_TS1 = range(14)

f32 = jnp.float32
bf16 = jnp.bfloat16
NT = (((1,), (1,)), ((), ()))
NN = (((1,), (0,)), ((), ()))
TN = (((0,), (0,)), ((), ()))
SDS = jax.ShapeDtypeStruct


def dot(left, right, dims=NN):
    return lax.dot_general(left, right, dims, preferred_element_type=f32)


def params(mib):
    return pltpu.CompilerParams(vmem_limit_bytes=mib * 2**20)


def cost(micros):
    return pl.CostEstimate(
        flops=micros * 10**9, transcendentals=0, bytes_accessed=micros * 3 * 10**6
    )


def whole(shape):
    rank = len(shape)
    return pl.BlockSpec(shape, lambda *_: (0,) * rank, pipeline_mode=pl.Buffered(1))


def norm(resid):
    centered = resid - jnp.mean(resid, -1, keepdims=True)
    inv = lax.rsqrt(jnp.mean(centered * centered, -1, keepdims=True) + EPS)
    return centered * inv, inv


def colsum(value):
    return jnp.sum(value, 0, keepdims=True)


def norm_back(e, normed, inv):
    return inv * (
        e - jnp.mean(e, -1, keepdims=True) - normed * jnp.mean(e * normed, -1, keepdims=True)
    )


def keep_rows(length):
    return (lax.broadcasted_iota(jnp.int32, (SEQ, 1), 0) < length).astype(f32)


def bin_cols(w, factor):
    return (jnp.mean(jnp.abs(w), 0, keepdims=True) * jnp.tanh(2.0 * w) * factor).astype(bf16)


def bin_rows(w, factor):
    return (jnp.mean(jnp.abs(w), 1, keepdims=True) * jnp.tanh(2.0 * w) * factor).astype(bf16)


SPLIT = (FH, FH, FH, DH, DH, DH, DH, DH)


def prep_kernel(*refs):
    wq, wk, wv, wo, wi, wu = refs[:6]
    split = refs[6:14]
    full = refs[14:24]
    qkv_o, wo_o, wi_o, wu_o, vec_o, rep_o = refs[24:]
    i = pl.program_id(0)
    root = 1.0 / math.sqrt(D)
    wi_o[...] = bin_cols(wi[...], root)
    wu_o[...] = bin_rows(wu[...], 1.0 / math.sqrt(FF))

    @pl.when(i == 0)
    def _():
        qkv_o[:, :DH] = bin_cols(wq[...], 2.0 * root)
        at = 0
        for ref, n in zip(split, SPLIT):
            vec_o[0, at : at + n] = ref[...]
            at += n
        at = 0
        for ref in full:
            if len(ref.shape) == 1:
                rep_o[at, :] = ref[...]
                at += 1
            else:
                rep_o[at : at + 2, :] = ref[...]
                at += 2

    @pl.when(i == 1)
    def _():
        qkv_o[:, DH : 2 * DH] = bin_cols(wk[...], 2.0 * root)

    @pl.when(i == 2)
    def _():
        qkv_o[:, 2 * DH :] = bin_cols(wv[...], root)

    @pl.when(i == 3)
    def _():
        wo_o[...] = bin_rows(wo[...], 8.0 * root)


def prep(weights, split, full):
    n = 4
    col = pl.BlockSpec((D, FH // n), lambda i: (0, i))
    row = pl.BlockSpec((FH // n, D), lambda i: (i, 0))
    return pl.pallas_call(
        prep_kernel,
        grid=(n,),
        in_specs=[whole((D, DH))] * 3
        + [whole((DH, D)), col, row]
        + [whole(v.shape) for v in (*split, *full)],
        out_specs=[
            whole((D, QW)), whole((DH, D)), col, row, whole((1, VEND)), whole((14, D)),
        ],
        out_shape=[
            SDS((D, QW), bf16),
            SDS((DH, D), bf16),
            SDS((D, FH), bf16),
            SDS((FH, D), bf16),
            SDS((1, VEND), f32),
            SDS((14, D), f32),
        ],
        compiler_params=params(60),
        name="prep",
        cost_estimate=cost(8),
    )(*weights, *split, *full)


def head_lanes(h):
    return lax.broadcasted_iota(jnp.int32, (1, 128), 1) // HD == h


def pair_of(value, h):
    return jnp.where(head_lanes(h), value, jnp.zeros((), value.dtype))


def with_mask(qq, kk, length, h):
    lane = lax.broadcasted_iota(jnp.int32, (1, 128), 1)
    spare = lane == HD * (1 - h)
    valid = lax.broadcasted_iota(jnp.int32, (SEQ, 1), 0) < length
    bias = jnp.where(valid, 0.0, -1e9).astype(bf16)
    k_h = jnp.where(spare, bias, pair_of(kk, h))
    return jnp.where(spare, jnp.ones((), bf16), qq), k_h


def attend(length, qkv_half, store):
    heads = [(half, p, h) for half in range(2) for p in range(3) for h in range(2)]

    def score(half, p, h):
        ref, base = qkv_half(half)
        at = base + p * 128
        q_h, k_h = with_mask(ref[:, at : at + 128], ref[:, at + DH : at + DH + 128], length, h)
        return dot(k_h, q_h, NT)

    ones = jnp.ones((16, SEQ), bf16)
    scores = [score(*heads[0]), score(*heads[1])]
    pair = []
    for i, (half, p, h) in enumerate(heads):
        if i + 2 < len(heads):
            scores.append(score(*heads[i + 2]))
        s = scores[i]
        top = jnp.max(s, 0, keepdims=True)
        e = jnp.exp(s - top).astype(bf16)
        ref, base = qkv_half(half)
        if h == 0:
            at = base + 2 * DH + p * 128
            v_t = ref[:, at : at + 128].T
        part = dot(jnp.concatenate([v_t[h * HD : (h + 1) * HD], ones], 0), e)
        total = part[HD : HD + 1]
        pair.append(part[:HD] * (1.0 / total))
        store(half, p, h, pair, top, total)
        if h:
            pair = []


def encode_kernel(lens, first, x, *refs, student):
    n = 1 if student else 3
    weights, refs = refs[: 2 * n], refs[2 * n :]
    wo_a, wo_b, v_a, v_b, rep = refs[:5]
    if student:
        qkv, ctx, lse, r1_o, h1_o, mid_o, xt_o, sum_o, wo = refs[5:]
    else:
        h1_o, mid_o, wo, qkv, ctx, w_all = refs[5:]
    i = pl.program_id(0)

    @pl.when(i == 0)
    def _():
        wo[:DH, :] = wo_a[...]
        wo[DH:, :] = wo_b[...]
        if student:
            sum_o[...] = jnp.zeros_like(sum_o)
        else:
            for k in range(6):
                w_all[:, k * DH : (k + 1) * DH] = weights[k][...]

    row = lambda k: rep[k : k + 1, :]
    length = lens[first[0] + i]
    xx = x[...]
    mine = xx.astype(f32)
    if student:
        clip = row(R_CI)
        xx = (clip * jnp.tanh(mine * (1.0 / clip))).astype(bf16)
        xt_o[...] = xx.T
    off_q, off_v = (BQ, BV) if student else (TQ, TV)
    for half, v in enumerate((v_a, v_b)):
        base = half * QW
        res = dot(xx, weights[half][...] if student else w_all[:, base : base + QW])
        q = (res[:, :DH] + v[:, off_q : off_q + DH]).astype(bf16)
        qkv[:, base : base + DH] = q * jnp.asarray(HD**-0.5, bf16)
        qkv[:, base + DH : base + 2 * DH] = res[:, DH : 2 * DH].astype(bf16)
        qkv[:, base + 2 * DH : base + QW] = (
            res[:, 2 * DH :] + v[:, off_v : off_v + DH]
        ).astype(bf16)

    def store(half, p, h, pair, top, total):
        if h:
            at = half * DH + p * 128
            ctx[:, at : at + 128] = jnp.concatenate(pair, 0).T.astype(ctx.dtype)
        if student:
            lse[half, 2 * p + h : 2 * p + h + 1, :] = top + jnp.log(total)

    attend(length, lambda half: (qkv, half * QW), store)
    if student:
        clip = jnp.concatenate([v_a[:, CC : CC + DH], v_b[:, CC : CC + DH]], 1)
        cin = (clip * jnp.tanh(ctx[...] * (1.0 / clip))).astype(bf16)
        branch = dot(cin, wo[...]) + row(R_BO)
        r1 = mine + branch
        normed, _ = norm(r1)
        h1 = normed * row(R_G0) + row(R_S0)
        cm = row(R_CM)
        r1_o[...] = r1
        h1_o[...] = h1
        mid_o[...] = (cm * jnp.tanh(h1 * (1.0 / cm))).astype(bf16)
        sum_o[0:1, :] += colsum(keep_rows(length) * branch * branch)
    else:
        branch = dot(ctx[...], wo[...]) + row(R_TBO)
        normed, _ = norm(mine + branch)
        h1 = normed * row(R_TG0) + row(R_TS0)
        h1_o[...] = h1
        mid_o[...] = h1.astype(bf16)


def encode(lens, x, weights, wo_a, wo_b, v_a, v_b, rep, student):
    rows = x.shape[0]
    block = pl.BlockSpec((SEQ, D), lambda i, *_: (i, 0))
    wide = SDS((rows, D), f32)
    if student:
        out_specs = [
            pl.BlockSpec((SEQ, 2 * QW), lambda i, *_: (i, 0)),
            block,
            pl.BlockSpec((2, 8, SEQ), lambda i, *_: (i, 0, 0)),
            block,
            block,
            block,
            pl.BlockSpec((D, SEQ), lambda i, *_: (0, i)),
            pl.BlockSpec((8, D), lambda i, *_: (0, 0)),
        ]
        out_shape = [
            SDS((rows, 2 * QW), bf16), wide, SDS((rows // SEQ * 2, 8, SEQ), f32),
            wide, wide, SDS((rows, D), bf16), SDS((D, rows), bf16), SDS((8, D), f32),
        ]
        scratch = [pltpu.VMEM((D, D), bf16)]
    else:
        out_specs = [block, block]
        out_shape = [wide, SDS((rows, D), bf16)]
        scratch = [
            pltpu.VMEM((D, D), bf16),
            pltpu.VMEM((SEQ, 2 * QW), bf16),
            pltpu.VMEM((SEQ, D), bf16),
            pltpu.VMEM((D, 2 * QW), bf16),
        ]
    return pl.pallas_call(
        partial(encode_kernel, student=student),
        grid_spec=pltpu.PrefetchScalarGridSpec(
            num_scalar_prefetch=2,
            grid=(rows // SEQ,),
            in_specs=[block]
            + [whole(w.shape) for w in weights]
            + [whole((DH, D)), whole((DH, D))]
            + [whole((1, VEND)), whole((1, VEND)), whole((14, D))],
            out_specs=out_specs,
            scratch_shapes=scratch,
        ),
        out_shape=out_shape,
        compiler_params=params(44 if student else 60),
        name="encode",
        cost_estimate=cost(25),
    )(*lens, x, *weights, wo_a, wo_b, v_a, v_b, rep)


ROWS = 256


def ff_kernel(
    lens, first, h1, mid, th1, tmid, cot, wi_a, wi_b, wu_a, wu_b, ti_a, ti_b, tu_a, tu_b,
    bi_a, bi_b, ch_a, ch_b, tb_a, tb_b, rep,
    ain_o, mul_o, cv_o, lo_o, dr2_o, dfr_o, sum_o, acc_s, acc_t, h1_v, th1_v, cot_v, sems,
):
    c = pl.program_id(0)
    rows = h1.shape[0]
    late = [
        pltpu.make_async_copy(src, dst, sems.at[n])
        for n, (src, dst) in enumerate(((h1, h1_v), (th1, th1_v), (cot, cot_v)))
    ]

    @pl.when(c == 0)
    def _():
        acc_s[...] = jnp.zeros_like(acc_s)
        acc_t[...] = jnp.zeros_like(acc_t)
        for copy in late:
            copy.start()

    def chunk(wi, wu, ti, tu, bi, ch, tb):
        inv_clip = 1.0 / ch[...]

        def block(i, carry):
            r = pl.ds(pl.multiple_of(i * ROWS, ROWS), ROWS)
            inner = dot(mid[r, :], wi[...]) + bi[...]
            t_inner = dot(tmid[r, :], ti[...]) + tb[...]
            cdf = 0.5 * (1.0 + lax.erf(inner * (2.0**-0.5)))
            act = inner * cdf
            deriv = cdf + inner * (jnp.exp(-0.5 * inner * inner) * (1.0 / math.sqrt(2.0 * math.pi)))
            ratio = act * inv_clip
            th = jnp.tanh(ratio)
            slope = 1.0 - th * th
            ain = (ch[...] * th).astype(bf16)
            ain_o[r, :] = ain
            mul_o[r, :] = (slope * deriv).astype(bf16)
            cv_o[r, :] = (th - ratio * slope).astype(bf16)
            acc_s[r, :] += dot(ain, wu[...])
            t_act = (t_inner * (0.5 * (1.0 + lax.erf(t_inner * (2.0**-0.5))))).astype(bf16)
            acc_t[r, :] += dot(t_act, tu[...])
            return carry

        lax.fori_loop(0, rows // ROWS, block, 0, unroll=True)

    @pl.when(c < NCH)
    def _():
        chunk(wi_a, wu_a, ti_a, tu_a, bi_a, ch_a, tb_a)

    @pl.when(c >= NCH)
    def _():
        chunk(wi_b, wu_b, ti_b, tu_b, bi_b, ch_b, tb_b)

    @pl.when(c == 2 * NCH - 1)
    def _():
        for copy in late:
            copy.wait()
        row = lambda n: rep[n : n + 1, :]
        total = [jnp.zeros((1, D), f32)] * 6
        for s in range(rows // SEQ):
            r = slice(s * SEQ, (s + 1) * SEQ)
            keep = keep_rows(lens[first[0] + s])
            branch = acc_s[r, :] + row(R_BU)
            r2 = h1_v[r, :] + branch
            normed, inv = norm(r2)
            out = normed * row(R_G1) + row(R_S1)
            t_normed, _ = norm(th1_v[r, :] + acc_t[r, :] + row(R_TBU))
            diff = keep * (out - (t_normed * row(R_TG1) + row(R_TS1)))
            d_out = cot_v[r, :].astype(f32) + diff
            dr2 = norm_back(d_out * row(R_G1), normed, inv)
            lo_o[r, :] = out.astype(bf16)
            dr2_o[r, :] = dr2
            dfr_o[r, :] = dr2.astype(bf16)
            parts = (
                d_out * normed, d_out, dr2, diff * diff, keep * r2 * r2, keep * branch * branch,
            )
            total = [t + colsum(p) for t, p in zip(total, parts)]
        for n in range(6):
            sum_o[n : n + 1, :] = total[n]
        sum_o[6:8, :] = jnp.zeros((2, D), f32)


def half_col(half, width, base=0):
    lo = half * NCH
    return pl.BlockSpec((width, CH_W), lambda c, *_: (0, base + jnp.clip(c - lo, 0, NCH - 1)))


def half_row(half):
    lo = half * NCH
    return pl.BlockSpec((CH_W, D), lambda c, *_: (jnp.clip(c - lo, 0, NCH - 1), 0))


def feed_forward(lens, h1, mid, th1, tmid, cot, wi, wu, ti, tu, v_a, v_b, rep):
    rows = h1.shape[0]
    full = whole((rows, D))
    anywhere = pl.BlockSpec(memory_space=pl.ANY)
    chunk_out = pl.BlockSpec((rows, CH_W), lambda c, *_: (0, c))
    return pl.pallas_call(
        ff_kernel,
        grid_spec=pltpu.PrefetchScalarGridSpec(
            num_scalar_prefetch=2,
            grid=(2 * NCH,),
            in_specs=[
                anywhere, full, anywhere, full, anywhere,
                half_col(0, D), half_col(1, D), half_row(0), half_row(1),
                half_col(0, D), half_col(1, D), half_row(0), half_row(1),
                half_col(0, 1, BI // CH_W), half_col(1, 1, BI // CH_W),
                half_col(0, 1, CHD // CH_W), half_col(1, 1, CHD // CH_W),
                half_col(0, 1, TI // CH_W), half_col(1, 1, TI // CH_W),
                whole((14, D)),
            ],
            out_specs=[chunk_out, chunk_out, chunk_out, full, full, full, whole((8, D))],
            scratch_shapes=[
                pltpu.VMEM((rows, D), f32),
                pltpu.VMEM((rows, D), f32),
                pltpu.VMEM((rows, D), f32),
                pltpu.VMEM((rows, D), f32),
                pltpu.VMEM((rows, D), bf16),
                pltpu.SemaphoreType.DMA((3,)),
            ],
        ),
        out_shape=[
            SDS((rows, FF), bf16),
            SDS((rows, FF), bf16),
            SDS((rows, FF), bf16),
            SDS((rows, D), bf16),
            SDS((rows, D), f32),
            SDS((rows, D), bf16),
            SDS((8, D), f32),
        ],
        compiler_params=params(42),
        name="feed_forward",
        cost_estimate=cost(45),
    )(
        *lens, h1, mid, th1, tmid, cot, wi[0], wi[1], wu[0], wu[1], ti[0], ti[1], tu[0], tu[1],
        v_a, v_b, v_a, v_b, v_a, v_b, rep,
    )


def fold(place, kind, own, got, high, low):
    n = high.shape[1]
    for r in range(BLOCKS):
        at = pl.ds(pl.multiple_of(place[kind * BLOCKS + r] * n, 16), n)
        value = (own[at, :] + got[at, :].astype(f32)).astype(bf16)
        if r >= BLOCKS // 2:
            high[r - BLOCKS // 2] = value
        else:
            low[r] = value


def fold_shapes(rows, cols):
    return [SDS((BLOCKS // 2, rows // BLOCKS, cols), bf16)] * 2


def outer_grad_kernel(place, dfr, ain, *refs):
    c = pl.program_id(0)
    part = dot(ain[...], dfr[...], TN)
    if len(refs) == 1:
        refs[0][...] = part.astype(bf16)
    else:
        got, high, low, acc = refs
        acc[pl.ds(pl.multiple_of(c * CH_W, CH_W), CH_W), :] = part

        @pl.when(c == NCH - 1)
        def _():
            fold(place, OUTER, acc, got, high, low)


def outer_grad(half, place, dfr, ain, got=None):
    rows = dfr.shape[0]
    in_specs = [
        whole((rows, D)), pl.BlockSpec((rows, CH_W), lambda c, *_: (0, half * NCH + c))
    ]
    if got is None:
        extra, scratch = [], []
        out_shape = SDS((FH, D), bf16)
        out_specs = pl.BlockSpec((CH_W, D), lambda c, *_: (c, 0))
    else:
        extra, scratch = [got], [pltpu.VMEM((FH, D), f32)]
        in_specs.append(whole((FH, D)))
        out_shape = fold_shapes(FH, D)
        out_specs = [whole(v.shape) for v in out_shape]
    return pl.pallas_call(
        outer_grad_kernel,
        grid_spec=pltpu.PrefetchScalarGridSpec(
            num_scalar_prefetch=1,
            grid=(NCH,),
            in_specs=in_specs,
            out_specs=out_specs,
            scratch_shapes=scratch,
        ),
        out_shape=out_shape,
        compiler_params=params(24),
        name="outer_grad",
        cost_estimate=cost(6),
    )(place, dfr, ain, *extra)


def ff_back_kernel(place, dfr, mid, mul, cv, wi, wu, *refs, first):
    if first:
        gi_o, sum_o, dh_o, mid_t = refs
    else:
        before, got, high, low, sum_o, dh_o, mid_t, acc = refs
    c = pl.program_id(0)

    @pl.when(c == 0)
    def _():
        mid_t[...] = mid[...].T
        dh_o[...] = jnp.zeros_like(dh_o) if first else before[...]

    d_ain = dot(dfr[...], wu[...], NT)
    sum_o[1:2, :] = colsum(d_ain * cv[...].astype(f32))
    d_inner = d_ain * mul[...].astype(f32)
    sum_o[0:1, :] = colsum(d_inner)
    sum_o[2:8, :] = jnp.zeros((6, CH_W), f32)
    dir_low = d_inner.astype(bf16)
    part = dot(mid_t[...], dir_low)
    if first:
        gi_o[...] = part.astype(bf16)
    else:
        acc[...] = part
        fold(place, INNER, acc, got, high, low)
    dh_o[...] += dot(dir_low, wi[...], NT)


def ff_back(half, place, dfr, mid, mul, cv, wi, wu, before=None, got=None):
    rows = dfr.shape[0]
    first = before is None
    full = whole((rows, D))
    chunk = pl.BlockSpec((rows, CH_W), lambda c, *_: (0, half * NCH + c))
    col = pl.BlockSpec((D, CH_W), lambda c, *_: (0, c))
    row = pl.BlockSpec((CH_W, D), lambda c, *_: (c, 0))
    in_specs = [full, full, chunk, chunk, col, row]
    scratch = [pltpu.VMEM((D, rows), bf16)]
    if first:
        extra, grad_shape, grad_specs = [], [SDS((D, FH), bf16)], [col]
    else:
        extra, grad_shape = [before, got], fold_shapes(D, FH)
        in_specs += [full, col]
        piece = grad_shape[0].shape
        grad_specs = [pl.BlockSpec(piece[:2] + (CH_W,), lambda c, *_: (0, 0, c))] * 2
        scratch.append(pltpu.VMEM((D, CH_W), f32))
    return pl.pallas_call(
        partial(ff_back_kernel, first=first),
        grid_spec=pltpu.PrefetchScalarGridSpec(
            num_scalar_prefetch=1,
            grid=(NCH,),
            in_specs=in_specs,
            out_specs=grad_specs + [pl.BlockSpec((8, CH_W), lambda c, *_: (0, c)), full],
            scratch_shapes=scratch,
        ),
        out_shape=grad_shape + [SDS((8, FH), f32), SDS((rows, D), f32)],
        compiler_params=params(32),
        name="ff_back",
        cost_estimate=cost(14),
    )(place, dfr, mid, mul, cv, wi, wu, *extra)


def mid_back_kernel(
    r1, dr2, dhin, ctx, wo_a, wo_b, v_a, v_b, rep, dr1_o, dcr_o, go_a, go_b, sum_o, wo, acc
):
    i = pl.program_id(0)

    @pl.when(i == 0)
    def _():
        wo[:DH, :] = wo_a[...]
        wo[DH:, :] = wo_b[...]
        acc[...] = jnp.zeros_like(acc)
        sum_o[...] = jnp.zeros_like(sum_o)

    row = lambda n: rep[n : n + 1, :]
    normed, inv = norm(r1[...])
    cm = row(R_CM)
    ratio = (normed * row(R_G0) + row(R_S0)) * (1.0 / cm)
    th = jnp.tanh(ratio)
    slope = 1.0 - th * th
    d_hin = dhin[...]
    sum_o[3:4, :] += colsum(d_hin * (th - ratio * slope))
    dh1 = dr2[...] + d_hin * slope
    sum_o[0:1, :] += colsum(dh1 * normed)
    sum_o[1:2, :] += colsum(dh1)
    dr1 = norm_back(dh1 * row(R_G0), normed, inv)
    sum_o[2:3, :] += colsum(dr1)
    dr1_o[...] = dr1
    dar = dr1.astype(bf16)
    clip = jnp.concatenate([v_a[:, CC : CC + DH], v_b[:, CC : CC + DH]], 1)
    ratio = ctx[...] * (1.0 / clip)
    th = jnp.tanh(ratio)
    slope = 1.0 - th * th
    acc[...] += dot(dar, (clip * th).astype(bf16), TN)
    d_cin = dot(dar, wo[...], NT)
    sum_o[4:5, :] += colsum(d_cin * (th - ratio * slope))
    dcr_o[...] = (d_cin * slope).astype(bf16)

    @pl.when(i == pl.num_programs(0) - 1)
    def _():
        go_a[...] = acc[:, :DH].astype(bf16)
        go_b[...] = acc[:, DH:].astype(bf16)


def mid_back(r1, dr2, dhin, ctx, wo_a, wo_b, v_a, v_b, rep):
    rows = r1.shape[0]
    block = pl.BlockSpec((RB, D), lambda i: (i, 0))
    return pl.pallas_call(
        mid_back_kernel,
        grid=(rows // RB,),
        in_specs=[block] * 4
        + [whole((DH, D)), whole((DH, D)), whole((1, VEND)), whole((1, VEND)), whole((14, D))],
        out_specs=[block, block, whole((D, DH)), whole((D, DH)), whole((8, D))],
        out_shape=[
            SDS((rows, D), f32),
            SDS((rows, D), bf16),
            SDS((D, DH), bf16),
            SDS((D, DH), bf16),
            SDS((8, D), f32),
        ],
        scratch_shapes=[pltpu.VMEM((D, D), bf16), pltpu.VMEM((D, D), f32)],
        compiler_params=params(20),
        name="mid_back",
        cost_estimate=cost(12),
    )(r1, dr2, dhin, ctx, wo_a, wo_b, v_a, v_b, rep)


LEAD, REST = 128, 256


def attn_back_kernel(
    lens, first, place, qkv, dc, ctx, lse, xt, *refs, pairs, kind, with_out, folded
):
    refs = list(refs)
    got_out = refs.pop(0) if with_out else None
    got = refs.pop(0) if folded else None
    d_o, *grads = refs[: 3 if folded else 2]
    sum_o, acc = refs[-2:]
    seq = pl.program_id(0)
    length = lens[first[0] + seq]
    width = 128 * len(pairs)
    lo = pairs[0] * 128
    pick = lax.broadcasted_iota(jnp.int32, (8, width), 1) // HD
    pick = (pick == lax.broadcasted_iota(jnp.int32, (8, width), 0)).astype(f32)
    cols = slice(lo, lo + width)
    deltas = lax.dot_general(
        pick, dc[:, cols].astype(f32) * ctx[:, cols], NT, precision=lax.Precision.HIGHEST,
        preferred_element_type=f32,
    )
    heads = [(n, h) for n in range(len(pairs)) for h in range(2)]

    def part_of(n, k):
        at = pairs[n] * 128 + k * DH
        return qkv[:, at : at + 128]

    def dc_of(n):
        return dc[:, pairs[n] * 128 : (pairs[n] + 1) * 128]

    def score(n, h):
        q_h, k_h = with_mask(part_of(n, 0), part_of(n, 1), length, h)
        return dot(k_h, q_h, NT), dot(pair_of(part_of(n, 2), h), dc_of(n), NT)

    @pl.when(seq == 0)
    def _():
        sum_o[...] = jnp.zeros_like(sum_o)

    scores = [score(*heads[0])]
    for i, (n, h) in enumerate(heads):
        if i + 1 < len(heads):
            scores.append(score(*heads[i + 1]))
        s, dp = scores[i]
        row = 2 * pairs[n] + h
        prob = jnp.exp(s - lse[0, row : row + 1, :])
        row = 2 * n + h
        ds = (prob * (dp - deltas[row : row + 1, :])).astype(bf16)
        if h == 0:
            k_t = part_of(n, 1).T
        part_q = dot(k_t[h * HD : (h + 1) * HD], ds)
        part_k = dot(ds, pair_of(part_of(n, 0), h))
        part_v = dot(prob.astype(bf16), pair_of(dc_of(n), h))
        if h == 0:
            d_q, d_k, d_v = part_q, part_k, part_v
        else:
            d_q = jnp.concatenate([d_q, part_q], 0).T * HD**-0.5
            d_v = d_v + part_v
            for k, d in enumerate((d_q, d_k + part_k, d_v)):
                at = k * width + n * 128
                d_o[:, at : at + 128] = d.astype(bf16)
            cols = slice(n * 128, (n + 1) * 128)
            sum_o[0:1, cols] += colsum(d_q)
            sum_o[1:2, cols] += colsum(d_v)
    part = dot(xt[...], d_o[...])
    n = 3 * width

    @pl.when(seq == 0)
    def _():
        acc[:, :n] = part
        if with_out:
            acc[:, n:] = got_out[...].astype(f32)

    @pl.when(seq > 0)
    def _():
        acc[:, :n] += part

    @pl.when(seq == pl.num_programs(0) - 1)
    def _():
        if folded:
            fold(place, kind, acc, got, *grads)
        else:
            grads[0][...] = acc[...].astype(bf16)


def attention_back(half, kind, lens, place, qkv, dcr, ctx, lse, x_t, out_grad=None, got=None):
    rows = qkv.shape[0]
    nseq = rows // SEQ
    pairs = (0,) if kind == FIRST else (1, 2)
    width = 128 * len(pairs)
    block = lambda n: pl.BlockSpec((SEQ, n), lambda s, *_: (s, half))
    in_specs = [
        block(QW),
        block(DH),
        block(DH),
        pl.BlockSpec((1, 8, SEQ), lambda s, *_: (2 * s + half, 0, 0)),
        pl.BlockSpec((D, SEQ), lambda s, *_: (0, s)),
    ]
    extra = [v for v in (out_grad, got) if v is not None]
    grad_shape = [SDS((D, D), bf16)] if got is None else fold_shapes(D, D)
    return pl.pallas_call(
        partial(
            attn_back_kernel,
            pairs=pairs, kind=kind, with_out=out_grad is not None, folded=got is not None,
        ),
        grid_spec=pltpu.PrefetchScalarGridSpec(
            num_scalar_prefetch=3,
            grid=(nseq,),
            in_specs=in_specs + [whole(v.shape) for v in extra],
            out_specs=[pl.BlockSpec((SEQ, 3 * width), lambda s, *_: (s, 0))]
            + [whole(v.shape) for v in grad_shape]
            + [whole((8, width))],
            scratch_shapes=[pltpu.VMEM((D, D), f32)],
        ),
        out_shape=[SDS((rows, 3 * width), bf16)] + grad_shape + [SDS((8, width), f32)],
        compiler_params=params(20),
        name="attention_back",
        cost_estimate=cost(6 * len(pairs)),
    )(*lens, place, qkv, dcr, ctx, lse, x_t, *extra)


def clip_in(x, rep):
    clip = rep[R_CI : R_CI + 1, :]
    ratio = x[...].astype(f32) * (1.0 / clip)
    return ratio, jnp.tanh(ratio)


def x_back_kernel(x, d_la, d_lb, d_a, d_b, dr1, w_a, w_b, rep, grad_o, sum_o, w_lead, w_rest):
    @pl.when(pl.program_id(0) == 0)
    def _():
        sum_o[...] = jnp.zeros_like(sum_o)
        for half, w in enumerate((w_a, w_b)):
            for k in range(3):
                at = half * DH + k * LEAD
                w_lead[:, at : at + LEAD] = w[:, k * DH : k * DH + LEAD]
                at = half * D + k * REST
                w_rest[:, at : at + REST] = w[:, k * DH + LEAD : (k + 1) * DH]

    total = (
        dot(jnp.concatenate([d_la[...], d_lb[...]], 1), w_lead[...], NT)
        + dot(d_a[...], w_rest[:, :D], NT)
        + dot(d_b[...], w_rest[:, D:], NT)
    )
    ratio, th = clip_in(x, rep)
    slope = 1.0 - th * th
    grad_o[...] = dr1[...] + total * slope
    sum_o[0:1, :] += colsum(total * (th - ratio * slope))


RB = 256


def x_back(x, d_la, d_lb, d_a, d_b, dr1, w_a, w_b, rep):
    rows = x.shape[0]
    block = pl.BlockSpec((RB, D), lambda i: (i, 0))
    narrow = pl.BlockSpec((RB, DH), lambda i: (i, 0))
    return pl.pallas_call(
        x_back_kernel,
        grid=(rows // RB,),
        in_specs=[block, narrow, narrow, block, block, block] + [whole((D, QW)), whole((D, QW)), whole((14, D))],
        out_specs=[block, whole((8, D))],
        out_shape=[SDS((rows, D), f32), SDS((8, D), f32)],
        scratch_shapes=[pltpu.VMEM((D, D), bf16), pltpu.VMEM((D, 2 * D), bf16)],
        compiler_params=params(20),
        name="x_back",
        cost_estimate=cost(8),
    )(x, d_la, d_lb, d_a, d_b, dr1, w_a, w_b, rep)


def pack_kernel(ha, hb, la, lb, qa, qb, m, f, a, x, out):
    for side, (h, l, q) in enumerate(((ha, la, qa), (hb, lb, qb))):
        base = 6 * side
        for n in range(2):
            out[base + 2 * n : base + 2 * n + 1, :] = h[n : n + 1, :D]
            out[base + 2 * n + 1 : base + 2 * n + 2, :] = h[n : n + 1, D:]
        for k in range(2):
            at = k * DH
            out[base + 4 : base + 5, at : at + LEAD] = l[k : k + 1, :]
            out[base + 4 : base + 5, at + LEAD : at + DH] = q[k : k + 1, :]
        out[base + 5 : base + 6, :DH] = m[4:5, side * DH : (side + 1) * DH]
        out[base + 5 : base + 6, DH:] = jnp.zeros((1, DH), f32)
    rows = (
        (m, 2), (f, 2), (m, 0), (f, 0), (m, 1), (f, 1), (x, 0), (m, 3),
        (f, 3), (f, 4), (a, 0), (f, 5),
    )
    for n, (ref, k) in enumerate(rows):
        out[12 + n : 13 + n, :] = ref[k : k + 1, :]


def pack(*sums):
    return pl.pallas_call(
        pack_kernel,
        grid=(1,),
        in_specs=[whole(v.shape) for v in sums],
        out_specs=whole((24, D)),
        out_shape=SDS((24, D), f32),
        compiler_params=params(4),
        name="pack",
        cost_estimate=cost(1),
    )(*sums)


BLOCKS = 16
OUTER, INNER, FIRST, LAST = range(4)
ORDERS = (
    ((1, 2, 4, 8), (2, 4, 1, 8)),
    ((4, 1, 2, 8), (1, 4, 2, 8)),
    ((4, 1, 2, 8), (1, 4, 2, 8)),
    ((1, 2, 4, 8), (2, 4, 1, 8)),
)


def spread(order, r):
    return sum(mask for p, mask in enumerate(order) if r & (BLOCKS >> (p + 1)))


def place_table(me, core):
    rows = []
    for pair in ORDERS:
        a, b = [jnp.asarray([spread(o, r) for r in range(BLOCKS)], jnp.int32) for o in pair]
        rows.append(jnp.where(core == 0, a, b) ^ me)
    return jnp.concatenate(rows)


def swap(value, masks, n_dp):
    pairs = [(2 * i + t, 2 * (i ^ masks[t]) + t) for i in range(n_dp) for t in range(2)]
    return lax.ppermute(value, ("dp", "tensor"), pairs)


class Sum:
    def __init__(self, pieces, kind, n_dp):
        self.kind, self.n_dp = kind, n_dp
        self.send, self.hold = pieces
        self.step = 0
        self.recv = self.swap(0)

    def swap(self, step):
        return swap(self.send, tuple(order[step] for order in ORDERS[self.kind]), self.n_dp)

    def advance(self, *done):
        self.recv, *done = lax.optimization_barrier((self.recv, *done))
        self.step += 1
        half = self.hold.shape[0] // 2
        if self.step <= 3:
            self.send = self.hold[half:] + self.recv[half:]
            self.hold = self.hold[:half] + self.recv[:half]
            self.recv = self.swap(self.step)
        elif self.step == 4:
            self.send = self.hold + self.recv
            mask = BLOCKS
            while mask < self.n_dp:
                self.send = self.send + swap(self.send, (mask, mask), self.n_dp)
                mask *= 2
            self.recv = self.swap(3)
        elif self.step <= 7:
            self.send = jnp.concatenate([self.send, self.recv], 0)
            self.recv = self.swap(7 - self.step)
        return done

    def result(self):
        assert self.step == 7
        return (self.send, self.recv)


class Small(Sum):
    def __init__(self, value, n_dp):
        self.n_dp = n_dp
        self.mask, self.send = 1, value
        self.recv = swap(value, (1, 1), n_dp)

    def advance(self, *done):
        self.recv, *done = lax.optimization_barrier((self.recv, *done))
        self.send = self.send + self.recv
        self.mask *= 2
        if self.mask < self.n_dp:
            self.recv = swap(self.send, (self.mask, self.mask), self.n_dp)
        return done

    def result(self):
        while self.mask < self.n_dp:
            self.advance()
        return self.send


def step(streams, *values):
    for stream in streams:
        values = stream.advance(*values)
    return behind(streams, *values)


def behind(streams, *values):
    sent = [s.send for s in streams]
    return lax.optimization_barrier((*sent, *values))[len(sent) :]


def latent(w, g, axis, factor):
    th = jnp.tanh(2.0 * w)
    n = w.shape[axis]
    mean = jnp.sum(jnp.abs(w), axis, keepdims=True) * (1.0 / n)
    inner = jnp.sum(g * th, axis, keepdims=True) * (1.0 / n)
    sign = jnp.where(w > 0, 1.0, jnp.where(w < 0, -1.0, 0.0))
    return factor * (2.0 * mean * (1.0 - th * th) * g + sign * inner)


def collect(place, mine, recv, kind, target):
    n = mine.shape[1]
    for r in range(BLOCKS):
        at = pl.multiple_of(place[kind * BLOCKS + r] * n, 16)
        target[pl.ds(at, n), :] = (mine if r < BLOCKS // 2 else recv)[r % 8]


def latent_kernel(place, mine, recv, w, out, g, *, kind):
    i = pl.program_id(0)

    @pl.when(i == 0)
    def _():
        collect(place, mine, recv, kind, g)

    n = FH // 4
    at = pl.ds(pl.multiple_of(i * n, 128), n)
    if kind == OUTER:
        out[...] = latent(w[...], g[at, :].astype(f32), 1, 1.0 / math.sqrt(FF))
    else:
        out[...] = latent(w[...], g[:, at].astype(f32), 0, 1.0 / math.sqrt(D))


def ffn_latent(kind, place, pieces, w):
    if kind == OUTER:
        block = pl.BlockSpec((FH // 4, D), lambda i, *_: (i, 0))
    else:
        block = pl.BlockSpec((D, FH // 4), lambda i, *_: (0, i))
    return pl.pallas_call(
        partial(latent_kernel, kind=kind),
        grid_spec=pltpu.PrefetchScalarGridSpec(
            num_scalar_prefetch=1,
            grid=(4,),
            in_specs=[whole(p.shape) for p in pieces] + [block],
            out_specs=block,
            scratch_shapes=[pltpu.VMEM(w.shape, bf16)],
        ),
        out_shape=SDS(w.shape, f32),
        compiler_params=params(16),
        name="ffn_latent",
        cost_estimate=cost(8),
    )(place, *pieces, w)


def attn_latent_kernel(place, *refs):
    pieces, w_in, wo, outs, go, g, h = refs[:4], refs[4:7], refs[7], refs[8:11], *refs[11:]
    root = 1.0 / math.sqrt(D)
    collect(place, *pieces[:2], FIRST, g)
    collect(place, *pieces[2:], LAST, h)
    for c in range(3):
        for src, at, n in ((g, 0, LEAD), (h, LEAD, REST)):
            grad = src[:, c * n : (c + 1) * n].astype(f32)
            cols = slice(at, at + n)
            outs[c][:, cols] = latent(w_in[c][:, cols], grad, 0, root if c == 2 else 2.0 * root)
    go[...] = latent(wo[...], g[:, DH:].astype(f32).T, 1, 8.0 * root)


def attn_latent(place, pieces, wq, wk, wv, wo):
    col, row = whole((D, DH)), whole((DH, D))
    return pl.pallas_call(
        attn_latent_kernel,
        grid_spec=pltpu.PrefetchScalarGridSpec(
            num_scalar_prefetch=1,
            grid=(1,),
            in_specs=[whole(p.shape) for p in pieces] + [col, col, col, row],
            out_specs=[col, col, col, row],
            scratch_shapes=[pltpu.VMEM((D, D), bf16)] * 2,
        ),
        out_shape=[SDS((D, DH), f32)] * 3 + [SDS((DH, D), f32)],
        compiler_params=params(24),
        name="attn_latent",
        cost_estimate=cost(9),
    )(place, *pieces, wq, wk, wv, wo)


def on_device(
    n_dp,
    tokens, cotangent, lengths, w_query, w_key, w_value, w_output, w_inner, w_outer,
    b_query, b_value, b_output, b_inner, b_outer, ln_gains, ln_shifts,
    clip_input, clip_context, clip_middle, clip_hidden,
    t_query, t_key, t_value, t_output, t_inner, t_outer,
    tb_query, tb_value, tb_output, tb_inner, tb_outer, t_gains, t_shifts,
):
    other = lambda value: lax.ppermute(value, "tensor", [(0, 1), (1, 0)])
    rows = tokens.shape[0]
    nseq = rows // SEQ
    core = lax.axis_index("tensor")
    place = place_table(lax.axis_index("dp").astype(jnp.int32), core)
    lens = (lengths, (core * nseq).astype(jnp.int32).reshape(1))

    t_own = (t_query, t_key, t_value)
    t_other = tuple(other(w) for w in t_own)
    t_out_b = other(t_output)
    wqkv, wo, wi, wu, v_a, rep = prep(
        (w_query, w_key, w_value, w_output, w_inner, w_outer),
        (b_inner, clip_hidden, tb_inner, b_query, b_value, clip_context, tb_query, tb_value),
        (
            b_output, b_outer, ln_gains, ln_shifts, clip_input, clip_middle,
            tb_output, tb_outer, t_gains, t_shifts,
        ),
    )
    v_a, *t_other, t_out_b = lax.optimization_barrier((v_a, *t_other, t_out_b))
    t_other = tuple(t_other)
    v_b = other(v_a)
    wqkv_b, wo_b = other(wqkv), other(wo)
    th1, tmid = encode(lens, tokens, t_own + t_other, t_output, t_out_b, v_a, v_b, rep, False)
    late = lax.optimization_barrier((v_b, t_inner, t_outer, wi, wu))[1:]
    ti_b, tu_b, wi_b, wu_b = [other(w) for w in late]
    qkv, ctx, lse, r1, h1, mid, x_t, sum_a = encode(
        lens, tokens, (wqkv, wqkv_b), wo, wo_b, v_a, v_b, rep, True
    )
    ain, mul, cv, layer_out, dr2, dfr, sum_f = feed_forward(
        lens, h1, mid, th1, tmid, cotangent, (wi, wi_b), (wu, wu_b), (t_inner, ti_b),
        (t_outer, tu_b), v_a, v_b, rep,
    )
    gu_b = outer_grad(1, place, dfr, ain)
    outer = Sum(outer_grad(0, place, dfr, ain, other(gu_b)), OUTER, n_dp)
    dfr, mid, mul, cv = behind([outer], dfr, mid, mul, cv)
    gi_b, sum_hb, dh_b = ff_back(1, place, dfr, mid, mul, cv, wi_b, wu_b)
    dh_b, gi_b = outer.advance(dh_b, gi_b)
    gi_c = other(gi_b)
    (dh_b,) = behind([outer], dh_b)
    *gi, sum_ha, dhin = ff_back(0, place, dfr, mid, mul, cv, wi, wu, dh_b, gi_c)
    (dhin,) = outer.advance(dhin)
    inner = Sum(gi, INNER, n_dp)
    (dhin,) = behind([outer, inner], dhin)
    dr1, dcr, go_a, go_b, sum_m = mid_back(r1, dr2, dhin, ctx, wo, wo_b, v_a, v_b, rep)
    (dcr,) = step([outer, inner], dcr)
    saved = (qkv, dcr, ctx, lse, x_t)
    d_lb, gl_b, sum_lb = attention_back(1, FIRST, lens, place, *saved, go_b)
    gl_c = other(gl_b)
    dcr, _ = step([inner], dcr, gl_b)
    saved = (qkv, dcr, ctx, lse, x_t)
    d_b, gs_b, sum_b = attention_back(1, LAST, lens, place, *saved)
    gs_c = other(gs_b)
    gl_c, dcr, _ = step([outer, inner], gl_c, dcr, gs_b)
    saved = (qkv, dcr, ctx, lse, x_t)
    d_la, *gl, sum_la = attention_back(0, FIRST, lens, place, *saved, go_a, gl_c)
    lead = Sum(gl, FIRST, n_dp)
    gs_c, dcr, _ = step([outer, inner], gs_c, dcr, d_la)
    gs_c, dcr = behind([lead], gs_c, dcr)
    saved = (qkv, dcr, ctx, lse, x_t)
    d_a, *gs, sum_q = attention_back(0, LAST, lens, place, *saved, None, gs_c)
    last = Sum(gs, LAST, n_dp)
    dr1, _ = step([lead, outer, inner], dr1, d_a)
    (dr1,) = behind([last], dr1)
    grad_tokens, sum_x = x_back(tokens, d_la, d_lb, d_a, d_b, dr1, wqkv, wqkv_b, rep)
    sums = pack(sum_ha, sum_hb, sum_la, sum_lb, sum_q, sum_b, sum_m, sum_f, sum_a, sum_x)
    from_other = other(sums[6:])
    (sums,) = last.advance(sums)
    lead.advance(last.send)
    small = Small(jnp.concatenate([sums[:6], sums[12:]], 0) + from_other, n_dp)
    outer.advance(lead.send)
    inner.advance(lead.send)
    for _ in range(3):
        last.advance()
        lead.advance(last.send)
        small.advance(lead.send)
    last.advance()
    lead.advance(last.send)
    small.advance(lead.send)
    (w_o,) = behind([last, lead], w_outer)
    g_outer = ffn_latent(OUTER, place, outer.result(), w_o)
    inner.advance(g_outer)
    last.advance()
    lead.advance(last.send)
    last.advance()
    (w_i,) = behind([last], w_inner)
    (small.recv,) = behind([last], small.recv)
    small = small.result()
    g_inner = ffn_latent(INNER, place, inner.result(), w_i)
    last.recv, g_inner = lax.optimization_barrier((last.recv, g_inner))
    g_query, g_key, g_value, g_output = attn_latent(
        place, lead.result() + last.result(), w_query, w_key, w_value, w_output
    )
    split, shared = small[:6], small[6:]
    count = jnp.asarray(rows * 2 * n_dp * D, f32)
    stats = jnp.sum(shared[8:], 1) / count
    summary = jnp.concatenate([stats[:1], jnp.sqrt(stats[1:])])
    return (
        layer_out,
        grad_tokens,
        g_query,
        g_key,
        g_value,
        g_output,
        g_inner,
        g_outer,
        split[4, :DH],
        split[4, DH:],
        shared[0],
        split[0:2].reshape(FH),
        shared[1],
        shared[2:4],
        shared[4:6],
        shared[6],
        split[5, :DH],
        shared[7],
        split[2:4].reshape(FH),
        summary,
    )


def solution(mesh):
    rows, cols, split, full = P(("dp", "tensor"), None), P(None, "tensor"), P("tensor"), P()
    down = P("tensor", None)
    return jax.shard_map(
        partial(on_device, mesh.shape["dp"]),
        mesh=mesh,
        in_specs=(
            rows, rows, P("dp"), cols, cols, cols, down, cols, down,
            split, split, full, split, full, full, full,
            full, split, full, split,
            cols, cols, cols, down, cols, down,
            split, split, full, split, full, full, full,
        ),
        out_specs=(
            rows, rows, cols, cols, cols, down, cols, down,
            split, split, full, split, full, full, full, full, split, full, split, full,
        ),
        check_vma=False,
    )
```
